256 devices in a mesh: wide: 16 (over x, y), narrow: 16 (over z, core).
Axes of the slice: x: 4, y: 4, z: 8, core: 2. Of those that a mesh axis runs over, the one named last changes fastest.
Arguments:
- entries: int32 [65536, 32, 256], P(('wide', 'narrow')), may hold values from 0 to 2
- factor_a: float32 [131072, 128], P(('wide', 'narrow')), may hold values from -4.2 to 4.2
- factor_b: float32 [131072, 128], P(('wide', 'narrow')), may hold values from -4.2 to 4.2
- factor_c: float32 [8192, 128], P('wide'), may hold values from -4.2 to 4.2
- index_a: int32 [65536], P(('wide', 'narrow')), may hold values from 0 to 511
- index_b: int32 [65536], P(('wide', 'narrow')), may hold values from 0 to 511
- index_c: int32 [8192], P(('wide', 'narrow')), may hold values from 0 to 511
Outputs:
- step_a: float32 [131072, 128], P(('wide', 'narrow'))
- step_b: float32 [131072, 128], P(('wide', 'narrow'))
- step_c: float32 [8192, 128], P('wide')
The draws below stay inside these ranges and needn't reach their ends.
All inputs are finite; a program needn't handle non-finite values.
Results may differ from the reference program's by a relative error of at most 0.0048.
Values may be sent and summed in bfloat16 or wider, within the bound.
No kernel may reach another device: no remote copies, remote signals or barrier semaphores. Data moves between devices by JAX's collectives and lax.ppermute only.
A program may use at most 128 MiB of HBM per device.

```python
import jax
import jax.numpy as jnp
from jax import lax

RANK = 128
BLOCK_I = 256
BLOCK_J = 256
BLOCK_K = 32
SHARD_A = 512
SHARD_B = 512
SHARD_C = 512
CG_ITERS = 2
BLOCKS = 256
A_SLOTS = 16
B_SLOTS = 16
C_SLOTS = 2
A_ROWS = 131072
B_ROWS = 131072
C_ROWS = 8192
N_NARROW = 16


def owner_scales(key, owner_count, low_scale, high_scale):
    order = jax.random.permutation(jax.random.fold_in(key, 5), owner_count).astype(jnp.float32)
    jitter = jax.random.uniform(jax.random.fold_in(key, 7), (owner_count,), jnp.float32, 0.0, 1.0)
    position = (order + jitter) / owner_count
    return low_scale * jnp.power(high_scale / low_scale, position)


def owner_rows(key, row_count, shard_rows, owner_count):
    owner_index = (jnp.arange(row_count) // shard_rows).astype(jnp.int32)
    base_draw = jnp.clip(jax.random.normal(jax.random.fold_in(key, 3), (row_count, RANK), jnp.float32), -4.0, 4.0)
    scales = owner_scales(key, owner_count, 0.02, 1.05)
    row_scale = scales[owner_index]
    return base_draw * row_scale[:, None]


def draw_factor_a(key, part):
    return owner_rows(jax.random.fold_in(key, 11), A_ROWS, SHARD_A, A_ROWS // SHARD_A)


def draw_factor_b(key, part):
    return owner_rows(jax.random.fold_in(key, 23), B_ROWS, SHARD_B, B_ROWS // SHARD_B)


def draw_factor_c(key, part):
    return owner_rows(jax.random.fold_in(key, 37), C_ROWS, SHARD_C, C_ROWS // SHARD_C)


def place_ends(drawn, rng, smallest, largest):
    index_at = [jax.random.randint(jax.random.fold_in(rng, axis), (), 0, length) for axis, length in enumerate(drawn.shape)]
    longest = drawn.shape.index(max(drawn.shape))
    beside = index_at[:longest] + [(index_at[longest] + 1) % drawn.shape[longest]] + index_at[longest + 1:]
    return drawn.at[tuple(index_at)].set(smallest).at[tuple(beside)].set(largest)


def setup_inputs(seed: int = 0) -> dict:
    key_list = jax.random.split(jax.random.key(seed), 8)
    return {
        "entries": place_ends(jax.random.randint(key_list[0], (BLOCKS * BLOCK_I, BLOCK_K, BLOCK_J), 0, 3), jax.random.fold_in(key_list[0], 1), 0, 2).astype(jnp.int32),
        "factor_a": draw_factor_a(jax.random.fold_in(key_list[7], 71), 0),
        "factor_b": draw_factor_b(jax.random.fold_in(key_list[7], 71), 0),
        "factor_c": draw_factor_c(jax.random.fold_in(key_list[7], 71), 0),
        "index_a": place_ends(jax.random.randint(key_list[4], (BLOCKS * BLOCK_I,), 0, SHARD_A), jax.random.fold_in(key_list[4], 1), 0, SHARD_A - 1).astype(jnp.int32),
        "index_b": place_ends(jax.random.randint(key_list[5], (BLOCKS * BLOCK_J,), 0, SHARD_B), jax.random.fold_in(key_list[5], 1), 0, SHARD_B - 1).astype(jnp.int32),
        "index_c": place_ends(jax.random.randint(key_list[6], (BLOCKS * BLOCK_K,), 0, SHARD_C), jax.random.fold_in(key_list[6], 1), 0, SHARD_C - 1).astype(jnp.int32),
    }


ridge_weight = 25.0


def block_rows(index_a, index_b, index_c):
    block = jnp.arange(BLOCKS, dtype=jnp.int32)
    wide_pos = block // N_NARROW
    narrow_pos = block % N_NARROW
    slot_a = jnp.arange(BLOCK_I, dtype=jnp.int32)
    owner_a = (slot_a // A_SLOTS)[None, :] * N_NARROW + narrow_pos[:, None]
    place_a = owner_a * BLOCK_I + wide_pos[:, None] * A_SLOTS + (slot_a % A_SLOTS)[None, :]
    rows_a = owner_a * SHARD_A + index_a[place_a]
    slot_b = jnp.arange(BLOCK_J, dtype=jnp.int32)
    owner_b = wide_pos[:, None] * N_NARROW + (slot_b // B_SLOTS)[None, :]
    place_b = owner_b * BLOCK_J + narrow_pos[:, None] * B_SLOTS + (slot_b % B_SLOTS)[None, :]
    rows_b = owner_b * SHARD_B + index_b[place_b]
    slot_c = jnp.arange(BLOCK_K, dtype=jnp.int32)
    group_c = (slot_c // C_SLOTS)[None, :]
    owner_c = group_c * N_NARROW + narrow_pos[:, None]
    place_c = owner_c * BLOCK_K + wide_pos[:, None] * C_SLOTS + (slot_c % C_SLOTS)[None, :]
    rows_c = group_c * SHARD_C + index_c[place_c]
    return rows_a.astype(jnp.int32), rows_b.astype(jnp.int32), rows_c.astype(jnp.int32)


def outer_pairs(rows_first, rows_third):
    product = rows_first.astype(jnp.float32)[:, None, :] * rows_third.astype(jnp.float32)[None, :, :]
    return product.astype(jnp.bfloat16).reshape(-1, rows_first.shape[1])


def model_values(pairs, rows_second):
    return lax.dot_general(pairs, rows_second, (((1,), (1,)), ((), ())), preferred_element_type=jnp.float32)


def fisher_terms(model, codes):
    sampled = (codes > 0).astype(jnp.float32)
    present = (codes == 2).astype(jnp.float32)
    prob = jax.nn.sigmoid(model)
    weight = sampled * prob * (1.0 - prob)
    slope = (sampled * (prob - present)).astype(jnp.bfloat16)
    return weight, slope


def transposed(upstream, pairs, rows_first, rows_second, rows_third):
    over = jnp.dot(upstream, rows_second, preferred_element_type=jnp.float32)
    over = over.reshape(rows_first.shape[0], rows_third.shape[0], -1)
    to_first = jnp.sum(over * rows_third.astype(jnp.float32)[None, :, :], axis=1)
    to_third = jnp.sum(over * rows_first.astype(jnp.float32)[:, None, :], axis=0)
    to_second = lax.dot_general(upstream, pairs, (((0,), (0,)), ((), ())), preferred_element_type=jnp.float32)
    return to_first, to_second, to_third


def add_scaled(base_set, factor, extra_set):
    return (base_set[0] + factor * extra_set[0], base_set[1] + factor * extra_set[1], base_set[2] + factor * extra_set[2])


def inner_all(first_set, second_set):
    return jnp.sum(first_set[0] * second_set[0]) + jnp.sum(first_set[1] * second_set[1]) + jnp.sum(first_set[2] * second_set[2])


def reference(entries, factor_a, factor_b, factor_c, index_a, index_b, index_c):
    rows_a, rows_b, rows_c = block_rows(index_a, index_b, index_c)
    codes = entries.reshape(BLOCKS, BLOCK_I * BLOCK_K, BLOCK_J)
    first = factor_a[rows_a].astype(jnp.bfloat16)
    second = factor_b[rows_b].astype(jnp.bfloat16)
    third = factor_c[rows_c].astype(jnp.bfloat16)

    def scatter_all(parts, field):
        sum_a = jnp.zeros((A_ROWS, RANK), jnp.float32).at[rows_a.reshape(-1)].add(parts[0].reshape(-1, RANK))
        sum_b = jnp.zeros((B_ROWS, RANK), jnp.float32).at[rows_b.reshape(-1)].add(parts[1].reshape(-1, RANK))
        sum_c = jnp.zeros((C_ROWS, RANK), jnp.float32).at[rows_c.reshape(-1)].add(parts[2].reshape(-1, RANK))
        return (sum_a + ridge_weight * field[0], sum_b + ridge_weight * field[1], sum_c + ridge_weight * field[2])

    def grad_block(packed):
        code_block, first_rows, second_rows, third_rows = packed
        pairs = outer_pairs(first_rows, third_rows)
        weight, slope = fisher_terms(model_values(pairs, second_rows), code_block)
        return transposed(slope, pairs, first_rows, second_rows, third_rows)

    gradient = scatter_all(lax.map(grad_block, (codes, first, second, third)), (factor_a, factor_b, factor_c))

    def fisher_product(field):
        move_first = field[0][rows_a].astype(jnp.bfloat16)
        move_second = field[1][rows_b].astype(jnp.bfloat16)
        move_third = field[2][rows_c].astype(jnp.bfloat16)

        def curve_block(packed):
            code_block, first_rows, second_rows, third_rows, d_first, d_second, d_third = packed
            pairs = outer_pairs(first_rows, third_rows)
            weight, slope = fisher_terms(model_values(pairs, second_rows), code_block)
            mixed = d_first.astype(jnp.float32)[:, None, :] * third_rows.astype(jnp.float32)[None, :, :]
            mixed = mixed + first_rows.astype(jnp.float32)[:, None, :] * d_third.astype(jnp.float32)[None, :, :]
            mixed = mixed.astype(jnp.bfloat16).reshape(-1, RANK)
            change = model_values(mixed, second_rows) + model_values(pairs, d_second)
            scaled = (weight * change).astype(jnp.bfloat16)
            return transposed(scaled, pairs, first_rows, second_rows, third_rows)

        parts = lax.map(curve_block, (codes, first, second, third, move_first, move_second, move_third))
        return scatter_all(parts, field)

    solution = (jnp.zeros_like(factor_a), jnp.zeros_like(factor_b), jnp.zeros_like(factor_c))
    residual = add_scaled(solution, -1.0, gradient)
    direction = residual
    norm_now = inner_all(residual, residual)
    for iteration in range(CG_ITERS):
        image = fisher_product(direction)
        alpha = norm_now / inner_all(direction, image)
        solution = add_scaled(solution, alpha, direction)
        residual = add_scaled(residual, -alpha, image)
        if iteration + 1 < CG_ITERS:
            norm_next = inner_all(residual, residual)
            direction = add_scaled(residual, norm_next / norm_now, direction)
            norm_now = norm_next
    return solution[0], solution[1], solution[2]
```

```python
import jax
import jax.numpy as jnp
from jax import lax
from jax.experimental import pallas as pl
from jax.experimental.pallas import tpu as pltpu
from jax.sharding import PartitionSpec as P

RIDGE = 25.0
F32, BF16, I32 = jnp.float32, jnp.bfloat16, jnp.int32

RANK = 128
SIDE = 16
BLOCK = 256
DEPTH = 32
ENTRY = 24
STEP_I = 32
SUB_I = 8


def full(shape):
    return pl.BlockSpec(shape, lambda *_: (0,) * len(shape))


def struct(shape, dtype):
    return jax.ShapeDtypeStruct(shape, dtype)


def dot(x, y, dims=(1, 0)):
    return lax.dot_general(
        x, y, (((dims[0],), (dims[1],)), ((), ())), preferred_element_type=F32
    )


def hot(x):
    return jnp.where(x, 1.0, 0.0).astype(BF16)


def column_hot(index_column, width):
    rows = index_column.shape[0]
    return hot(lax.broadcasted_iota(I32, (rows, width), 1) == index_column)


def row_hot(index_row, height):
    columns = index_row.shape[1]
    return hot(lax.broadcasted_iota(I32, (height, columns), 0) == index_row)


def split_dot(one_hot, x):
    high = x.astype(BF16)
    rest = x - high.astype(F32)
    middle = rest.astype(BF16)
    low = (rest - middle.astype(F32)).astype(BF16)
    return dot(one_hot, high) + dot(one_hot, middle) + dot(one_hot, low)


def pick_main():
    q = lax.broadcasted_iota(I32, (BLOCK, SIDE * ENTRY), 0)
    p = lax.broadcasted_iota(I32, (BLOCK, SIDE * ENTRY), 1)
    return hot(p == (q >> 4) * ENTRY + (q & 15))


def pick_third():
    q = lax.broadcasted_iota(I32, (DEPTH, SIDE * ENTRY), 0)
    p = lax.broadcasted_iota(I32, (DEPTH, SIDE * ENTRY), 1)
    return hot(p == (q >> 1) * ENTRY + 16 + (q & 1))


def first_send_kernel(at_wide, at_narrow, extra, fa, fb, fc, send_wide, send_narrow):
    table = jnp.concatenate([fa[...], fc[...]], axis=0).astype(BF16)
    send_wide[...] = dot(column_hot(at_wide[...], 1024), table).astype(BF16)
    rows = dot(column_hot(at_narrow[...], 512), fb[...].astype(BF16))
    r = lax.broadcasted_iota(I32, (SIDE * ENTRY, 1), 0) % ENTRY
    rows = jnp.where(r == 16, extra[0:1, :], rows)
    rows = jnp.where(r == 17, extra[1:2, :], rows)
    send_narrow[...] = rows.astype(BF16)


def accumulate(upstream, pairs, a_part, c, b, to_a, to_c, to_bt, first_row):
    over = dot(upstream, b).reshape(SUB_I, DEPTH, RANK)
    to_a[pl.ds(first_row, SUB_I), :] = jnp.sum(over * c[None], axis=1)
    to_c[...] += jnp.sum(over * a_part[:, None, :], axis=0)
    to_bt[...] += dot(pairs, upstream, (0, 0))


def fill_send(send, to_bt, to_c, spare):
    to_b = to_bt[...].T
    for peer in range(SIDE):
        base = peer * ENTRY
        send[base : base + 16, :] = to_b[peer * 16 : peer * 16 + 16, :]
        tail = jnp.concatenate([to_c[2 * peer : 2 * peer + 2, :], spare], axis=0)
        send[base + 16 : base + ENTRY, :] = tail


def gradient_kernel(
    from_wide, from_narrow, codes, weight, send, to_a, a_out, b_out, c_out, to_c, to_bt
):
    step = pl.program_id(0)

    @pl.when(step == 0)
    def _():
        a_out[...] = dot(pick_main(), from_wide[...])
        c_out[...] = dot(pick_third(), from_wide[...])
        b_out[...] = dot(pick_main(), from_narrow[...]).astype(BF16)
        to_c[...] = jnp.zeros_like(to_c)
        to_bt[...] = jnp.zeros_like(to_bt)

    b = b_out[...]
    c = c_out[...]
    for part in range(STEP_I // SUB_I):
        first_row = pl.multiple_of(step * STEP_I + part * SUB_I, SUB_I)
        inside = slice(part * SUB_I, (part + 1) * SUB_I)
        a_part = a_out[pl.ds(first_row, SUB_I), :]
        pairs = (a_part[:, None, :] * c[None]).astype(BF16).reshape(-1, RANK)
        half = jnp.tanh(0.5 * dot(pairs, b, (1, 1)))
        code = codes[inside].reshape(-1, BLOCK)
        sampled = code > 0
        value = jnp.where(sampled, 0.25 - 0.25 * half * half, 0.0)
        weight[inside] = value.reshape(SUB_I, DEPTH, BLOCK)
        slope = jnp.where(sampled, 0.5 * half + (1.5 - code.astype(F32)), 0.0).astype(BF16)
        accumulate(slope, pairs, a_part, c, b, to_a, to_c, to_bt, first_row)

    @pl.when(step == pl.num_programs(0) - 1)
    def _():
        fill_send(send, to_bt, to_c, jnp.zeros((ENTRY - 18, RANK), F32))


def moved_setup(from_wide, from_narrow, b, d_first, d_third, both):
    d_first[...] = from_wide[...].astype(F32)
    d_third[...] = dot(pick_third(), from_narrow[...])
    both[:, :RANK] = b[...]
    both[:, RANK:] = dot(pick_main(), from_narrow[...]).astype(BF16)


def moved_change(a_part, d_part, c, d_third, both):
    pairs = (a_part[:, None, :] * c[None]).astype(BF16).reshape(-1, RANK)
    mixed = d_part[:, None, :] * c[None] + a_part[:, None, :] * d_third[None]
    mixed = mixed.astype(BF16).reshape(-1, RANK)
    return pairs, dot(jnp.concatenate([mixed, pairs], axis=1), both, (1, 1))


def fold(x):
    return jnp.sum(x.reshape(-1, 8, BLOCK), axis=0)


def image_kernel(
    from_wide, from_narrow, weight, a, b, c, norm, send, to_a, d_first, d_third, both, to_c, to_bt, total
):
    step = pl.program_id(0)

    @pl.when(step == 0)
    def _():
        moved_setup(from_wide, from_narrow, b, d_first, d_third, both)
        to_c[...] = jnp.zeros_like(to_c)
        to_bt[...] = jnp.zeros_like(to_bt)
        total[...] = jnp.zeros_like(total)

    third = c[...]
    for part in range(STEP_I // SUB_I):
        first_row = pl.multiple_of(step * STEP_I + part * SUB_I, SUB_I)
        inside = slice(part * SUB_I, (part + 1) * SUB_I)
        a_part = a[pl.ds(first_row, SUB_I), :]
        d_part = d_first[pl.ds(first_row, SUB_I), :]
        pairs, change = moved_change(a_part, d_part, third, d_third[...], both[...])
        scaled = weight[inside].reshape(-1, BLOCK) * change
        total[...] += fold(scaled * change)
        accumulate(scaled.astype(BF16), pairs, a_part, third, b[...], to_a, to_c, to_bt, first_row)

    @pl.when(step == pl.num_programs(0) - 1)
    def _():
        energy = jnp.sum(total[:, :RANK] + total[:, RANK:], axis=0, keepdims=True)
        spare = jnp.concatenate([norm[0:1, :], energy, jnp.zeros((ENTRY - 20, RANK), F32)], axis=0)
        fill_send(send, to_bt, to_c, spare)


def energy_kernel(from_wide, from_narrow, weight, a, b, c, sums, send, d_first, d_third, both, total):
    step = pl.program_id(0)

    @pl.when(step == 0)
    def _():
        moved_setup(from_wide, from_narrow, b, d_first, d_third, both)
        total[...] = jnp.zeros_like(total)

    third = c[...]
    for part in range(STEP_I // SUB_I):
        first_row = pl.multiple_of(step * STEP_I + part * SUB_I, SUB_I)
        inside = slice(part * SUB_I, (part + 1) * SUB_I)
        a_part = a[pl.ds(first_row, SUB_I), :]
        d_part = d_first[pl.ds(first_row, SUB_I), :]
        _, change = moved_change(a_part, d_part, third, d_third[...], both[...])
        total[...] += fold(weight[inside].reshape(-1, BLOCK) * change * change)

    @pl.when(step == pl.num_programs(0) - 1)
    def _():
        energy = jnp.sum(total[...], keepdims=True)
        norm = jnp.sum(sums[0:1, :], axis=1, keepdims=True)
        cross = jnp.sum(sums[1:2, :], axis=1, keepdims=True)
        lane = lax.broadcasted_iota(I32, (1, RANK), 1)
        row = jnp.where(lane == 0, norm, jnp.where(lane == 1, cross, energy))
        send[...] = jnp.broadcast_to(row, send.shape)


def owner_sums(from_narrow, from_wide, b_row, a_row, c_row):
    sum_b = split_dot(row_hot(b_row[...], 512), from_narrow[...])
    received = from_wide[...]
    both = jnp.concatenate([row_hot(a_row[...], 512), row_hot(c_row[...], 512)], axis=0)
    sum_ac = split_dot(both, received)
    return sum_ac[:512], sum_b, sum_ac[512:]


def send_rows(at_narrow, at_wide, r_a, r_b, r_c, send_narrow, send_wide):
    table = jnp.concatenate([r_b, r_c], axis=0).astype(BF16)
    send_narrow[...] = dot(column_hot(at_narrow[...], 1024), table).astype(BF16)
    send_wide[...] = dot(column_hot(at_wide[...], 512), r_a.astype(BF16)).astype(BF16)


def inner(x, y, count_third):
    column = jnp.sum(x[0] * y[0] + x[1] * y[1], axis=0, keepdims=True)
    return column + count_third * jnp.sum(x[2] * y[2], axis=0, keepdims=True)


def residual_kernel(
    from_narrow, from_wide, b_row, a_row, c_row, at_narrow, at_wide, count_third, fa, fb, fc,
    r_a, r_b, r_c, send_narrow, send_wide, norm,
):
    sums = owner_sums(from_narrow, from_wide, b_row, a_row, c_row)
    rest = [-(s + RIDGE * f[...]) for s, f in zip(sums, (fa, fb, fc))]
    r_a[...], r_b[...], r_c[...] = rest
    norm[...] = jnp.broadcast_to(inner(rest, rest, count_third[0:1, :]), norm.shape)
    send_rows(at_narrow, at_wide, *rest, send_narrow, send_wide)


def update_kernel(
    from_narrow, from_wide, b_row, a_row, c_row, at_narrow, at_wide, count_third, r_a, r_b, r_c,
    n_a, n_b, n_c, send_narrow, send_wide, sums, scalars,
):
    width = from_wide.shape[0] // SIDE
    norm = jnp.zeros((1, RANK), F32)
    energy = jnp.zeros((1, RANK), F32)
    for peer in range(SIDE):
        at = peer * width + 16 + DEPTH
        norm += from_wide[at : at + 1, :]
        energy += from_wide[at + 1 : at + 2, :]
    norm = jnp.sum(norm, axis=1, keepdims=True)
    curved = RIDGE * norm + jnp.sum(energy, axis=1, keepdims=True)
    alpha = norm / curved
    old = [r_a[...], r_b[...], r_c[...]]
    image = [
        s + RIDGE * r
        for s, r in zip(owner_sums(from_narrow, from_wide, b_row, a_row, c_row), old)
    ]
    rest = [r - alpha * q for r, q in zip(old, image)]
    n_a[...], n_b[...], n_c[...] = rest
    send_rows(at_narrow, at_wide, *rest, send_narrow, send_wide)
    row = lax.broadcasted_iota(I32, (8, RANK), 0)
    new_norm = inner(rest, rest, count_third[0:1, :])
    cross = inner(rest, image, count_third[0:1, :])
    sums[...] = jnp.where(row == 0, new_norm, cross)
    scalars[...] = jnp.where(row == 0, norm, jnp.where(row == 1, curved, alpha))


def step_kernel(received, scalars, r_a, r_b, r_c, n_a, n_b, n_c, s_a, s_b, s_c):
    total = jnp.sum(received[...], axis=0, keepdims=True)
    new, cross, energy = total[:, 0:1], total[:, 1:2], total[:, 2:3]
    norm, curved, alpha = scalars[0:1, 0:1], scalars[1:2, 0:1], scalars[2:3, 0:1]
    beta = new / norm
    second = new / (RIDGE * new + energy + 2.0 * beta * cross + beta * beta * curved)
    for old, rest, out in ((r_a, n_a, s_a), (r_b, n_b, s_b), (r_c, n_c, s_c)):
        out[...] = alpha * old[...] + second * (rest[...] + beta * old[...])


def call(kernel, outs, *operands, name):
    return pl.pallas_call(
        kernel,
        out_shape=outs,
        name=name,
        compiler_params=pltpu.CompilerParams(vmem_limit_bytes=24 << 20),
    )(*operands)


def block_call(kernel, outs, out_specs, in_specs, scratch, *operands, name):
    return pl.pallas_call(
        kernel,
        grid=(BLOCK // STEP_I,),
        in_specs=in_specs,
        out_specs=out_specs,
        out_shape=outs,
        scratch_shapes=scratch,
        name=name,
        compiler_params=pltpu.CompilerParams(
            vmem_limit_bytes=40 << 20, dimension_semantics=("arbitrary",)
        ),
    )(*operands)


def exchange(x, axis):
    return lax.all_to_all(x, axis, split_axis=0, concat_axis=0, tiled=True)


def local(entries, factor_a, factor_b, factor_c, index_a, index_b, index_c):
    across = [(w * SIDE + n, n * SIDE + w) for w in range(SIDE) for n in range(SIDE)]
    wide_at = lax.axis_index("wide")

    def transposed_place(x):
        return lax.ppermute(x, ("wide", "narrow"), across)

    rows = SIDE * ENTRY
    none = lambda *shape: jnp.full(shape, -1, I32)
    ia, ib, ic = index_a.reshape(16, 16), index_b.reshape(16, 16), index_c.reshape(16, 2)
    at_first = jnp.concatenate([ia, ic + 512, none(16, 6)], 1).reshape(rows, 1)
    at_b = jnp.concatenate([ib, none(16, 8)], 1)
    extra = jnp.pad(jnp.stack([index_c // 16, index_c % 16]), ((0, 6), (0, 96))).astype(F32)

    send_wide, send_narrow = call(
        first_send_kernel,
        (struct((rows, RANK), BF16), struct((rows, RANK), BF16)),
        at_first, at_b.reshape(rows, 1), extra, factor_a, factor_b, factor_c,
        name="first_send",
    )
    from_narrow = exchange(send_narrow, "narrow")
    from_wide = exchange(send_wide, "wide")
    third_t = transposed_place(factor_c)
    group_index = transposed_place(from_narrow.reshape(SIDE, ENTRY, RANK)[:, 16:18, :DEPTH])
    group_index = group_index.astype(F32)
    group_index = (group_index[:, 0] * 16.0 + group_index[:, 1]).astype(I32)
    group_index = group_index.reshape(16, 16, 2)

    weight_shape = struct((BLOCK, DEPTH, BLOCK), F32)
    slab = pl.BlockSpec((STEP_I, DEPTH, BLOCK), lambda i: (i, 0, 0))
    both_scratch = [
        pltpu.VMEM((BLOCK, RANK), F32), pltpu.VMEM((DEPTH, RANK), F32),
        pltpu.VMEM((BLOCK, 2 * RANK), BF16),
    ]
    sum_scratch = [pltpu.VMEM((DEPTH, RANK), F32), pltpu.VMEM((RANK, BLOCK), F32)]
    total_scratch = [pltpu.VMEM((8, BLOCK), F32)]

    weight, send, to_a, a, b, c = block_call(
        gradient_kernel,
        (
            weight_shape, struct((rows, RANK), F32), struct((BLOCK, RANK), F32),
            struct((BLOCK, RANK), F32), struct((BLOCK, RANK), BF16), struct((DEPTH, RANK), F32),
        ),
        (
            slab, full((rows, RANK)), full((BLOCK, RANK)),
            full((BLOCK, RANK)), full((BLOCK, RANK)), full((DEPTH, RANK)),
        ),
        [full((rows, RANK)), full((rows, RANK)), slab],
        sum_scratch,
        from_wide, from_narrow, entries,
        name="gradient",
    )

    b_row = at_b.reshape(1, rows)
    group_slots = group_index.transpose(1, 0, 2).reshape(16, DEPTH)
    a_row = jnp.concatenate([ia, none(16, DEPTH + 8)], 1).reshape(1, -1)
    c_row = jnp.concatenate([none(16, 16), group_slots, none(16, 8)], 1).reshape(1, -1)
    mine = lax.dynamic_slice_in_dim(group_slots, wide_at, 1, 0).reshape(16, 2)
    at_narrow = jnp.concatenate([ib, mine + 512, none(16, 6)], 1).reshape(rows, 1)
    at_wide = index_a.reshape(BLOCK, 1)
    count_third = jnp.broadcast_to((wide_at == 0).astype(F32), (8, RANK))
    places = (b_row, a_row, c_row, at_narrow, at_wide, count_third)

    def give_back(send, to_a):
        from_narrow = exchange(send, "narrow")
        tail = from_narrow.reshape(SIDE, ENTRY, RANK)[:, 16:, :]
        third = tail[:, :2].reshape(DEPTH, RANK)
        sums = jnp.sum(tail[:, 2:4], axis=0)
        extra = jnp.concatenate([third, sums, jnp.zeros((6, RANK), F32)], 0)
        extra = jnp.broadcast_to(extra[None], (SIDE, DEPTH + 8, RANK))
        packed = jnp.concatenate([to_a.reshape(SIDE, 16, RANK), extra], 1)
        return from_narrow, exchange(packed.reshape(-1, RANK), "wide")

    table = struct((512, RANK), F32)
    row_sends = (struct((rows, RANK), BF16), struct((BLOCK, RANK), BF16))

    back_narrow, back_wide = give_back(send, to_a)
    r_a, r_b, r_c, send_narrow, send_wide, norm = call(
        residual_kernel,
        (table, table, table, *row_sends, struct((8, RANK), F32)),
        back_narrow, back_wide, *places, factor_a, factor_b, third_t,
        name="residual",
    )
    old_third = transposed_place(r_c)
    from_narrow = exchange(send_narrow, "narrow")
    from_wide = exchange(send_wide, "wide")
    fixed_specs = [
        full((BLOCK, RANK)), full((rows, RANK)), slab,
        full((BLOCK, RANK)), full((BLOCK, RANK)), full((DEPTH, RANK)), full((8, RANK)),
    ]
    send, to_a = block_call(
        image_kernel,
        (struct((rows, RANK), F32), struct((BLOCK, RANK), F32)),
        (full((rows, RANK)), full((BLOCK, RANK))),
        fixed_specs,
        both_scratch + sum_scratch + total_scratch,
        from_wide, from_narrow, weight, a, b, c, norm,
        name="image",
    )
    back_narrow, back_wide = give_back(send, to_a)
    n_a, n_b, n_c, send_narrow, send_wide, sums, scalars = call(
        update_kernel,
        (table, table, table, *row_sends, struct((8, RANK), F32), struct((8, RANK), F32)),
        back_narrow, back_wide, *places, r_a, r_b, r_c,
        name="update",
    )
    new_third = transposed_place(n_c)
    from_narrow = exchange(send_narrow, "narrow")
    from_wide = exchange(send_wide, "wide")
    partial = block_call(
        energy_kernel,
        struct((BLOCK, RANK), F32),
        full((BLOCK, RANK)),
        fixed_specs,
        both_scratch + total_scratch,
        from_wide, from_narrow, weight, a, b, c, sums,
        name="energy",
    )
    received = exchange(partial, ("wide", "narrow"))
    return call(
        step_kernel,
        (table, table, table),
        received, scalars, r_a, r_b, old_third, n_a, n_b, new_third,
        name="step",
    )


def solution(mesh):
    placed = (
        P(("wide", "narrow"), None, None),
        P(("wide", "narrow"), None),
        P(("wide", "narrow"), None),
        P("wide", None),
        P(("wide", "narrow")),
        P(("wide", "narrow")),
        P(("wide", "narrow")),
    )
    return jax.shard_map(
        local,
        mesh=mesh,
        in_specs=placed,
        out_specs=(P(("wide", "narrow"), None), P(("wide", "narrow"), None), P("wide", None)),
        check_vma=False,
    )
```

```python
import jax
import jax.numpy as jnp
from jax import lax
from jax.experimental import pallas as pl
from jax.experimental.pallas import tpu as pltpu
from jax.sharding import PartitionSpec as P

RIDGE = 25.0
F32, BF16, I32 = jnp.float32, jnp.bfloat16, jnp.int32

RANK = 128
SIDE = 16
BLOCK = 256
DEPTH = 32
ENTRY = 24
STEP_I = 64
STEPS = BLOCK // STEP_I
AHEAD = 4
SUB_I = 8


def full(shape):
    return pl.BlockSpec(shape, lambda *_: (0,) * len(shape))


def struct(shape, dtype):
    return jax.ShapeDtypeStruct(shape, dtype)


def dot(x, y, dims=(1, 0)):
    return lax.dot_general(
        x, y, (((dims[0],), (dims[1],)), ((), ())), preferred_element_type=F32
    )


def hot(x):
    return jnp.where(x, 1.0, 0.0).astype(BF16)


def row_hot(index_row, height):
    columns = index_row.shape[1]
    return hot(lax.broadcasted_iota(I32, (height, columns), 0) == index_row)


def dot_parts(one_hot, x):
    high = x.astype(BF16)
    rest = x - high.astype(F32)
    middle = rest.astype(BF16)
    low = (rest - middle.astype(F32)).astype(BF16)
    return dot(one_hot, high) + dot(one_hot, middle) + dot(one_hot, low)


def pick_main():
    q = lax.broadcasted_iota(I32, (BLOCK, SIDE * ENTRY), 0)
    p = lax.broadcasted_iota(I32, (BLOCK, SIDE * ENTRY), 1)
    return hot(p == (q >> 4) * ENTRY + (q & 15))


def pick_third():
    q = lax.broadcasted_iota(I32, (DEPTH, SIDE * ENTRY), 0)
    p = lax.broadcasted_iota(I32, (DEPTH, SIDE * ENTRY), 1)
    return hot(p == (q >> 1) * ENTRY + 16 + (q & 1))


def spread(width, per_peer, offset):
    shift = per_peer.bit_length() - 1
    p = lax.broadcasted_iota(I32, (SIDE * ENTRY, width), 0)
    q = lax.broadcasted_iota(I32, (SIDE * ENTRY, width), 1)
    return hot(p == (q >> shift) * ENTRY + offset + (q & (per_peer - 1)))


def gather(index_row, table):
    return dot(row_hot(index_row, 512), table.astype(BF16), (0, 0)).astype(BF16)


def wide_rows(ia, ic, table_a, table_c):
    return dot(spread(BLOCK, 16, 0), gather(ia, table_a)) + dot(
        spread(DEPTH, 2, 16), gather(ic, table_c)
    )


def first_narrow_kernel(ib, ic, fb, send):
    rows = dot(spread(BLOCK, 16, 0), gather(ib[...], fb[...]))
    lane = lax.broadcasted_iota(I32, (DEPTH, RANK), 1)
    to_lanes = hot(lane == lax.broadcasted_iota(I32, (DEPTH, RANK), 0))
    high, low = ((ic[...] >> 4).astype(BF16), (ic[...] & 15).astype(BF16))
    r = lax.broadcasted_iota(I32, (SIDE * ENTRY, 1), 0) % ENTRY
    rows = jnp.where(r == 16, dot(high, to_lanes), rows)
    rows = jnp.where(r == 17, dot(low, to_lanes), rows)
    send[...] = rows.astype(BF16)


def first_wide_kernel(ia, ic, fa, fc, send):
    send[...] = wide_rows(ia[...], ic[...], fa[...], fc[...]).astype(BF16)


def chunk_copy(source, held, arrived, k):
    here = pl.ds(k * STEP_I, STEP_I)
    return pltpu.make_async_copy(source.at[here], held.at[here], arrived.at[k])


def stream(source, held, arrived, step):
    @pl.when(step == 0)
    def _():
        for k in range(AHEAD):
            chunk_copy(source, held, arrived, k).start()

    @pl.when(step + AHEAD < STEPS)
    def _():
        chunk_copy(source, held, arrived, step + AHEAD).start()

    chunk_copy(source, held, arrived, step).wait()


def accumulate(upstream, pairs, a_part, c, b, to_a, to_c, to_bt, first_row):
    over = dot(upstream, b).reshape(SUB_I, DEPTH, RANK)
    to_a[pl.ds(first_row, SUB_I), :] = jnp.sum(over * c[None], axis=1)
    to_c[...] += jnp.sum(over * a_part[:, None, :], axis=0)
    to_bt[...] += dot(pairs, upstream, (0, 0))


def fill_send(send, to_b, acc_a, acc_c, acc_bt, spare):
    to_b[...] = acc_bt[...].T
    for peer in range(SIDE):
        base = peer * ENTRY
        send[base : base + 16, :] = acc_a[peer * 16 : peer * 16 + 16, :]
        tail = jnp.concatenate([acc_c[2 * peer : 2 * peer + 2, :], spare], axis=0)
        send[base + 16 : base + ENTRY, :] = tail


def gradient_kernel(
    from_wide, from_narrow, codes_from, weight_to, send, to_b, a_out, b_out, c_out,
    codes, weight, arrived, left, to_a, to_c, to_bt,
):
    step = pl.program_id(0)
    stream(codes_from, codes, arrived, step)

    @pl.when(step == 0)
    def _():
        a_out[...] = dot(pick_main(), from_wide[...])
        c_out[...] = dot(pick_third(), from_wide[...])
        b_out[...] = dot(pick_main(), from_narrow[...]).astype(BF16)
        to_c[...] = jnp.zeros_like(to_c)
        to_bt[...] = jnp.zeros_like(to_bt)

    b_half = 0.5 * b_out[...]
    c = c_out[...]
    for part in range(STEP_I // SUB_I):
        first_row = pl.multiple_of(step * STEP_I + part * SUB_I, SUB_I)
        inside = pl.ds(first_row, SUB_I)
        a_part = a_out[pl.ds(first_row, SUB_I), :]
        pairs = (a_part[:, None, :] * c[None]).astype(BF16).reshape(-1, RANK)
        half = jnp.tanh(dot(pairs, b_half, (1, 1)))
        code = codes[inside].reshape(-1, BLOCK)
        sampled = code > 0
        value = jnp.where(sampled, 1.0 - half * half, 0.0)
        weight[inside] = value.astype(BF16).reshape(SUB_I, DEPTH, BLOCK)
        twice = half + jnp.where(code == 2, -1.0, 1.0)
        twice = jnp.where(sampled, twice, 0.0).astype(BF16)
        accumulate(twice, pairs, a_part, c, b_half, to_a, to_c, to_bt, first_row)

    chunk_copy(weight, weight_to, left, step).start()

    @pl.when(step == STEPS - 1)
    def _():
        for k in range(STEPS):
            chunk_copy(weight, weight_to, left, k).wait()
        to_bt[...] = 0.5 * to_bt[...]
        fill_send(send, to_b, to_a, to_c, to_bt, jnp.zeros((ENTRY - 18, RANK), F32))


def moved_setup(from_wide, from_narrow, b, d_first, d_third, both):
    d_first[...] = dot(pick_main(), from_wide[...])
    d_third[...] = dot(pick_third(), from_wide[...])
    both[:, :RANK] = 0.25 * b[...]
    both[:, RANK:] = 0.25 * from_narrow[...]


def quarter_change(a_part, d_part, c, d_third, both):
    pairs = (a_part[:, None, :] * c[None]).astype(BF16).reshape(-1, RANK)
    mixed = d_part[:, None, :] * c[None] + a_part[:, None, :] * d_third[None]
    mixed = mixed.astype(BF16).reshape(-1, RANK)
    return pairs, dot(jnp.concatenate([mixed, pairs], axis=1), both, (1, 1))


def fold(x):
    return jnp.sum(x.reshape(-1, 8, BLOCK), axis=0)


def image_kernel(
    from_wide, from_narrow, weight_from, a, b, c, norm, send, to_b,
    weight, arrived, d_first, d_third, both, to_a, to_c, to_bt, total,
):
    step = pl.program_id(0)
    stream(weight_from, weight, arrived, step)

    @pl.when(step == 0)
    def _():
        moved_setup(from_wide, from_narrow, b, d_first, d_third, both)
        to_c[...] = jnp.zeros_like(to_c)
        to_bt[...] = jnp.zeros_like(to_bt)
        total[...] = jnp.zeros_like(total)

    third = c[...]
    for part in range(STEP_I // SUB_I):
        first_row = pl.multiple_of(step * STEP_I + part * SUB_I, SUB_I)
        inside = pl.ds(first_row, SUB_I)
        a_part = a[pl.ds(first_row, SUB_I), :]
        d_part = d_first[pl.ds(first_row, SUB_I), :]
        pairs, change = quarter_change(a_part, d_part, third, d_third[...], both[...])
        scaled = weight[inside].reshape(-1, BLOCK).astype(F32) * change
        total[...] += fold(scaled * change)
        accumulate(scaled.astype(BF16), pairs, a_part, third, b[...], to_a, to_c, to_bt, first_row)

    @pl.when(step == STEPS - 1)
    def _():
        energy = 4.0 * jnp.sum(total[:, :RANK] + total[:, RANK:], axis=0, keepdims=True)
        spare = jnp.concatenate([norm[0:1, :], energy, jnp.zeros((ENTRY - 20, RANK), F32)], axis=0)
        fill_send(send, to_b, to_a, to_c, to_bt, spare)


def energy_kernel(
    from_wide, from_narrow, weight_from, a, b, c, sums, send,
    weight, arrived, d_first, d_third, both, total,
):
    step = pl.program_id(0)
    stream(weight_from, weight, arrived, step)

    @pl.when(step == 0)
    def _():
        moved_setup(from_wide, from_narrow, b, d_first, d_third, both)
        total[...] = jnp.zeros_like(total)

    third = c[...]
    for part in range(STEP_I // SUB_I):
        first_row = pl.multiple_of(step * STEP_I + part * SUB_I, SUB_I)
        inside = pl.ds(first_row, SUB_I)
        a_part = a[pl.ds(first_row, SUB_I), :]
        d_part = d_first[pl.ds(first_row, SUB_I), :]
        _, change = quarter_change(a_part, d_part, third, d_third[...], both[...])
        total[...] += fold(weight[inside].reshape(-1, BLOCK).astype(F32) * change * change)

    @pl.when(step == STEPS - 1)
    def _():
        energy = 4.0 * jnp.sum(total[...], keepdims=True)
        norm = jnp.sum(sums[0:1, :], axis=1, keepdims=True)
        cross = jnp.sum(sums[1:2, :], axis=1, keepdims=True)
        lane = lax.broadcasted_iota(I32, (1, RANK), 1)
        row = jnp.where(lane == 0, norm, jnp.where(lane == 1, cross, energy))
        send[...] = jnp.broadcast_to(row, send.shape)


def pack_kernel(from_wide, to_b, send):
    width = send.shape[0] // SIDE
    third = dot_parts(pick_third(), from_wide[...])
    if width > 16 + DEPTH:
        spare = jnp.zeros((8, RANK), F32)
        for peer in range(SIDE):
            spare += from_wide[peer * ENTRY + 16 : peer * ENTRY + ENTRY, :]
        spare = jnp.concatenate([spare[2:], spare[:2]], axis=0)
        third = jnp.concatenate([third, spare], axis=0)
    for peer in range(SIDE):
        send[peer * width : peer * width + 16, :] = to_b[peer * 16 : peer * 16 + 16, :]
        send[peer * width + 16 : peer * width + width, :] = third


def inner(x, y):
    return jnp.sum(x * y, axis=0, keepdims=True)


def rows_of(*values):
    row = lax.broadcasted_iota(I32, (8, RANK), 0)
    out = jnp.broadcast_to(values[-1], (8, RANK))
    for k in range(len(values) - 1):
        out = jnp.where(row == k, values[k], out)
    return out


def residual_narrow_kernel(from_narrow, b_row, ib, fb, r_b, send, norm):
    rest = -(dot_parts(row_hot(b_row[...], 512), from_narrow[...]) + RIDGE * fb[...])
    r_b[...] = rest
    norm[...] = rows_of(inner(rest, rest))
    send[...] = gather(ib[...], rest)


def residual_wide_kernel(
    from_wide, from_narrow, a_row, c_row, ia, ic, count_third, fa, fc, part, r_a, r_c, send, norm
):
    rest_a = -(dot_parts(row_hot(a_row[...], 512), from_wide[...]) + RIDGE * fa[...])
    rest_c = -(dot_parts(row_hot(c_row[...], 512), from_narrow[...]) + RIDGE * fc[...])
    r_a[...] = rest_a
    r_c[...] = rest_c
    send[...] = wide_rows(ia[...], ic[...], rest_a, rest_c).astype(BF16)
    third = inner(rest_c, rest_c) * count_third[0:1, :]
    norm[...] = rows_of(part[0:1, :] + inner(rest_a, rest_a) + third)


def update_narrow_kernel(from_narrow, b_row, ib, r_b, n_b, send, sums, scalars):
    width = from_narrow.shape[0] // SIDE
    spare = jnp.zeros((8, RANK), F32)
    for peer in range(SIDE):
        spare += from_narrow[peer * width + 16 + DEPTH : (peer + 1) * width, :]
    norm = jnp.sum(spare[0:1], axis=1, keepdims=True)
    curved = RIDGE * norm + jnp.sum(spare[1:2], axis=1, keepdims=True)
    alpha = norm / curved
    image = dot_parts(row_hot(b_row[...], 512), from_narrow[...]) + RIDGE * r_b[...]
    rest = r_b[...] - alpha * image
    n_b[...] = rest
    send[...] = gather(ib[...], rest)
    sums[...] = rows_of(inner(rest, rest), inner(rest, image))
    scalars[...] = rows_of(norm, curved, alpha)


def update_wide_kernel(
    from_wide, from_narrow, a_row, c_row, ia, ic, count_third, r_a, r_c, part, scalars,
    n_a, n_c, send, sums,
):
    alpha = scalars[2:3, 0:1]
    image_a = dot_parts(row_hot(a_row[...], 512), from_wide[...]) + RIDGE * r_a[...]
    image_c = dot_parts(row_hot(c_row[...], 512), from_narrow[...]) + RIDGE * r_c[...]
    rest_a = r_a[...] - alpha * image_a
    rest_c = r_c[...] - alpha * image_c
    n_a[...] = rest_a
    n_c[...] = rest_c
    send[...] = wide_rows(ia[...], ic[...], rest_a, rest_c).astype(BF16)
    count = count_third[0:1, :]
    sums[...] = rows_of(
        part[0:1, :] + inner(rest_a, rest_a) + count * inner(rest_c, rest_c),
        part[1:2, :] + inner(rest_a, image_a) + count * inner(rest_c, image_c),
    )


def step_kernel(received, scalars, r_a, r_b, r_c, n_a, n_b, n_c, s_a, s_b, s_c):
    total = jnp.sum(received[...], axis=0, keepdims=True)
    new, cross, energy = total[:, 0:1], total[:, 1:2], total[:, 2:3]
    norm, curved, alpha = scalars[0:1, 0:1], scalars[1:2, 0:1], scalars[2:3, 0:1]
    beta = new / norm
    second = new / (RIDGE * new + energy + 2.0 * beta * cross + beta * beta * curved)
    for old, rest, out in ((r_a, n_a, s_a), (r_b, n_b, s_b), (r_c, n_c, s_c)):
        out[...] = alpha * old[...] + second * (rest[...] + beta * old[...])


def call(kernel, outs, *operands, name, limit=24):
    return pl.pallas_call(
        kernel,
        out_shape=outs,
        name=name,
        cost_estimate=pl.CostEstimate(flops=10**8, bytes_accessed=3 << 20, transcendentals=0),
        compiler_params=pltpu.CompilerParams(vmem_limit_bytes=limit << 20),
    )(*operands)


def block_call(kernel, outs, out_specs, in_specs, scratch, *operands, name):
    return pl.pallas_call(
        kernel,
        grid=(STEPS,),
        in_specs=in_specs,
        out_specs=out_specs,
        out_shape=outs,
        scratch_shapes=scratch,
        name=name,
        compiler_params=pltpu.CompilerParams(
            vmem_limit_bytes=50 << 20, dimension_semantics=("arbitrary",)
        ),
    )(*operands)


def exchange(x, axis):
    return lax.all_to_all(x, axis, split_axis=0, concat_axis=0, tiled=True)


def after(x, earlier):
    return lax.optimization_barrier((x, earlier))[0]


def local(entries, factor_a, factor_b, factor_c, index_a, index_b, index_c):
    rows = SIDE * ENTRY
    ia, ib, ic = index_a.reshape(1, BLOCK), index_b.reshape(1, BLOCK), index_c.reshape(1, DEPTH)
    rows_bf16, block_bf16 = struct((rows, RANK), BF16), struct((BLOCK, RANK), BF16)
    block_f32, rows_f32 = struct((BLOCK, RANK), F32), struct((rows, RANK), F32)
    small = struct((8, RANK), F32)
    table = struct((512, RANK), F32)

    send_narrow = call(
        first_narrow_kernel, rows_bf16, ib, ic, factor_b, name="first_narrow", limit=60
    )
    from_narrow = exchange(send_narrow, "narrow")
    send_wide = call(
        first_wide_kernel, rows_bf16, ia, ic, factor_a, factor_c, name="first_wide", limit=60
    )
    from_wide = exchange(after(send_wide, from_narrow), "wide")
    group_index = from_narrow.reshape(SIDE, ENTRY, RANK)[:, 16:18, :DEPTH].astype(F32)
    group_index = (group_index[:, 0] * 16.0 + group_index[:, 1]).astype(I32)

    def none(width):
        return jnp.full((SIDE, width), -1, I32)

    def place(*parts):
        return jnp.concatenate(parts, axis=1).reshape(1, -1)

    a_row = place(index_a.reshape(SIDE, 16), none(ENTRY - 16))

    def narrow_places(spare):
        return (
            place(index_b.reshape(SIDE, 16), none(DEPTH + spare)),
            place(none(16), group_index, none(spare)),
        )

    count_third = jnp.broadcast_to((lax.axis_index("narrow") == 0).astype(F32), (8, RANK))

    def give_back(send, to_b, spare):
        from_wide = exchange(send, "wide")
        width = 16 + DEPTH + spare
        send = call(pack_kernel, struct((SIDE * width, RANK), F32), from_wide, to_b, name="pack")
        return exchange(send, "narrow"), from_wide

    slab = pl.BlockSpec(memory_space=pl.ANY)
    cube = (BLOCK, DEPTH, BLOCK)
    arrivals = pltpu.SemaphoreType.DMA((STEPS,))
    both_scratch = [
        pltpu.VMEM(cube, BF16), arrivals,
        pltpu.VMEM((BLOCK, RANK), F32), pltpu.VMEM((DEPTH, RANK), F32),
        pltpu.VMEM((BLOCK, 2 * RANK), BF16),
    ]
    sum_scratch = [
        pltpu.VMEM((BLOCK, RANK), F32), pltpu.VMEM((DEPTH, RANK), F32),
        pltpu.VMEM((RANK, BLOCK), F32),
    ]
    total_scratch = [pltpu.VMEM((8, BLOCK), F32)]

    weight, send, to_b, a, b, c = block_call(
        gradient_kernel,
        (
            pltpu.HBM(cube, BF16), rows_f32, block_f32,
            block_f32, struct((BLOCK, RANK), BF16), struct((DEPTH, RANK), F32),
        ),
        (
            slab, full((rows, RANK)), full((BLOCK, RANK)),
            full((BLOCK, RANK)), full((BLOCK, RANK)), full((DEPTH, RANK)),
        ),
        [full((rows, RANK)), full((rows, RANK)), slab],
        [pltpu.VMEM(cube, I32), pltpu.VMEM(cube, BF16), arrivals, arrivals] + sum_scratch,
        from_wide, from_narrow, entries,
        name="gradient",
    )
    back_narrow, back_wide = give_back(send, to_b, 0)
    b_row, c_row = narrow_places(0)
    r_b, send_narrow, part = call(
        residual_narrow_kernel,
        (table, block_bf16, small),
        back_narrow, b_row, ib, factor_b,
        name="residual_narrow",
    )
    from_narrow = exchange(send_narrow, "narrow")
    r_a, r_c, send_wide, norm = call(
        residual_wide_kernel,
        (table, table, rows_bf16, small),
        back_wide, back_narrow, a_row, c_row, ia, ic, count_third, factor_a, factor_c, part,
        name="residual_wide",
    )
    from_wide = exchange(after(send_wide, from_narrow), "wide")
    fixed_specs = [
        full((rows, RANK)), full((BLOCK, RANK)), slab,
        full((BLOCK, RANK)), full((BLOCK, RANK)), full((DEPTH, RANK)), full((8, RANK)),
    ]
    send, to_b = block_call(
        image_kernel,
        (rows_f32, block_f32),
        (full((rows, RANK)), full((BLOCK, RANK))),
        fixed_specs,
        both_scratch + sum_scratch + total_scratch,
        from_wide, from_narrow, weight, a, b, c, norm,
        name="image",
    )
    back_narrow, back_wide = give_back(send, to_b, 8)
    b_row, c_row = narrow_places(8)
    n_b, send_narrow, part, scalars = call(
        update_narrow_kernel,
        (table, block_bf16, small, small),
        back_narrow, b_row, ib, r_b,
        name="update_narrow",
    )
    from_narrow = exchange(send_narrow, "narrow")
    n_a, n_c, send_wide, sums = call(
        update_wide_kernel,
        (table, table, rows_bf16, small),
        back_wide, back_narrow, a_row, c_row, ia, ic, count_third, r_a, r_c, part, scalars,
        name="update_wide",
    )
    from_wide = exchange(after(send_wide, from_narrow), "wide")
    partial = block_call(
        energy_kernel,
        block_f32,
        full((BLOCK, RANK)),
        fixed_specs,
        both_scratch + total_scratch,
        from_wide, from_narrow, weight, a, b, c, sums,
        name="energy",
    )
    received = exchange(partial, ("wide", "narrow"))
    return call(
        step_kernel,
        (table, table, table),
        received, scalars, r_a, r_b, r_c, n_a, n_b, n_c,
        name="step",
    )


def solution(mesh):
    placed = (
        P(("wide", "narrow"), None, None),
        P(("wide", "narrow"), None),
        P(("wide", "narrow"), None),
        P("wide", None),
        P(("wide", "narrow")),
        P(("wide", "narrow")),
        P(("wide", "narrow")),
    )
    return jax.shard_map(
        local,
        mesh=mesh,
        in_specs=placed,
        out_specs=(P(("wide", "narrow"), None), P(("wide", "narrow"), None), P("wide", None)),
        check_vma=False,
    )
```

```python
import jax
import jax.numpy as jnp
from jax import lax
from jax.experimental import pallas as pl
from jax.experimental.pallas import tpu as pltpu
from jax.sharding import PartitionSpec as P

RIDGE = 25.0
F32, BF16, I32 = jnp.float32, jnp.bfloat16, jnp.int32

RANK = 128
SIDE = 16
BLOCK = 256
DEPTH = 32
ENTRY = 24
STEP_I = 64
STEPS = BLOCK // STEP_I
AHEAD = 4
SUB_I = 8


def full(shape):
    return pl.BlockSpec(shape, lambda *_: (0,) * len(shape))


def struct(shape, dtype):
    return jax.ShapeDtypeStruct(shape, dtype)


def dot(x, y, dims=(1, 0)):
    return lax.dot_general(
        x, y, (((dims[0],), (dims[1],)), ((), ())), preferred_element_type=F32
    )


def hot(x):
    return jnp.where(x, 1.0, 0.0).astype(BF16)


def row_hot(index_row, height):
    columns = index_row.shape[1]
    return hot(lax.broadcasted_iota(I32, (height, columns), 0) == index_row)


def parts_of(x):
    high = x.astype(BF16).astype(F32)
    middle = (x - high).astype(BF16).astype(F32)
    return [high, middle, x - high - middle]


def spare_sums(x, first, width):
    k = lax.broadcasted_iota(I32, (8, x.shape[0]), 0)
    p = lax.broadcasted_iota(I32, (8, x.shape[0]), 1) % width - first
    return dot(hot((p >= 3 * k) & (p < 3 * k + 3) & (k < 2)), x)


def pick_main():
    q = lax.broadcasted_iota(I32, (BLOCK, SIDE * ENTRY), 0)
    p = lax.broadcasted_iota(I32, (BLOCK, SIDE * ENTRY), 1)
    return hot(p == (q >> 4) * ENTRY + (q & 15))


def pick_third():
    q = lax.broadcasted_iota(I32, (DEPTH, SIDE * ENTRY), 0)
    p = lax.broadcasted_iota(I32, (DEPTH, SIDE * ENTRY), 1)
    return hot(p == (q >> 1) * ENTRY + 16 + (q & 1))


def spread(width, per_peer, offset):
    shift = per_peer.bit_length() - 1
    p = lax.broadcasted_iota(I32, (SIDE * ENTRY, width), 0)
    q = lax.broadcasted_iota(I32, (SIDE * ENTRY, width), 1)
    return hot(p == (q >> shift) * ENTRY + offset + (q & (per_peer - 1)))


def gather(index_row, table):
    return dot(row_hot(index_row, 512), table.astype(BF16), (0, 0)).astype(BF16)


def wide_rows(ia, ic, table_a, table_c):
    return dot(spread(BLOCK, 16, 0), gather(ia, table_a)) + dot(
        spread(DEPTH, 2, 16), gather(ic, table_c)
    )


def first_narrow_kernel(ib, ic, fb, send):
    rows = dot(spread(BLOCK, 16, 0), gather(ib[...], fb[...]))
    lane = lax.broadcasted_iota(I32, (DEPTH, RANK), 1)
    to_lanes = hot(lane == lax.broadcasted_iota(I32, (DEPTH, RANK), 0))
    high, low = ((ic[...] >> 4).astype(BF16), (ic[...] & 15).astype(BF16))
    r = lax.broadcasted_iota(I32, (SIDE * ENTRY, 1), 0) % ENTRY
    rows = jnp.where(r == 16, dot(high, to_lanes), rows)
    rows = jnp.where(r == 17, dot(low, to_lanes), rows)
    send[...] = rows.astype(BF16)


def first_wide_kernel(ia, ic, fa, fc, send):
    send[...] = wide_rows(ia[...], ic[...], fa[...], fc[...]).astype(BF16)


def chunk_copy(source, held, arrived, k):
    here = pl.ds(k * STEP_I, STEP_I)
    return pltpu.make_async_copy(source.at[here], held.at[here], arrived.at[k])


def stream(source, held, arrived, step):
    @pl.when(step == 0)
    def _():
        for k in range(AHEAD):
            chunk_copy(source, held, arrived, k).start()

    @pl.when(step + AHEAD < STEPS)
    def _():
        chunk_copy(source, held, arrived, step + AHEAD).start()

    chunk_copy(source, held, arrived, step).wait()


def accumulate(upstream, pairs, a_part, c, b, to_a, to_c, to_bt, first_row):
    over = dot(upstream, b).reshape(SUB_I, DEPTH, RANK)
    to_a[pl.ds(first_row, SUB_I), :] = jnp.sum(over * c[None], axis=1)
    to_c[...] += jnp.sum(over * a_part[:, None, :], axis=0)
    to_bt[...] += dot(pairs, upstream, (0, 0))


def fill_send(send, to_b, acc_a, acc_c, acc_bt, spare, rows):
    to_b[...] = acc_bt[...].T
    for peer in range(SIDE):
        base = peer * ENTRY
        rows[base : base + 16, :] = acc_a[peer * 16 : peer * 16 + 16, :]
        tail = jnp.concatenate([acc_c[2 * peer : 2 * peer + 2, :], spare], axis=0)
        rows[base + 16 : base + ENTRY, :] = tail
    send[...] = rows[...].astype(BF16)


def gradient_kernel(
    from_wide, from_narrow, codes_from, weight_to, send, to_b, a_out, b_out, c_out,
    codes, weight, arrived, left, to_a, to_c, to_bt, rows,
):
    step = pl.program_id(0)
    stream(codes_from, codes, arrived, step)

    @pl.when(step == 0)
    def _():
        a_out[...] = dot(pick_main(), from_wide[...])
        c_out[...] = dot(pick_third(), from_wide[...])
        b_out[...] = dot(pick_main(), from_narrow[...]).astype(BF16)
        to_c[...] = jnp.zeros_like(to_c)
        to_bt[...] = jnp.zeros_like(to_bt)

    b_half = 0.5 * b_out[...]
    c = c_out[...]
    for part in range(STEP_I // SUB_I):
        first_row = pl.multiple_of(step * STEP_I + part * SUB_I, SUB_I)
        inside = pl.ds(first_row, SUB_I)
        a_part = a_out[pl.ds(first_row, SUB_I), :]
        pairs = (a_part[:, None, :] * c[None]).astype(BF16).reshape(-1, RANK)
        half = jnp.tanh(dot(pairs, b_half, (1, 1)))
        code = codes[inside].reshape(-1, BLOCK)
        sampled = code > 0
        value = jnp.where(sampled, 1.0 - half * half, 0.0)
        weight[inside] = value.astype(BF16).reshape(SUB_I, DEPTH, BLOCK)
        twice = half + jnp.where(code == 2, -1.0, 1.0)
        twice = jnp.where(sampled, twice, 0.0).astype(BF16)
        accumulate(twice, pairs, a_part, c, b_half, to_a, to_c, to_bt, first_row)

    chunk_copy(weight, weight_to, left, step).start()

    @pl.when(step == STEPS - 1)
    def _():
        for k in range(STEPS):
            chunk_copy(weight, weight_to, left, k).wait()
        to_bt[...] = 0.5 * to_bt[...]
        fill_send(send, to_b, to_a, to_c, to_bt, jnp.zeros((ENTRY - 18, RANK), F32), rows)


def moved_setup(from_wide, from_narrow, b, d_first, d_third, both):
    d_first[...] = dot(pick_main(), from_wide[...])
    d_third[...] = dot(pick_third(), from_wide[...])
    both[:, :RANK] = 0.25 * b[...]
    both[:, RANK:] = 0.25 * from_narrow[...]


def quarter_change(a_part, d_part, c, d_third, both):
    pairs = (a_part[:, None, :] * c[None]).astype(BF16).reshape(-1, RANK)
    mixed = d_part[:, None, :] * c[None] + a_part[:, None, :] * d_third[None]
    mixed = mixed.astype(BF16).reshape(-1, RANK)
    return pairs, dot(jnp.concatenate([mixed, pairs], axis=1), both, (1, 1))


def fold(x):
    return jnp.sum(x.reshape(-1, 8, BLOCK), axis=0)


def image_kernel(
    from_wide, from_narrow, weight_from, a, b, c, norm, send, to_b,
    weight, arrived, d_first, d_third, both, to_a, to_c, to_bt, rows, total,
):
    step = pl.program_id(0)
    stream(weight_from, weight, arrived, step)

    @pl.when(step == 0)
    def _():
        moved_setup(from_wide, from_narrow, b, d_first, d_third, both)
        to_c[...] = jnp.zeros_like(to_c)
        to_bt[...] = jnp.zeros_like(to_bt)
        total[...] = jnp.zeros_like(total)

    third = c[...]
    for part in range(STEP_I // SUB_I):
        first_row = pl.multiple_of(step * STEP_I + part * SUB_I, SUB_I)
        inside = pl.ds(first_row, SUB_I)
        a_part = a[pl.ds(first_row, SUB_I), :]
        d_part = d_first[pl.ds(first_row, SUB_I), :]
        pairs, change = quarter_change(a_part, d_part, third, d_third[...], both[...])
        scaled = weight[inside].reshape(-1, BLOCK).astype(F32) * change
        total[...] += fold(scaled * change)
        accumulate(scaled.astype(BF16), pairs, a_part, third, b[...], to_a, to_c, to_bt, first_row)

    @pl.when(step == STEPS - 1)
    def _():
        energy = 4.0 * jnp.sum(total[:, :RANK] + total[:, RANK:], axis=0, keepdims=True)
        spare = jnp.concatenate(parts_of(norm[0:1, :]) + parts_of(energy), axis=0)
        fill_send(send, to_b, to_a, to_c, to_bt, spare, rows)


def energy_kernel(
    from_wide, from_narrow, weight_from, a, b, c, sums, send,
    weight, arrived, d_first, d_third, both, total,
):
    step = pl.program_id(0)
    stream(weight_from, weight, arrived, step)

    @pl.when(step == 0)
    def _():
        moved_setup(from_wide, from_narrow, b, d_first, d_third, both)
        total[...] = jnp.zeros_like(total)

    third = c[...]
    for part in range(STEP_I // SUB_I):
        first_row = pl.multiple_of(step * STEP_I + part * SUB_I, SUB_I)
        inside = pl.ds(first_row, SUB_I)
        a_part = a[pl.ds(first_row, SUB_I), :]
        d_part = d_first[pl.ds(first_row, SUB_I), :]
        _, change = quarter_change(a_part, d_part, third, d_third[...], both[...])
        total[...] += fold(weight[inside].reshape(-1, BLOCK).astype(F32) * change * change)

    @pl.when(step == STEPS - 1)
    def _():
        energy = 4.0 * jnp.sum(total[...], keepdims=True)
        norm = jnp.sum(sums[0:1, :], axis=1, keepdims=True)
        cross = jnp.sum(sums[1:2, :], axis=1, keepdims=True)
        lane = lax.broadcasted_iota(I32, (1, RANK), 1)
        row = jnp.where(lane == 0, norm, jnp.where(lane == 1, cross, energy))
        send[...] = jnp.broadcast_to(row, send.shape)


def pack_kernel(from_wide, to_b, send, rows):
    width = send.shape[0] // SIDE
    third = dot(pick_third(), from_wide[...])
    if width > 16 + DEPTH:
        sums = spare_sums(from_wide[...], 18, ENTRY)
        spare = parts_of(sums[0:1]) + parts_of(sums[1:2]) + [jnp.zeros((2, RANK), F32)]
        third = jnp.concatenate([third] + spare, axis=0)
    for peer in range(SIDE):
        rows[peer * width : peer * width + 16, :] = to_b[peer * 16 : peer * 16 + 16, :]
        rows[peer * width + 16 : peer * width + width, :] = third
    send[...] = rows[...].astype(BF16)


def inner(x, y):
    return jnp.sum(x * y, axis=0, keepdims=True)


def rows_of(*values):
    row = lax.broadcasted_iota(I32, (8, RANK), 0)
    out = jnp.broadcast_to(values[-1], (8, RANK))
    for k in range(len(values) - 1):
        out = jnp.where(row == k, values[k], out)
    return out


def residual_narrow_kernel(from_narrow, b_row, ib, fb, r_b, send, norm):
    rest = -(dot(row_hot(b_row[...], 512), from_narrow[...]) + RIDGE * fb[...])
    r_b[...] = rest
    norm[...] = rows_of(inner(rest, rest))
    send[...] = gather(ib[...], rest)


def residual_wide_kernel(
    from_wide, from_narrow, a_row, c_row, ia, ic, count_third, fa, fc, part, r_a, r_c, send, norm
):
    rest_a = -(dot(row_hot(a_row[...], 512), from_wide[...]) + RIDGE * fa[...])
    rest_c = -(dot(row_hot(c_row[...], 512), from_narrow[...]) + RIDGE * fc[...])
    r_a[...] = rest_a
    r_c[...] = rest_c
    send[...] = wide_rows(ia[...], ic[...], rest_a, rest_c).astype(BF16)
    third = inner(rest_c, rest_c) * count_third[0:1, :]
    norm[...] = rows_of(part[0:1, :] + inner(rest_a, rest_a) + third)


def update_narrow_kernel(from_narrow, b_row, ib, r_b, n_b, send, sums, scalars):
    spare = spare_sums(from_narrow[...], 16 + DEPTH, from_narrow.shape[0] // SIDE)
    norm = jnp.sum(spare[0:1], axis=1, keepdims=True)
    curved = RIDGE * norm + jnp.sum(spare[1:2], axis=1, keepdims=True)
    alpha = norm / curved
    image = dot(row_hot(b_row[...], 512), from_narrow[...]) + RIDGE * r_b[...]
    rest = r_b[...] - alpha * image
    n_b[...] = rest
    send[...] = gather(ib[...], rest)
    sums[...] = rows_of(inner(rest, rest), inner(rest, image))
    scalars[...] = rows_of(norm, curved, alpha)


def update_wide_kernel(
    from_wide, from_narrow, a_row, c_row, ia, ic, count_third, r_a, r_c, part, scalars,
    n_a, n_c, send, sums,
):
    alpha = scalars[2:3, 0:1]
    image_a = dot(row_hot(a_row[...], 512), from_wide[...]) + RIDGE * r_a[...]
    image_c = dot(row_hot(c_row[...], 512), from_narrow[...]) + RIDGE * r_c[...]
    rest_a = r_a[...] - alpha * image_a
    rest_c = r_c[...] - alpha * image_c
    n_a[...] = rest_a
    n_c[...] = rest_c
    send[...] = wide_rows(ia[...], ic[...], rest_a, rest_c).astype(BF16)
    count = count_third[0:1, :]
    sums[...] = rows_of(
        part[0:1, :] + inner(rest_a, rest_a) + count * inner(rest_c, rest_c),
        part[1:2, :] + inner(rest_a, image_a) + count * inner(rest_c, image_c),
    )


def step_kernel(received, scalars, r_a, r_b, r_c, n_a, n_b, n_c, s_a, s_b, s_c):
    total = jnp.sum(received[...], axis=0, keepdims=True)
    new, cross, energy = total[:, 0:1], total[:, 1:2], total[:, 2:3]
    norm, curved, alpha = scalars[0:1, 0:1], scalars[1:2, 0:1], scalars[2:3, 0:1]
    beta = new / norm
    second = new / (RIDGE * new + energy + 2.0 * beta * cross + beta * beta * curved)
    for old, rest, out in ((r_a, n_a, s_a), (r_b, n_b, s_b), (r_c, n_c, s_c)):
        out[...] = alpha * old[...] + second * (rest[...] + beta * old[...])


def call(kernel, outs, *operands, name, limit=24, scratch=()):
    return pl.pallas_call(
        kernel,
        out_shape=outs,
        scratch_shapes=scratch,
        name=name,
        cost_estimate=pl.CostEstimate(flops=10**8, bytes_accessed=3 << 20, transcendentals=0),
        compiler_params=pltpu.CompilerParams(vmem_limit_bytes=limit << 20),
    )(*operands)


def block_call(kernel, outs, out_specs, in_specs, scratch, *operands, name):
    return pl.pallas_call(
        kernel,
        grid=(STEPS,),
        in_specs=in_specs,
        out_specs=out_specs,
        out_shape=outs,
        scratch_shapes=scratch,
        name=name,
        compiler_params=pltpu.CompilerParams(
            vmem_limit_bytes=50 << 20, dimension_semantics=("arbitrary",)
        ),
    )(*operands)


def exchange(x, axis):
    return lax.all_to_all(x, axis, split_axis=0, concat_axis=0, tiled=True)


def after(x, earlier):
    return lax.optimization_barrier((x, earlier))[0]


def local(entries, factor_a, factor_b, factor_c, index_a, index_b, index_c):
    rows = SIDE * ENTRY
    ia, ib, ic = index_a.reshape(1, BLOCK), index_b.reshape(1, BLOCK), index_c.reshape(1, DEPTH)
    rows_bf16, block_bf16 = struct((rows, RANK), BF16), struct((BLOCK, RANK), BF16)
    block_f32 = struct((BLOCK, RANK), F32)
    small = struct((8, RANK), F32)
    table = struct((512, RANK), F32)

    send_narrow = call(
        first_narrow_kernel, rows_bf16, ib, ic, factor_b, name="first_narrow", limit=60
    )
    from_narrow = exchange(send_narrow, "narrow")
    send_wide = call(
        first_wide_kernel, rows_bf16, ia, ic, factor_a, factor_c, name="first_wide", limit=60
    )
    from_wide = exchange(after(send_wide, from_narrow), "wide")
    group_index = from_narrow.reshape(SIDE, ENTRY, RANK)[:, 16:18, :DEPTH].astype(F32)
    group_index = (group_index[:, 0] * 16.0 + group_index[:, 1]).astype(I32)

    def none(width):
        return jnp.full((SIDE, width), -1, I32)

    def place(*parts):
        return jnp.concatenate(parts, axis=1).reshape(1, -1)

    a_row = place(index_a.reshape(SIDE, 16), none(ENTRY - 16))

    def narrow_places(spare):
        return (
            place(index_b.reshape(SIDE, 16), none(DEPTH + spare)),
            place(none(16), group_index, none(spare)),
        )

    count_third = jnp.broadcast_to((lax.axis_index("narrow") == 0).astype(F32), (8, RANK))

    def give_back(send, to_b, spare):
        from_wide = exchange(send, "wide")
        width = 16 + DEPTH + spare
        shape = (SIDE * width, RANK)
        send = call(
            pack_kernel, struct(shape, BF16), from_wide, to_b,
            name="pack", scratch=[pltpu.VMEM(shape, F32)],
        )
        return exchange(send, "narrow"), from_wide

    slab = pl.BlockSpec(memory_space=pl.ANY)
    cube = (BLOCK, DEPTH, BLOCK)
    arrivals = pltpu.SemaphoreType.DMA((STEPS,))
    both_scratch = [
        pltpu.VMEM(cube, BF16), arrivals,
        pltpu.VMEM((BLOCK, RANK), F32), pltpu.VMEM((DEPTH, RANK), F32),
        pltpu.VMEM((BLOCK, 2 * RANK), BF16),
    ]
    sum_scratch = [
        pltpu.VMEM((BLOCK, RANK), F32), pltpu.VMEM((DEPTH, RANK), F32),
        pltpu.VMEM((RANK, BLOCK), F32), pltpu.VMEM((rows, RANK), F32),
    ]
    total_scratch = [pltpu.VMEM((8, BLOCK), F32)]

    weight, send, to_b, a, b, c = block_call(
        gradient_kernel,
        (
            pltpu.HBM(cube, BF16), rows_bf16, block_f32,
            block_f32, struct((BLOCK, RANK), BF16), struct((DEPTH, RANK), F32),
        ),
        (
            slab, full((rows, RANK)), full((BLOCK, RANK)),
            full((BLOCK, RANK)), full((BLOCK, RANK)), full((DEPTH, RANK)),
        ),
        [full((rows, RANK)), full((rows, RANK)), slab],
        [pltpu.VMEM(cube, I32), pltpu.VMEM(cube, BF16), arrivals, arrivals] + sum_scratch,
        from_wide, from_narrow, entries,
        name="gradient",
    )
    back_narrow, back_wide = give_back(send, to_b, 0)
    b_row, c_row = narrow_places(0)
    r_b, send_narrow, part = call(
        residual_narrow_kernel,
        (table, block_bf16, small),
        back_narrow, b_row, ib, factor_b,
        name="residual_narrow",
    )
    from_narrow = exchange(send_narrow, "narrow")
    r_a, r_c, send_wide, norm = call(
        residual_wide_kernel,
        (table, table, rows_bf16, small),
        back_wide, back_narrow, a_row, c_row, ia, ic, count_third, factor_a, factor_c, part,
        name="residual_wide",
    )
    from_wide = exchange(after(send_wide, from_narrow), "wide")
    fixed_specs = [
        full((rows, RANK)), full((BLOCK, RANK)), slab,
        full((BLOCK, RANK)), full((BLOCK, RANK)), full((DEPTH, RANK)), full((8, RANK)),
    ]
    send, to_b = block_call(
        image_kernel,
        (rows_bf16, block_f32),
        (full((rows, RANK)), full((BLOCK, RANK))),
        fixed_specs,
        both_scratch + sum_scratch + total_scratch,
        from_wide, from_narrow, weight, a, b, c, norm,
        name="image",
    )
    back_narrow, back_wide = give_back(send, to_b, 8)
    b_row, c_row = narrow_places(8)
    n_b, send_narrow, part, scalars = call(
        update_narrow_kernel,
        (table, block_bf16, small, small),
        back_narrow, b_row, ib, r_b,
        name="update_narrow",
    )
    from_narrow = exchange(send_narrow, "narrow")
    n_a, n_c, send_wide, sums = call(
        update_wide_kernel,
        (table, table, rows_bf16, small),
        back_wide, back_narrow, a_row, c_row, ia, ic, count_third, r_a, r_c, part, scalars,
        name="update_wide",
    )
    from_wide = exchange(after(send_wide, from_narrow), "wide")
    partial = block_call(
        energy_kernel,
        block_f32,
        full((BLOCK, RANK)),
        fixed_specs,
        both_scratch + total_scratch,
        from_wide, from_narrow, weight, a, b, c, sums,
        name="energy",
    )
    received = exchange(partial, ("wide", "narrow"))
    return call(
        step_kernel,
        (table, table, table),
        received, scalars, r_a, r_b, r_c, n_a, n_b, n_c,
        name="step",
    )


def solution(mesh):
    placed = (
        P(("wide", "narrow"), None, None),
        P(("wide", "narrow"), None),
        P(("wide", "narrow"), None),
        P("wide", None),
        P(("wide", "narrow")),
        P(("wide", "narrow")),
        P(("wide", "narrow")),
    )
    return jax.shard_map(
        local,
        mesh=mesh,
        in_specs=placed,
        out_specs=(P(("wide", "narrow"), None), P(("wide", "narrow"), None), P("wide", None)),
        check_vma=False,
    )
```

```python
import jax
import jax.numpy as jnp
from jax import lax
from jax.experimental import pallas as pl
from jax.experimental.pallas import tpu as pltpu
from jax.sharding import PartitionSpec as P

RIDGE = 25.0
F32, BF16, I32 = jnp.float32, jnp.bfloat16, jnp.int32

RANK = 128
SIDE = 16
BLOCK = 256
DEPTH = 32
ENTRY = 24
STEP_I = 64
STEPS = BLOCK // STEP_I
AHEAD = 4
SUB_I = 8
WIDE_SUB = 16


def full(shape):
    return pl.BlockSpec(shape, lambda *_: (0,) * len(shape))


def struct(shape, dtype):
    return jax.ShapeDtypeStruct(shape, dtype)


def dot(x, y, dims=(1, 0)):
    return lax.dot_general(
        x, y, (((dims[0],), (dims[1],)), ((), ())), preferred_element_type=F32
    )


def hot(x):
    return jnp.where(x, 1.0, 0.0).astype(BF16)


def row_hot(index_row, height):
    columns = index_row.shape[1]
    return hot(lax.broadcasted_iota(I32, (height, columns), 0) == index_row)


def parts_of(x):
    high = x.astype(BF16).astype(F32)
    middle = (x - high).astype(BF16).astype(F32)
    return [high, middle, x - high - middle]


def spare_sums(x, first, width):
    k = lax.broadcasted_iota(I32, (8, x.shape[0]), 0)
    p = lax.broadcasted_iota(I32, (8, x.shape[0]), 1) % width - first
    return dot(hot((p >= 3 * k) & (p < 3 * k + 3) & (k < 2)), x)


def pick_main():
    q = lax.broadcasted_iota(I32, (BLOCK, SIDE * ENTRY), 0)
    p = lax.broadcasted_iota(I32, (BLOCK, SIDE * ENTRY), 1)
    return hot(p == (q >> 4) * ENTRY + (q & 15))


def pick_third():
    q = lax.broadcasted_iota(I32, (DEPTH, SIDE * ENTRY), 0)
    p = lax.broadcasted_iota(I32, (DEPTH, SIDE * ENTRY), 1)
    return hot(p == (q >> 1) * ENTRY + 16 + (q & 1))


def spread(width, per_peer, offset):
    shift = per_peer.bit_length() - 1
    p = lax.broadcasted_iota(I32, (SIDE * ENTRY, width), 0)
    q = lax.broadcasted_iota(I32, (SIDE * ENTRY, width), 1)
    return hot(p == (q >> shift) * ENTRY + offset + (q & (per_peer - 1)))


def gather(index_row, table):
    return dot(row_hot(index_row, 512), table.astype(BF16), (0, 0)).astype(BF16)


def wide_rows(ia, ic, table_a, table_c):
    return dot(spread(BLOCK, 16, 0), gather(ia, table_a)) + dot(
        spread(DEPTH, 2, 16), gather(ic, table_c)
    )


def first_narrow_kernel(ib, ic, fb_from, send, fb, arrived):
    copy = pltpu.make_async_copy(fb_from, fb, arrived)
    copy.start()
    chosen = row_hot(ib[...], 512)
    places = spread(BLOCK, 16, 0)
    lane = lax.broadcasted_iota(I32, (DEPTH, RANK), 1)
    to_lanes = hot(lane == lax.broadcasted_iota(I32, (DEPTH, RANK), 0))
    high, low = ((ic[...] >> 4).astype(BF16), (ic[...] & 15).astype(BF16))
    high, low = dot(high, to_lanes), dot(low, to_lanes)
    r = lax.broadcasted_iota(I32, (SIDE * ENTRY, 1), 0) % ENTRY
    copy.wait()
    rows = dot(places, dot(chosen, fb[...].astype(BF16), (0, 0)).astype(BF16))
    rows = jnp.where(r == 16, high, rows)
    rows = jnp.where(r == 17, low, rows)
    send[...] = rows.astype(BF16)


def first_wide_kernel(ia, ic, fa, fc, send):
    send[...] = wide_rows(ia[...], ic[...], fa[...], fc[...]).astype(BF16)


def chunk_copy(source, held, arrived, k):
    here = pl.ds(k * STEP_I, STEP_I)
    return pltpu.make_async_copy(source.at[here], held.at[here], arrived.at[k])


def bring(source, held, arrived, step):
    @pl.when(step == 0)
    def _():
        for k in range(AHEAD):
            chunk_copy(source, held, arrived, k).start()

    @pl.when(step + AHEAD < STEPS)
    def _():
        chunk_copy(source, held, arrived, step + AHEAD).start()


def accumulate(upstream, pairs, a_part, c, b, to_a, to_c, to_bt, first_row):
    over = dot(upstream, b).reshape(-1, DEPTH, RANK)
    to_a[pl.ds(first_row, a_part.shape[0]), :] = jnp.sum(over * c[None], axis=1)
    to_c[...] += jnp.sum(over * a_part[:, None, :], axis=0)
    to_bt[...] += dot(pairs, upstream, (0, 0))


def fill_send(send, to_b, acc_a, acc_c, acc_bt, spare, rows):
    to_b[...] = acc_bt[...].T
    for peer in range(SIDE):
        base = peer * ENTRY
        rows[base : base + 16, :] = acc_a[peer * 16 : peer * 16 + 16, :]
        tail = jnp.concatenate([acc_c[2 * peer : 2 * peer + 2, :], spare], axis=0)
        rows[base + 16 : base + ENTRY, :] = tail
    send[...] = rows[...].astype(BF16)


def gradient_kernel(
    from_wide, from_narrow, codes_from, send, to_b, a_out, b_out, c_out,
    codes, arrived, to_a, to_c, to_bt, rows,
):
    step = pl.program_id(0)
    bring(codes_from, codes, arrived, step)

    @pl.when(step == 0)
    def _():
        a_out[...] = dot(pick_main(), from_wide[...])
        c_out[...] = dot(pick_third(), from_wide[...])
        b_out[...] = dot(pick_main(), from_narrow[...]).astype(BF16)
        to_c[...] = jnp.zeros_like(to_c)
        to_bt[...] = jnp.zeros_like(to_bt)

    b_half = 0.5 * b_out[...]
    c = c_out[...]
    chunk_copy(codes_from, codes, arrived, step).wait()
    for part in range(STEP_I // WIDE_SUB):
        first_row = pl.multiple_of(step * STEP_I + part * WIDE_SUB, WIDE_SUB)
        a_part = a_out[pl.ds(first_row, WIDE_SUB), :]
        pairs = (a_part[:, None, :] * c[None]).astype(BF16).reshape(-1, RANK)
        half = jnp.tanh(dot(pairs, b_half, (1, 1)))
        code = codes[pl.ds(first_row, WIDE_SUB)].reshape(-1, BLOCK)
        twice = half + jnp.where(code == 2, -1.0, 1.0)
        twice = jnp.where(code > 0, twice, 0.0).astype(BF16)
        accumulate(twice, pairs, a_part, c, b_half, to_a, to_c, to_bt, first_row)

    @pl.when(step == STEPS - 1)
    def _():
        to_bt[...] = 0.5 * to_bt[...]
        fill_send(send, to_b, to_a, to_c, to_bt, jnp.zeros((ENTRY - 18, RANK), F32), rows)


def weight_kernel(codes_from, a, b, c, weight_to, codes, weight, arrived, left):
    step = pl.program_id(0)
    bring(codes_from, codes, arrived, step)
    b_half = 0.5 * b[...]
    chunk_copy(codes_from, codes, arrived, step).wait()
    for part in range(STEP_I // WIDE_SUB):
        first_row = pl.multiple_of(step * STEP_I + part * WIDE_SUB, WIDE_SUB)
        inside = pl.ds(first_row, WIDE_SUB)
        pairs = (a[inside, :][:, None, :] * c[...][None]).astype(BF16).reshape(-1, RANK)
        half = jnp.tanh(dot(pairs, b_half, (1, 1)))
        value = jnp.where(codes[inside].reshape(-1, BLOCK) > 0, 1.0 - half * half, 0.0)
        weight[inside] = value.astype(BF16).reshape(WIDE_SUB, DEPTH, BLOCK)
    chunk_copy(weight, weight_to, left, step).start()

    @pl.when(step == STEPS - 1)
    def _():
        for k in range(STEPS):
            chunk_copy(weight, weight_to, left, k).wait()


def moved_setup(from_wide, from_narrow, b, d_first, d_third, both):
    d_first[...] = dot(pick_main(), from_wide[...])
    d_third[...] = dot(pick_third(), from_wide[...])
    both[:, :RANK] = 0.25 * b[...]
    both[:, RANK:] = 0.25 * from_narrow[...]


def quarter_change(a_part, d_part, c, d_third, both):
    pairs = (a_part[:, None, :] * c[None]).astype(BF16).reshape(-1, RANK)
    mixed = d_part[:, None, :] * c[None] + a_part[:, None, :] * d_third[None]
    mixed = mixed.astype(BF16).reshape(-1, RANK)
    return pairs, dot(jnp.concatenate([mixed, pairs], axis=1), both, (1, 1))


def fold(x):
    return jnp.sum(x.reshape(-1, 8, BLOCK), axis=0)


def image_kernel(
    from_wide, from_narrow, weight_from, a, b, c, norm, send, to_b,
    weight, arrived, d_first, d_third, both, to_a, to_c, to_bt, rows, total,
):
    step = pl.program_id(0)
    bring(weight_from, weight, arrived, step)

    @pl.when(step == 0)
    def _():
        moved_setup(from_wide, from_narrow, b, d_first, d_third, both)
        to_c[...] = jnp.zeros_like(to_c)
        to_bt[...] = jnp.zeros_like(to_bt)
        total[...] = jnp.zeros_like(total)

    third = c[...]
    chunk_copy(weight_from, weight, arrived, step).wait()
    for part in range(STEP_I // SUB_I):
        first_row = pl.multiple_of(step * STEP_I + part * SUB_I, SUB_I)
        inside = pl.ds(first_row, SUB_I)
        a_part = a[pl.ds(first_row, SUB_I), :]
        d_part = d_first[pl.ds(first_row, SUB_I), :]
        pairs, change = quarter_change(a_part, d_part, third, d_third[...], both[...])
        scaled = weight[inside].reshape(-1, BLOCK).astype(F32) * change
        total[...] += fold(scaled * change)
        accumulate(scaled.astype(BF16), pairs, a_part, third, b[...], to_a, to_c, to_bt, first_row)

    @pl.when(step == STEPS - 1)
    def _():
        energy = 4.0 * jnp.sum(total[:, :RANK] + total[:, RANK:], axis=0, keepdims=True)
        spare = jnp.concatenate(parts_of(norm[0:1, :]) + parts_of(energy), axis=0)
        fill_send(send, to_b, to_a, to_c, to_bt, spare, rows)


def energy_kernel(
    from_wide, from_narrow, weight_from, a, b, c, sums, send,
    weight, arrived, d_first, d_third, both, total,
):
    step = pl.program_id(0)
    bring(weight_from, weight, arrived, step)

    @pl.when(step == 0)
    def _():
        moved_setup(from_wide, from_narrow, b, d_first, d_third, both)
        total[...] = jnp.zeros_like(total)

    third = c[...]
    chunk_copy(weight_from, weight, arrived, step).wait()
    for part in range(STEP_I // SUB_I):
        first_row = pl.multiple_of(step * STEP_I + part * SUB_I, SUB_I)
        inside = pl.ds(first_row, SUB_I)
        a_part = a[pl.ds(first_row, SUB_I), :]
        d_part = d_first[pl.ds(first_row, SUB_I), :]
        _, change = quarter_change(a_part, d_part, third, d_third[...], both[...])
        total[...] += fold(weight[inside].reshape(-1, BLOCK).astype(F32) * change * change)

    @pl.when(step == STEPS - 1)
    def _():
        energy = 4.0 * jnp.sum(total[...], keepdims=True)
        norm = jnp.sum(sums[0:1, :], axis=1, keepdims=True)
        cross = jnp.sum(sums[1:2, :], axis=1, keepdims=True)
        lane = lax.broadcasted_iota(I32, (1, RANK), 1)
        row = jnp.where(lane == 0, norm, jnp.where(lane == 1, cross, energy))
        send[...] = jnp.broadcast_to(row, send.shape)


def pack_kernel(from_wide, to_b, send, rows):
    width = send.shape[0] // SIDE
    third = dot(pick_third(), from_wide[...])
    if width > 16 + DEPTH:
        sums = spare_sums(from_wide[...], 18, ENTRY)
        spare = parts_of(sums[0:1]) + parts_of(sums[1:2]) + [jnp.zeros((2, RANK), F32)]
        third = jnp.concatenate([third] + spare, axis=0)
    for peer in range(SIDE):
        rows[peer * width : peer * width + 16, :] = to_b[peer * 16 : peer * 16 + 16, :]
        rows[peer * width + 16 : peer * width + width, :] = third
    send[...] = rows[...].astype(BF16)


def inner(x, y):
    return jnp.sum(x * y, axis=0, keepdims=True)


def rows_of(*values):
    row = lax.broadcasted_iota(I32, (8, RANK), 0)
    out = jnp.broadcast_to(values[-1], (8, RANK))
    for k in range(len(values) - 1):
        out = jnp.where(row == k, values[k], out)
    return out


def residual_narrow_kernel(from_narrow, b_row, ib, fb, r_b, send, norm):
    rest = -(dot(row_hot(b_row[...], 512), from_narrow[...]) + RIDGE * fb[...])
    r_b[...] = rest
    norm[...] = rows_of(inner(rest, rest))
    send[...] = gather(ib[...], rest)


def residual_wide_kernel(
    from_wide, from_narrow, a_row, c_row, ia, ic, count_third, fa, fc, part, r_a, r_c, send, norm
):
    rest_a = -(dot(row_hot(a_row[...], 512), from_wide[...]) + RIDGE * fa[...])
    rest_c = -(dot(row_hot(c_row[...], 512), from_narrow[...]) + RIDGE * fc[...])
    r_a[...] = rest_a
    r_c[...] = rest_c
    send[...] = wide_rows(ia[...], ic[...], rest_a, rest_c).astype(BF16)
    third = inner(rest_c, rest_c) * count_third[0:1, :]
    norm[...] = rows_of(part[0:1, :] + inner(rest_a, rest_a) + third)


def update_narrow_kernel(from_narrow, b_row, ib, r_b, n_b, send, sums, scalars):
    spare = spare_sums(from_narrow[...], 16 + DEPTH, from_narrow.shape[0] // SIDE)
    norm = jnp.sum(spare[0:1], axis=1, keepdims=True)
    curved = RIDGE * norm + jnp.sum(spare[1:2], axis=1, keepdims=True)
    alpha = norm / curved
    image = dot(row_hot(b_row[...], 512), from_narrow[...]) + RIDGE * r_b[...]
    rest = r_b[...] - alpha * image
    n_b[...] = rest
    send[...] = gather(ib[...], rest)
    sums[...] = rows_of(inner(rest, rest), inner(rest, image))
    scalars[...] = rows_of(norm, curved, alpha)


def update_wide_kernel(
    from_wide, from_narrow, a_row, c_row, ia, ic, count_third, r_a, r_c, part, scalars,
    n_a, n_c, send, sums,
):
    alpha = scalars[2:3, 0:1]
    image_a = dot(row_hot(a_row[...], 512), from_wide[...]) + RIDGE * r_a[...]
    image_c = dot(row_hot(c_row[...], 512), from_narrow[...]) + RIDGE * r_c[...]
    rest_a = r_a[...] - alpha * image_a
    rest_c = r_c[...] - alpha * image_c
    n_a[...] = rest_a
    n_c[...] = rest_c
    send[...] = wide_rows(ia[...], ic[...], rest_a, rest_c).astype(BF16)
    count = count_third[0:1, :]
    sums[...] = rows_of(
        part[0:1, :] + inner(rest_a, rest_a) + count * inner(rest_c, rest_c),
        part[1:2, :] + inner(rest_a, image_a) + count * inner(rest_c, image_c),
    )


def step_kernel(received, scalars, r_a, r_b, r_c, n_a, n_b, n_c, s_a, s_b, s_c):
    total = jnp.sum(received[...], axis=0, keepdims=True)
    new, cross, energy = total[:, 0:1], total[:, 1:2], total[:, 2:3]
    norm, curved, alpha = scalars[0:1, 0:1], scalars[1:2, 0:1], scalars[2:3, 0:1]
    beta = new / norm
    second = new / (RIDGE * new + energy + 2.0 * beta * cross + beta * beta * curved)
    for old, rest, out in ((r_a, n_a, s_a), (r_b, n_b, s_b), (r_c, n_c, s_c)):
        out[...] = alpha * old[...] + second * (rest[...] + beta * old[...])


def call(kernel, outs, *operands, name, limit=24, scratch=(), **specs):
    return pl.pallas_call(
        kernel,
        out_shape=outs,
        scratch_shapes=scratch,
        name=name,
        **specs,
        cost_estimate=pl.CostEstimate(flops=10**8, bytes_accessed=3 << 20, transcendentals=0),
        compiler_params=pltpu.CompilerParams(vmem_limit_bytes=limit << 20),
    )(*operands)


def block_call(kernel, outs, out_specs, in_specs, scratch, *operands, name, cost=5 * 10**9):
    return pl.pallas_call(
        kernel,
        grid=(STEPS,),
        in_specs=in_specs,
        out_specs=out_specs,
        out_shape=outs,
        scratch_shapes=scratch,
        name=name,
        cost_estimate=pl.CostEstimate(flops=cost, bytes_accessed=12 << 20, transcendentals=0),
        compiler_params=pltpu.CompilerParams(
            vmem_limit_bytes=50 << 20, dimension_semantics=("arbitrary",)
        ),
    )(*operands)


def exchange(x, axis):
    return lax.all_to_all(x, axis, split_axis=0, concat_axis=0, tiled=True)


def after(x, earlier):
    return lax.optimization_barrier((x, earlier))[0]


def local(entries, factor_a, factor_b, factor_c, index_a, index_b, index_c):
    rows = SIDE * ENTRY
    ia, ib, ic = index_a.reshape(1, BLOCK), index_b.reshape(1, BLOCK), index_c.reshape(1, DEPTH)
    rows_bf16, block_bf16 = struct((rows, RANK), BF16), struct((BLOCK, RANK), BF16)
    block_f32 = struct((BLOCK, RANK), F32)
    small = struct((8, RANK), F32)
    table = struct((512, RANK), F32)

    send_narrow = call(
        first_narrow_kernel, rows_bf16, ib, ic, factor_b, name="first_narrow", limit=60,
        scratch=[pltpu.VMEM((512, RANK), F32), pltpu.SemaphoreType.DMA(())],
        in_specs=[full((1, BLOCK)), full((1, DEPTH)), pl.BlockSpec(memory_space=pl.ANY)],
    )
    from_narrow = exchange(send_narrow, "narrow")
    send_wide = call(
        first_wide_kernel, rows_bf16, ia, ic, factor_a, factor_c, name="first_wide", limit=60
    )
    from_wide = exchange(after(send_wide, from_narrow), "wide")
    group_index = from_narrow.reshape(SIDE, ENTRY, RANK)[:, 16:18, :DEPTH].astype(F32)
    group_index = (group_index[:, 0] * 16.0 + group_index[:, 1]).astype(I32)

    def none(width):
        return jnp.full((SIDE, width), -1, I32)

    def place(*parts):
        return jnp.concatenate(parts, axis=1).reshape(1, -1)

    a_row = place(index_a.reshape(SIDE, 16), none(ENTRY - 16))

    def narrow_places(spare):
        return (
            place(index_b.reshape(SIDE, 16), none(DEPTH + spare)),
            place(none(16), group_index, none(spare)),
        )

    count_third = jnp.broadcast_to((lax.axis_index("narrow") == 0).astype(F32), (8, RANK))

    def give_back(send, to_b, spare):
        from_wide = exchange(send, "wide")
        width = 16 + DEPTH + spare
        shape = (SIDE * width, RANK)
        send = call(
            pack_kernel, struct(shape, BF16), from_wide, to_b,
            name="pack", scratch=[pltpu.VMEM(shape, F32)],
        )
        return exchange(send, "narrow"), from_wide

    slab = pl.BlockSpec(memory_space=pl.ANY)
    cube = (BLOCK, DEPTH, BLOCK)
    arrivals = pltpu.SemaphoreType.DMA((STEPS,))
    both_scratch = [
        pltpu.VMEM(cube, BF16), arrivals,
        pltpu.VMEM((BLOCK, RANK), F32), pltpu.VMEM((DEPTH, RANK), F32),
        pltpu.VMEM((BLOCK, 2 * RANK), BF16),
    ]
    sum_scratch = [
        pltpu.VMEM((BLOCK, RANK), F32), pltpu.VMEM((DEPTH, RANK), F32),
        pltpu.VMEM((RANK, BLOCK), F32), pltpu.VMEM((rows, RANK), F32),
    ]
    total_scratch = [pltpu.VMEM((8, BLOCK), F32)]

    send, to_b, a, b, c = block_call(
        gradient_kernel,
        (rows_bf16, block_f32, block_f32, block_bf16, struct((DEPTH, RANK), F32)),
        (
            full((rows, RANK)), full((BLOCK, RANK)), full((BLOCK, RANK)), full((BLOCK, RANK)),
            full((DEPTH, RANK)),
        ),
        [full((rows, RANK)), full((rows, RANK)), slab],
        [pltpu.VMEM(cube, I32), arrivals] + sum_scratch,
        from_wide, from_narrow, entries,
        name="gradient",
    )
    weight = block_call(
        weight_kernel,
        pltpu.HBM(cube, BF16),
        slab,
        [slab, full((BLOCK, RANK)), full((BLOCK, RANK)), full((DEPTH, RANK))],
        [pltpu.VMEM(cube, I32), pltpu.VMEM(cube, BF16), arrivals, arrivals],
        entries, a, b, c,
        name="weight", cost=6 * 10**9,
    )
    back_narrow, back_wide = give_back(send, to_b, 0)
    b_row, c_row = narrow_places(0)
    r_b, send_narrow, part = call(
        residual_narrow_kernel,
        (table, block_bf16, small),
        back_narrow, b_row, ib, factor_b,
        name="residual_narrow",
    )
    from_narrow = exchange(send_narrow, "narrow")
    r_a, r_c, send_wide, norm = call(
        residual_wide_kernel,
        (table, table, rows_bf16, small),
        back_wide, back_narrow, a_row, c_row, ia, ic, count_third, factor_a, factor_c, part,
        name="residual_wide",
    )
    from_wide = exchange(after(send_wide, from_narrow), "wide")
    fixed_specs = [
        full((rows, RANK)), full((BLOCK, RANK)), slab,
        full((BLOCK, RANK)), full((BLOCK, RANK)), full((DEPTH, RANK)), full((8, RANK)),
    ]
    send, to_b = block_call(
        image_kernel,
        (rows_bf16, block_f32),
        (full((rows, RANK)), full((BLOCK, RANK))),
        fixed_specs,
        both_scratch + sum_scratch + total_scratch,
        from_wide, from_narrow, weight, a, b, c, norm,
        name="image",
    )
    back_narrow, back_wide = give_back(send, to_b, 8)
    b_row, c_row = narrow_places(8)
    n_b, send_narrow, part, scalars = call(
        update_narrow_kernel,
        (table, block_bf16, small, small),
        back_narrow, b_row, ib, r_b,
        name="update_narrow",
    )
    from_narrow = exchange(send_narrow, "narrow")
    n_a, n_c, send_wide, sums = call(
        update_wide_kernel,
        (table, table, rows_bf16, small),
        back_wide, back_narrow, a_row, c_row, ia, ic, count_third, r_a, r_c, part, scalars,
        name="update_wide",
    )
    from_wide = exchange(after(send_wide, from_narrow), "wide")
    partial = block_call(
        energy_kernel,
        block_f32,
        full((BLOCK, RANK)),
        fixed_specs,
        both_scratch + total_scratch,
        from_wide, from_narrow, weight, a, b, c, sums,
        name="energy",
    )
    received = exchange(partial, ("wide", "narrow"))
    return call(
        step_kernel,
        (table, table, table),
        received, scalars, r_a, r_b, r_c, n_a, n_b, n_c,
        name="step",
    )


def solution(mesh):
    placed = (
        P(("wide", "narrow"), None, None),
        P(("wide", "narrow"), None),
        P(("wide", "narrow"), None),
        P("wide", None),
        P(("wide", "narrow")),
        P(("wide", "narrow")),
        P(("wide", "narrow")),
    )
    return jax.shard_map(
        local,
        mesh=mesh,
        in_specs=placed,
        out_specs=(P(("wide", "narrow"), None), P(("wide", "narrow"), None), P("wide", None)),
        check_vma=False,
    )
```

```python
import jax
import jax.numpy as jnp
from jax import lax
from jax.experimental import pallas as pl
from jax.experimental.pallas import tpu as pltpu
from jax.sharding import PartitionSpec as P

RIDGE = 25.0
F32, BF16, I32 = jnp.float32, jnp.bfloat16, jnp.int32

RANK = 128
SIDE = 16
BLOCK = 256
DEPTH = 32
ENTRY = 24
STEP_I = 64
STEPS = BLOCK // STEP_I
AHEAD = 4
SUB_I = 8
WIDE_SUB = 16


def full(shape):
    return pl.BlockSpec(shape, lambda *_: (0,) * len(shape))


def struct(shape, dtype):
    return jax.ShapeDtypeStruct(shape, dtype)


def dot(x, y, dims=(1, 0)):
    return lax.dot_general(
        x, y, (((dims[0],), (dims[1],)), ((), ())), preferred_element_type=F32
    )


def hot(x):
    return jnp.where(x, 1.0, 0.0).astype(BF16)


def row_hot(index_row, height):
    columns = index_row.shape[1]
    return hot(lax.broadcasted_iota(I32, (height, columns), 0) == index_row)


def parts_of(x):
    high = x.astype(BF16).astype(F32)
    middle = (x - high).astype(BF16).astype(F32)
    return [high, middle, x - high - middle]


def spare_sums(x, first, width):
    k = lax.broadcasted_iota(I32, (8, x.shape[0]), 0)
    p = lax.broadcasted_iota(I32, (8, x.shape[0]), 1) % width - first
    return dot(hot((p >= 3 * k) & (p < 3 * k + 3) & (k < 2)), x)


def pick_main():
    q = lax.broadcasted_iota(I32, (BLOCK, SIDE * ENTRY), 0)
    p = lax.broadcasted_iota(I32, (BLOCK, SIDE * ENTRY), 1)
    return hot(p == (q >> 4) * ENTRY + (q & 15))


def pick_third():
    q = lax.broadcasted_iota(I32, (DEPTH, SIDE * ENTRY), 0)
    p = lax.broadcasted_iota(I32, (DEPTH, SIDE * ENTRY), 1)
    return hot(p == (q >> 1) * ENTRY + 16 + (q & 1))


def spread(width, per_peer, offset):
    shift = per_peer.bit_length() - 1
    p = lax.broadcasted_iota(I32, (SIDE * ENTRY, width), 0)
    q = lax.broadcasted_iota(I32, (SIDE * ENTRY, width), 1)
    return hot(p == (q >> shift) * ENTRY + offset + (q & (per_peer - 1)))


def gather(index_row, table):
    return dot(row_hot(index_row, 512), table.astype(BF16), (0, 0)).astype(BF16)


def wide_rows(ia, ic, table_a, table_c):
    return dot(spread(BLOCK, 16, 0), gather(ia, table_a)) + dot(
        spread(DEPTH, 2, 16), gather(ic, table_c)
    )


def first_narrow_kernel(ib, ic, fb, send):
    rows = dot(spread(BLOCK, 16, 0), gather(ib[...], fb[...]))
    lane = lax.broadcasted_iota(I32, (DEPTH, RANK), 1)
    to_lanes = hot(lane == lax.broadcasted_iota(I32, (DEPTH, RANK), 0))
    high, low = ((ic[...] >> 4).astype(BF16), (ic[...] & 15).astype(BF16))
    r = lax.broadcasted_iota(I32, (SIDE * ENTRY, 1), 0) % ENTRY
    rows = jnp.where(r == 16, dot(high, to_lanes), rows)
    rows = jnp.where(r == 17, dot(low, to_lanes), rows)
    send[...] = rows.astype(BF16)


def first_wide_kernel(ia, ic, fa, fc, send):
    send[...] = wide_rows(ia[...], ic[...], fa[...], fc[...]).astype(BF16)


def chunk_copy(source, held, arrived, k):
    here = pl.ds(k * STEP_I, STEP_I)
    return pltpu.make_async_copy(source.at[here], held.at[here], arrived.at[k])


def bring(source, held, arrived, step):
    @pl.when(step == 0)
    def _():
        for k in range(AHEAD):
            chunk_copy(source, held, arrived, k).start()

    @pl.when(step + AHEAD < STEPS)
    def _():
        chunk_copy(source, held, arrived, step + AHEAD).start()


def accumulate(upstream, pairs, a_part, c, b, to_a, to_c, to_bt, first_row):
    over = dot(upstream, b).reshape(-1, DEPTH, RANK)
    to_a[pl.ds(first_row, a_part.shape[0]), :] = jnp.sum(over * c[None], axis=1)
    to_c[...] += jnp.sum(over * a_part[:, None, :], axis=0)
    to_bt[...] += dot(pairs, upstream, (0, 0))


def fill_send(send, to_b, acc_a, acc_c, acc_bt, spare, rows):
    to_b[...] = acc_bt[...].T
    for peer in range(SIDE):
        base = peer * ENTRY
        rows[base : base + 16, :] = acc_a[peer * 16 : peer * 16 + 16, :]
        tail = jnp.concatenate([acc_c[2 * peer : 2 * peer + 2, :], spare], axis=0)
        rows[base + 16 : base + ENTRY, :] = tail
    send[...] = rows[...].astype(BF16)


def gradient_kernel(
    from_wide, from_narrow, codes_from, send, to_b, a_out, b_out, c_out,
    codes, arrived, to_a, to_c, to_bt, rows,
):
    step = pl.program_id(0)
    bring(codes_from, codes, arrived, step)

    @pl.when(step == 0)
    def _():
        a_out[...] = dot(pick_main(), from_wide[...])
        c_out[...] = dot(pick_third(), from_wide[...])
        b_out[...] = dot(pick_main(), from_narrow[...]).astype(BF16)
        to_c[...] = jnp.zeros_like(to_c)
        to_bt[...] = jnp.zeros_like(to_bt)

    b_half = 0.5 * b_out[...]
    c = c_out[...]
    chunk_copy(codes_from, codes, arrived, step).wait()
    for part in range(STEP_I // WIDE_SUB):
        first_row = pl.multiple_of(step * STEP_I + part * WIDE_SUB, WIDE_SUB)
        a_part = a_out[pl.ds(first_row, WIDE_SUB), :]
        pairs = (a_part[:, None, :] * c[None]).astype(BF16).reshape(-1, RANK)
        half = jnp.tanh(dot(pairs, b_half, (1, 1)))
        code = codes[pl.ds(first_row, WIDE_SUB)].reshape(-1, BLOCK)
        twice = half + jnp.where(code == 2, -1.0, 1.0)
        twice = jnp.where(code > 0, twice, 0.0).astype(BF16)
        accumulate(twice, pairs, a_part, c, b_half, to_a, to_c, to_bt, first_row)

    @pl.when(step == STEPS - 1)
    def _():
        to_bt[...] = 0.5 * to_bt[...]
        fill_send(send, to_b, to_a, to_c, to_bt, jnp.zeros((ENTRY - 18, RANK), F32), rows)


def weight_kernel(codes_from, a, b, c, weight_to, codes, weight, arrived, left):
    step = pl.program_id(0)
    bring(codes_from, codes, arrived, step)
    b_half = 0.5 * b[...]
    chunk_copy(codes_from, codes, arrived, step).wait()
    for part in range(STEP_I // WIDE_SUB):
        first_row = pl.multiple_of(step * STEP_I + part * WIDE_SUB, WIDE_SUB)
        inside = pl.ds(first_row, WIDE_SUB)
        pairs = (a[inside, :][:, None, :] * c[...][None]).astype(BF16).reshape(-1, RANK)
        half = jnp.tanh(dot(pairs, b_half, (1, 1)))
        value = jnp.where(codes[inside].reshape(-1, BLOCK) > 0, 1.0 - half * half, 0.0)
        weight[inside] = value.astype(BF16).reshape(WIDE_SUB, DEPTH, BLOCK)
    chunk_copy(weight, weight_to, left, step).start()

    @pl.when(step == STEPS - 1)
    def _():
        for k in range(STEPS):
            chunk_copy(weight, weight_to, left, k).wait()


def moved_setup(from_wide, from_narrow, b, d_first, d_third, both):
    d_first[...] = dot(pick_main(), from_wide[...])
    d_third[...] = dot(pick_third(), from_wide[...])
    both[:, :RANK] = 0.25 * b[...]
    both[:, RANK:] = 0.25 * from_narrow[...]


def quarter_change(a_part, d_part, c, d_third, both):
    pairs = (a_part[:, None, :] * c[None]).astype(BF16).reshape(-1, RANK)
    mixed = d_part[:, None, :] * c[None] + a_part[:, None, :] * d_third[None]
    mixed = mixed.astype(BF16).reshape(-1, RANK)
    return pairs, dot(jnp.concatenate([mixed, pairs], axis=1), both, (1, 1))


def fold(x):
    return jnp.sum(x.reshape(-1, 8, BLOCK), axis=0)


def image_kernel(
    from_wide, from_narrow, weight_from, a, b, c, norm, send, to_b,
    weight, arrived, d_first, d_third, both, to_a, to_c, to_bt, rows, total,
):
    step = pl.program_id(0)
    bring(weight_from, weight, arrived, step)

    @pl.when(step == 0)
    def _():
        moved_setup(from_wide, from_narrow, b, d_first, d_third, both)
        to_c[...] = jnp.zeros_like(to_c)
        to_bt[...] = jnp.zeros_like(to_bt)
        total[...] = jnp.zeros_like(total)

    third = c[...]
    chunk_copy(weight_from, weight, arrived, step).wait()
    for part in range(STEP_I // SUB_I):
        first_row = pl.multiple_of(step * STEP_I + part * SUB_I, SUB_I)
        inside = pl.ds(first_row, SUB_I)
        a_part = a[pl.ds(first_row, SUB_I), :]
        d_part = d_first[pl.ds(first_row, SUB_I), :]
        pairs, change = quarter_change(a_part, d_part, third, d_third[...], both[...])
        scaled = weight[inside].reshape(-1, BLOCK).astype(F32) * change
        total[...] += fold(scaled * change)
        accumulate(scaled.astype(BF16), pairs, a_part, third, b[...], to_a, to_c, to_bt, first_row)

    @pl.when(step == STEPS - 1)
    def _():
        energy = 4.0 * jnp.sum(total[:, :RANK] + total[:, RANK:], axis=0, keepdims=True)
        spare = jnp.concatenate(parts_of(norm[0:1, :]) + parts_of(energy), axis=0)
        fill_send(send, to_b, to_a, to_c, to_bt, spare, rows)


def energy_kernel(
    from_wide, from_narrow, weight_from, a, b, c, sums, send,
    weight, arrived, d_first, d_third, both, total,
):
    step = pl.program_id(0)
    bring(weight_from, weight, arrived, step)

    @pl.when(step == 0)
    def _():
        moved_setup(from_wide, from_narrow, b, d_first, d_third, both)
        total[...] = jnp.zeros_like(total)

    third = c[...]
    chunk_copy(weight_from, weight, arrived, step).wait()
    for part in range(STEP_I // SUB_I):
        first_row = pl.multiple_of(step * STEP_I + part * SUB_I, SUB_I)
        inside = pl.ds(first_row, SUB_I)
        a_part = a[pl.ds(first_row, SUB_I), :]
        d_part = d_first[pl.ds(first_row, SUB_I), :]
        _, change = quarter_change(a_part, d_part, third, d_third[...], both[...])
        total[...] += fold(weight[inside].reshape(-1, BLOCK).astype(F32) * change * change)

    @pl.when(step == STEPS - 1)
    def _():
        energy = 4.0 * jnp.sum(total[...], keepdims=True)
        norm = jnp.sum(sums[0:1, :], axis=1, keepdims=True)
        cross = jnp.sum(sums[1:2, :], axis=1, keepdims=True)
        lane = lax.broadcasted_iota(I32, (1, RANK), 1)
        row = jnp.where(lane == 0, norm, jnp.where(lane == 1, cross, energy))
        send[...] = jnp.broadcast_to(row, send.shape)


def pick_half(core):
    q = lax.broadcasted_iota(I32, (SIDE, SIDE * ENTRY), 0)
    p = lax.broadcasted_iota(I32, (SIDE, SIDE * ENTRY), 1)
    return hot(p == q * ENTRY + 16 + core)


def pack_kernel(from_wide, to_b, send, rows):
    width = send.shape[0] // SIDE
    halves = [dot(pick_half(core), from_wide[...]) for core in range(2)]
    if width > 32:
        sums = spare_sums(from_wide[...], 18, ENTRY)
        spare = parts_of(sums[0:1]) + parts_of(sums[1:2]) + [jnp.zeros((2, RANK), F32)]
        halves = [jnp.concatenate([half] + spare, axis=0) for half in halves]
    for peer in range(SIDE):
        rows[peer * width : peer * width + 16, :] = to_b[peer * 16 : peer * 16 + 16, :]
        rows[peer * width + 16 : peer * width + width, :] = halves[peer % 2]
    send[...] = rows[...].astype(BF16)


def inner(x, y):
    return jnp.sum(x * y, axis=0, keepdims=True)


def rows_of(*values):
    row = lax.broadcasted_iota(I32, (8, RANK), 0)
    out = jnp.broadcast_to(values[-1], (8, RANK))
    for k in range(len(values) - 1):
        out = jnp.where(row == k, values[k], out)
    return out


def third_sum(from_narrow, from_pair, c_row, pair_row):
    mine = dot(row_hot(c_row[...], 512), from_narrow[...])
    return mine + dot(row_hot(pair_row[...], 512), from_pair[...])


def residual_narrow_kernel(from_narrow, b_row, ib, fb, r_b, send, norm):
    rest = -(dot(row_hot(b_row[...], 512), from_narrow[...]) + RIDGE * fb[...])
    r_b[...] = rest
    norm[...] = rows_of(inner(rest, rest))
    send[...] = gather(ib[...], rest)


def residual_wide_kernel(
    from_wide, from_narrow, from_pair, a_row, c_row, pair_row, ia, ic, count_third, fa, fc, part,
    r_a, r_c, send, norm,
):
    rest_a = -(dot(row_hot(a_row[...], 512), from_wide[...]) + RIDGE * fa[...])
    sum_c = third_sum(from_narrow, from_pair, c_row, pair_row)
    rest_c = -(sum_c + RIDGE * fc[...])
    r_a[...] = rest_a
    r_c[...] = rest_c
    send[...] = wide_rows(ia[...], ic[...], rest_a, rest_c).astype(BF16)
    third = inner(rest_c, rest_c) * count_third[0:1, :]
    norm[...] = rows_of(part[0:1, :] + inner(rest_a, rest_a) + third)


def update_narrow_kernel(from_narrow, b_row, ib, r_b, n_b, send, sums, scalars):
    spare = spare_sums(from_narrow[...], 32, from_narrow.shape[0] // SIDE)
    norm = jnp.sum(spare[0:1], axis=1, keepdims=True)
    curved = RIDGE * norm + jnp.sum(spare[1:2], axis=1, keepdims=True)
    alpha = norm / curved
    image = dot(row_hot(b_row[...], 512), from_narrow[...]) + RIDGE * r_b[...]
    rest = r_b[...] - alpha * image
    n_b[...] = rest
    send[...] = gather(ib[...], rest)
    sums[...] = rows_of(inner(rest, rest), inner(rest, image))
    scalars[...] = rows_of(norm, curved, alpha)


def update_wide_kernel(
    from_wide, from_narrow, from_pair, a_row, c_row, pair_row, ia, ic, count_third, r_a, r_c, part,
    scalars, n_a, n_c, send, sums,
):
    alpha = scalars[2:3, 0:1]
    image_a = dot(row_hot(a_row[...], 512), from_wide[...]) + RIDGE * r_a[...]
    image_c = third_sum(from_narrow, from_pair, c_row, pair_row) + RIDGE * r_c[...]
    rest_a = r_a[...] - alpha * image_a
    rest_c = r_c[...] - alpha * image_c
    n_a[...] = rest_a
    n_c[...] = rest_c
    send[...] = wide_rows(ia[...], ic[...], rest_a, rest_c).astype(BF16)
    count = count_third[0:1, :]
    sums[...] = rows_of(
        part[0:1, :] + inner(rest_a, rest_a) + count * inner(rest_c, rest_c),
        part[1:2, :] + inner(rest_a, image_a) + count * inner(rest_c, image_c),
    )


def step_kernel(received, scalars, r_a, r_b, r_c, n_a, n_b, n_c, s_a, s_b, s_c):
    total = jnp.sum(received[...], axis=0, keepdims=True)
    new, cross, energy = total[:, 0:1], total[:, 1:2], total[:, 2:3]
    norm, curved, alpha = scalars[0:1, 0:1], scalars[1:2, 0:1], scalars[2:3, 0:1]
    beta = new / norm
    second = new / (RIDGE * new + energy + 2.0 * beta * cross + beta * beta * curved)
    for old, rest, out in ((r_a, n_a, s_a), (r_b, n_b, s_b), (r_c, n_c, s_c)):
        out[...] = alpha * old[...] + second * (rest[...] + beta * old[...])


def call(kernel, outs, *operands, name, limit=24, scratch=()):
    return pl.pallas_call(
        kernel,
        out_shape=outs,
        scratch_shapes=scratch,
        name=name,
        cost_estimate=pl.CostEstimate(flops=10**8, bytes_accessed=3 << 20, transcendentals=0),
        compiler_params=pltpu.CompilerParams(vmem_limit_bytes=limit << 20),
    )(*operands)


def block_call(kernel, outs, out_specs, in_specs, scratch, *operands, name, cost=5 * 10**9):
    return pl.pallas_call(
        kernel,
        grid=(STEPS,),
        in_specs=in_specs,
        out_specs=out_specs,
        out_shape=outs,
        scratch_shapes=scratch,
        name=name,
        cost_estimate=pl.CostEstimate(flops=cost, bytes_accessed=12 << 20, transcendentals=0),
        compiler_params=pltpu.CompilerParams(
            vmem_limit_bytes=50 << 20, dimension_semantics=("arbitrary",)
        ),
    )(*operands)


def exchange(x, axis):
    return lax.all_to_all(x, axis, split_axis=0, concat_axis=0, tiled=True)


def after(x, earlier):
    return lax.optimization_barrier((x, earlier))[0]


def local(entries, factor_a, factor_b, factor_c, index_a, index_b, index_c):
    rows = SIDE * ENTRY
    ia, ib, ic = index_a.reshape(1, BLOCK), index_b.reshape(1, BLOCK), index_c.reshape(1, DEPTH)
    rows_bf16, block_bf16 = struct((rows, RANK), BF16), struct((BLOCK, RANK), BF16)
    block_f32 = struct((BLOCK, RANK), F32)
    small = struct((8, RANK), F32)
    table = struct((512, RANK), F32)

    send_narrow = call(
        first_narrow_kernel, rows_bf16, ib, ic, factor_b, name="first_narrow", limit=60
    )
    from_narrow = exchange(send_narrow, "narrow")
    send_wide = call(
        first_wide_kernel, rows_bf16, ia, ic, factor_a, factor_c, name="first_wide", limit=60
    )
    from_wide = exchange(after(send_wide, from_narrow), "wide")
    group_index = from_narrow.reshape(SIDE, ENTRY, RANK)[:, 16:18, :DEPTH].astype(F32)
    group_index = (group_index[:, 0] * 16.0 + group_index[:, 1]).astype(I32)

    def none(width):
        return jnp.full((SIDE, width), -1, I32)

    def place(*parts):
        return jnp.concatenate(parts, axis=1).reshape(1, -1)

    a_row = place(index_a.reshape(SIDE, 16), none(ENTRY - 16))

    core = lax.axis_index("narrow") % 2
    by_core = group_index.reshape(SIDE, SIDE, 2)
    own_half = jnp.where(core == 0, by_core[:, :, 0], by_core[:, :, 1])
    pair_half = jnp.where(core == 0, by_core[:, :, 1], by_core[:, :, 0])

    def narrow_places(spare):
        return (
            place(index_b.reshape(SIDE, 16), none(16 + spare)),
            place(none(16), own_half, none(spare)),
            place(none(16), pair_half, none(spare)),
        )

    count_third = jnp.broadcast_to((lax.axis_index("narrow") == 0).astype(F32), (8, RANK))

    def give_back(send, to_b, spare):
        from_wide = exchange(send, "wide")
        shape = (SIDE * (32 + spare), RANK)
        send = call(
            pack_kernel, struct(shape, BF16), from_wide, to_b,
            name="pack", scratch=[pltpu.VMEM(shape, F32)],
        )
        return from_wide, send, exchange(send, "narrow")

    def from_other_core(x):
        return lax.ppermute(x, "narrow", [(n, n ^ 1) for n in range(SIDE)])

    slab = pl.BlockSpec(memory_space=pl.ANY)
    cube = (BLOCK, DEPTH, BLOCK)
    arrivals = pltpu.SemaphoreType.DMA((STEPS,))
    both_scratch = [
        pltpu.VMEM(cube, BF16), arrivals,
        pltpu.VMEM((BLOCK, RANK), F32), pltpu.VMEM((DEPTH, RANK), F32),
        pltpu.VMEM((BLOCK, 2 * RANK), BF16),
    ]
    sum_scratch = [
        pltpu.VMEM((BLOCK, RANK), F32), pltpu.VMEM((DEPTH, RANK), F32),
        pltpu.VMEM((RANK, BLOCK), F32), pltpu.VMEM((rows, RANK), F32),
    ]
    total_scratch = [pltpu.VMEM((8, BLOCK), F32)]

    send, to_b, a, b, c = block_call(
        gradient_kernel,
        (rows_bf16, block_f32, block_f32, block_bf16, struct((DEPTH, RANK), F32)),
        (
            full((rows, RANK)), full((BLOCK, RANK)), full((BLOCK, RANK)), full((BLOCK, RANK)),
            full((DEPTH, RANK)),
        ),
        [full((rows, RANK)), full((rows, RANK)), slab],
        [pltpu.VMEM(cube, I32), arrivals] + sum_scratch,
        from_wide, from_narrow, entries,
        name="gradient",
    )
    places_first, places_second = narrow_places(0), narrow_places(8)
    to_b = after(to_b, (places_first, places_second, a_row))
    back_wide, packed, back_narrow = give_back(send, to_b, 0)
    weight = block_call(
        weight_kernel,
        pltpu.HBM(cube, BF16),
        slab,
        [slab, full((BLOCK, RANK)), full((BLOCK, RANK)), full((DEPTH, RANK))],
        [pltpu.VMEM(cube, I32), pltpu.VMEM(cube, BF16), arrivals, arrivals],
        entries, after(a, packed), b, c,
        name="weight", cost=6 * 10**9,
    )
    back_narrow, weight = lax.optimization_barrier((back_narrow, weight))
    back_pair = from_other_core(back_narrow)
    b_row, c_row, pair_row = places_first
    r_b, send_narrow, part = call(
        residual_narrow_kernel,
        (table, block_bf16, small),
        back_narrow, b_row, ib, factor_b,
        name="residual_narrow",
    )
    from_narrow = exchange(send_narrow, "narrow")
    r_a, r_c, send_wide, norm = call(
        residual_wide_kernel,
        (table, table, rows_bf16, small),
        back_wide, back_narrow, back_pair, a_row, c_row, pair_row, ia, ic, count_third, factor_a,
        factor_c, part,
        name="residual_wide",
    )
    from_wide = exchange(after(send_wide, from_narrow), "wide")
    fixed_specs = [
        full((rows, RANK)), full((BLOCK, RANK)), slab,
        full((BLOCK, RANK)), full((BLOCK, RANK)), full((DEPTH, RANK)), full((8, RANK)),
    ]
    send, to_b = block_call(
        image_kernel,
        (rows_bf16, block_f32),
        (full((rows, RANK)), full((BLOCK, RANK))),
        fixed_specs,
        both_scratch + sum_scratch + total_scratch,
        from_wide, from_narrow, weight, a, b, c, norm,
        name="image",
    )
    back_wide, packed, back_narrow = give_back(send, to_b, 8)
    back_pair = from_other_core(back_narrow)
    b_row, c_row, pair_row = places_second
    n_b, send_narrow, part, scalars = call(
        update_narrow_kernel,
        (table, block_bf16, small, small),
        back_narrow, b_row, ib, r_b,
        name="update_narrow",
    )
    from_narrow = exchange(send_narrow, "narrow")
    n_a, n_c, send_wide, sums = call(
        update_wide_kernel,
        (table, table, rows_bf16, small),
        back_wide, back_narrow, back_pair, a_row, c_row, pair_row, ia, ic, count_third, r_a,
        r_c, part, scalars,
        name="update_wide",
    )
    from_wide = exchange(after(send_wide, from_narrow), "wide")
    partial = block_call(
        energy_kernel,
        block_f32,
        full((BLOCK, RANK)),
        fixed_specs,
        both_scratch + total_scratch,
        from_wide, from_narrow, weight, a, b, c, sums,
        name="energy",
    )
    received = exchange(partial, ("wide", "narrow"))
    return call(
        step_kernel,
        (table, table, table),
        received, scalars, r_a, r_b, r_c, n_a, n_b, n_c,
        name="step",
    )


def solution(mesh):
    placed = (
        P(("wide", "narrow"), None, None),
        P(("wide", "narrow"), None),
        P(("wide", "narrow"), None),
        P("wide", None),
        P(("wide", "narrow")),
        P(("wide", "narrow")),
        P(("wide", "narrow")),
    )
    return jax.shard_map(
        local,
        mesh=mesh,
        in_specs=placed,
        out_specs=(P(("wide", "narrow"), None), P(("wide", "narrow"), None), P("wide", None)),
        check_vma=False,
    )
```

```python
import jax
import jax.numpy as jnp
from jax import lax
from jax.experimental import pallas as pl
from jax.experimental.pallas import tpu as pltpu
from jax.sharding import PartitionSpec as P

RIDGE = 25.0
F32, BF16, I32 = jnp.float32, jnp.bfloat16, jnp.int32

RANK = 128
SIDE = 16
BLOCK = 256
DEPTH = 32
ENTRY = 24
STEP_I = 64
STEPS = BLOCK // STEP_I
AHEAD = 4
SUB_I = 8
WIDE_SUB = 16


def full(shape):
    return pl.BlockSpec(shape, lambda *_: (0,) * len(shape))


def struct(shape, dtype):
    return jax.ShapeDtypeStruct(shape, dtype)


def dot(x, y, dims=(1, 0)):
    return lax.dot_general(
        x, y, (((dims[0],), (dims[1],)), ((), ())), preferred_element_type=F32
    )


def hot(x):
    return jnp.where(x, 1.0, 0.0).astype(BF16)


def row_hot(index_row, height):
    columns = index_row.shape[1]
    return hot(lax.broadcasted_iota(I32, (height, columns), 0) == index_row)


def parts_of(x):
    high = x.astype(BF16).astype(F32)
    middle = (x - high).astype(BF16).astype(F32)
    return [high, middle, x - high - middle]


def spare_sums(x, first, width):
    k = lax.broadcasted_iota(I32, (8, x.shape[0]), 0)
    p = lax.broadcasted_iota(I32, (8, x.shape[0]), 1) % width - first
    return dot(hot((p >= 3 * k) & (p < 3 * k + 3) & (k < 2)), x)


def pick_main():
    q = lax.broadcasted_iota(I32, (BLOCK, SIDE * ENTRY), 0)
    p = lax.broadcasted_iota(I32, (BLOCK, SIDE * ENTRY), 1)
    return hot(p == (q >> 4) * ENTRY + (q & 15))


def pick_third():
    q = lax.broadcasted_iota(I32, (DEPTH, SIDE * ENTRY), 0)
    p = lax.broadcasted_iota(I32, (DEPTH, SIDE * ENTRY), 1)
    return hot(p == (q >> 1) * ENTRY + 16 + (q & 1))


def spread(width, per_peer, offset):
    shift = per_peer.bit_length() - 1
    p = lax.broadcasted_iota(I32, (SIDE * ENTRY, width), 0)
    q = lax.broadcasted_iota(I32, (SIDE * ENTRY, width), 1)
    return hot(p == (q >> shift) * ENTRY + offset + (q & (per_peer - 1)))


def gather(index_row, table):
    return dot(row_hot(index_row, 512), table.astype(BF16), (0, 0)).astype(BF16)


def wide_rows(ia, ic, table_a, table_c):
    return dot(spread(BLOCK, 16, 0), gather(ia, table_a)) + dot(
        spread(DEPTH, 2, 16), gather(ic, table_c)
    )


def first_narrow_kernel(ib, ic, fb, send):
    rows = dot(row_hot(ib[...], 512), fb[...].astype(BF16), (0, 0)).reshape(SIDE, 16, RANK)
    lane = lax.broadcasted_iota(I32, (DEPTH, RANK), 1)
    to_lanes = hot(lane == lax.broadcasted_iota(I32, (DEPTH, RANK), 0))
    high, low = (ic[...] >> 4).astype(BF16), (ic[...] & 15).astype(BF16)
    spare = jnp.zeros((ENTRY - 18, RANK), F32)
    tail = jnp.concatenate([dot(high, to_lanes), dot(low, to_lanes), spare], axis=0)
    tail = jnp.broadcast_to(tail[None], (SIDE, ENTRY - 16, RANK))
    send[...] = jnp.concatenate([rows, tail], axis=1).reshape(SIDE * ENTRY, RANK).astype(BF16)


def first_wide_kernel(ia, ic, fa, fc, send):
    send[...] = wide_rows(ia[...], ic[...], fa[...], fc[...]).astype(BF16)


def chunk_copy(source, held, arrived, k):
    here = pl.ds(k * STEP_I, STEP_I)
    return pltpu.make_async_copy(source.at[here], held.at[here], arrived.at[k])


def bring(source, held, arrived, step):
    @pl.when(step == 0)
    def _():
        for k in range(AHEAD):
            chunk_copy(source, held, arrived, k).start()

    @pl.when(step + AHEAD < STEPS)
    def _():
        chunk_copy(source, held, arrived, step + AHEAD).start()


def accumulate(upstream, pairs, a_part, c, b, to_a, to_c, to_bt, first_row):
    over = dot(upstream, b).reshape(-1, DEPTH, RANK)
    to_a[pl.ds(first_row, a_part.shape[0]), :] = jnp.sum(over * c[None], axis=1)
    to_c[...] += jnp.sum(over * a_part[:, None, :], axis=0)
    to_bt[...] += dot(pairs, upstream, (0, 0))


def fill_send(send, to_b, acc_a, acc_c, acc_bt, spare, rows):
    to_b[...] = acc_bt[...].T
    for peer in range(SIDE):
        base = peer * ENTRY
        rows[base : base + 16, :] = acc_a[peer * 16 : peer * 16 + 16, :]
        tail = jnp.concatenate([acc_c[2 * peer : 2 * peer + 2, :], spare], axis=0)
        rows[base + 16 : base + ENTRY, :] = tail
    send[...] = rows[...].astype(BF16)


def gradient_kernel(
    from_wide, from_narrow, codes_from, send, to_b, a_out, b_out, c_out,
    codes, arrived, to_a, to_c, to_bt, rows,
):
    step = pl.program_id(0)
    bring(codes_from, codes, arrived, step)

    @pl.when(step == 0)
    def _():
        a_out[...] = dot(pick_main(), from_wide[...])
        c_out[...] = dot(pick_third(), from_wide[...])
        b_out[...] = dot(pick_main(), from_narrow[...]).astype(BF16)
        to_c[...] = jnp.zeros_like(to_c)
        to_bt[...] = jnp.zeros_like(to_bt)

    b_half = 0.5 * b_out[...]
    c = c_out[...]
    chunk_copy(codes_from, codes, arrived, step).wait()
    for part in range(STEP_I // WIDE_SUB):
        first_row = pl.multiple_of(step * STEP_I + part * WIDE_SUB, WIDE_SUB)
        a_part = a_out[pl.ds(first_row, WIDE_SUB), :]
        pairs = (a_part[:, None, :] * c[None]).astype(BF16).reshape(-1, RANK)
        half = jnp.tanh(dot(pairs, b_half, (1, 1)))
        code = codes[pl.ds(first_row, WIDE_SUB)].reshape(-1, BLOCK)
        twice = half + jnp.where(code == 2, -1.0, 1.0)
        twice = jnp.where(code > 0, twice, 0.0).astype(BF16)
        accumulate(twice, pairs, a_part, c, b_half, to_a, to_c, to_bt, first_row)

    @pl.when(step == STEPS - 1)
    def _():
        to_bt[...] = 0.5 * to_bt[...]
        fill_send(send, to_b, to_a, to_c, to_bt, jnp.zeros((ENTRY - 18, RANK), F32), rows)


def weight_kernel(codes_from, a, b, c, weight_to, codes, weight, arrived, left):
    step = pl.program_id(0)
    bring(codes_from, codes, arrived, step)
    b_half = 0.5 * b[...]
    chunk_copy(codes_from, codes, arrived, step).wait()
    for part in range(STEP_I // WIDE_SUB):
        first_row = pl.multiple_of(step * STEP_I + part * WIDE_SUB, WIDE_SUB)
        inside = pl.ds(first_row, WIDE_SUB)
        pairs = (a[inside, :][:, None, :] * c[...][None]).astype(BF16).reshape(-1, RANK)
        half = jnp.tanh(dot(pairs, b_half, (1, 1)))
        value = jnp.where(codes[inside].reshape(-1, BLOCK) > 0, 1.0 - half * half, 0.0)
        weight[inside] = value.astype(BF16).reshape(WIDE_SUB, DEPTH, BLOCK)
    chunk_copy(weight, weight_to, left, step).start()

    @pl.when(step == STEPS - 1)
    def _():
        for k in range(STEPS):
            chunk_copy(weight, weight_to, left, k).wait()


def moved_setup(from_wide, from_narrow, b, d_first, d_third, both):
    d_first[...] = dot(pick_main(), from_wide[...])
    d_third[...] = dot(pick_third(), from_wide[...])
    both[:, :RANK] = 0.25 * b[...]
    both[:, RANK:] = 0.25 * from_narrow[...]


def quarter_change(a_part, d_part, c, d_third, both):
    pairs = (a_part[:, None, :] * c[None]).astype(BF16).reshape(-1, RANK)
    mixed = d_part[:, None, :] * c[None] + a_part[:, None, :] * d_third[None]
    mixed = mixed.astype(BF16).reshape(-1, RANK)
    return pairs, dot(jnp.concatenate([mixed, pairs], axis=1), both, (1, 1))


def fold(x):
    return jnp.sum(x.reshape(-1, 8, BLOCK), axis=0)


def image_kernel(
    from_wide, from_narrow, weight_from, a, b, c, norm, send, to_b,
    weight, arrived, d_first, d_third, both, to_a, to_c, to_bt, rows, total,
):
    step = pl.program_id(0)
    bring(weight_from, weight, arrived, step)

    @pl.when(step == 0)
    def _():
        moved_setup(from_wide, from_narrow, b, d_first, d_third, both)
        to_c[...] = jnp.zeros_like(to_c)
        to_bt[...] = jnp.zeros_like(to_bt)
        total[...] = jnp.zeros_like(total)

    third = c[...]
    chunk_copy(weight_from, weight, arrived, step).wait()
    for part in range(STEP_I // SUB_I):
        first_row = pl.multiple_of(step * STEP_I + part * SUB_I, SUB_I)
        inside = pl.ds(first_row, SUB_I)
        a_part = a[pl.ds(first_row, SUB_I), :]
        d_part = d_first[pl.ds(first_row, SUB_I), :]
        pairs, change = quarter_change(a_part, d_part, third, d_third[...], both[...])
        scaled = weight[inside].reshape(-1, BLOCK).astype(F32) * change
        total[...] += fold(scaled * change)
        accumulate(scaled.astype(BF16), pairs, a_part, third, b[...], to_a, to_c, to_bt, first_row)

    @pl.when(step == STEPS - 1)
    def _():
        energy = 4.0 * jnp.sum(total[:, :RANK] + total[:, RANK:], axis=0, keepdims=True)
        spare = jnp.concatenate(parts_of(norm[0:1, :]) + parts_of(energy), axis=0)
        fill_send(send, to_b, to_a, to_c, to_bt, spare, rows)


def energy_kernel(
    from_wide, from_narrow, weight_from, a, b, c, sums, send,
    weight, arrived, d_first, d_third, both, total,
):
    step = pl.program_id(0)
    bring(weight_from, weight, arrived, step)

    @pl.when(step == 0)
    def _():
        moved_setup(from_wide, from_narrow, b, d_first, d_third, both)
        total[...] = jnp.zeros_like(total)

    third = c[...]
    chunk_copy(weight_from, weight, arrived, step).wait()
    for part in range(STEP_I // SUB_I):
        first_row = pl.multiple_of(step * STEP_I + part * SUB_I, SUB_I)
        inside = pl.ds(first_row, SUB_I)
        a_part = a[pl.ds(first_row, SUB_I), :]
        d_part = d_first[pl.ds(first_row, SUB_I), :]
        _, change = quarter_change(a_part, d_part, third, d_third[...], both[...])
        total[...] += fold(weight[inside].reshape(-1, BLOCK).astype(F32) * change * change)

    @pl.when(step == STEPS - 1)
    def _():
        energy = 4.0 * jnp.sum(total[...], keepdims=True)
        norm = jnp.sum(sums[0:1, :], axis=1, keepdims=True)
        cross = jnp.sum(sums[1:2, :], axis=1, keepdims=True)
        lane = lax.broadcasted_iota(I32, (1, RANK), 1)
        row = jnp.where(lane == 0, norm, jnp.where(lane == 1, cross, energy))
        send[...] = jnp.broadcast_to(row, send.shape)


def pick_half(core):
    q = lax.broadcasted_iota(I32, (SIDE, SIDE * ENTRY), 0)
    p = lax.broadcasted_iota(I32, (SIDE, SIDE * ENTRY), 1)
    return hot(p == q * ENTRY + 16 + core)


def pack_kernel(from_wide, to_b, send, rows):
    width = send.shape[0] // SIDE
    halves = [dot(pick_half(core), from_wide[...]) for core in range(2)]
    if width > 32:
        sums = spare_sums(from_wide[...], 18, ENTRY)
        spare = parts_of(sums[0:1]) + parts_of(sums[1:2]) + [jnp.zeros((2, RANK), F32)]
        halves = [jnp.concatenate([half] + spare, axis=0) for half in halves]
    for peer in range(SIDE):
        rows[peer * width : peer * width + 16, :] = to_b[peer * 16 : peer * 16 + 16, :]
        rows[peer * width + 16 : peer * width + width, :] = halves[peer % 2]
    send[...] = rows[...].astype(BF16)


def inner(x, y):
    return jnp.sum(x * y, axis=0, keepdims=True)


def rows_of(*values):
    row = lax.broadcasted_iota(I32, (8, RANK), 0)
    out = jnp.broadcast_to(values[-1], (8, RANK))
    for k in range(len(values) - 1):
        out = jnp.where(row == k, values[k], out)
    return out


def third_sum(from_narrow, from_pair, c_row, pair_row):
    mine = dot(row_hot(c_row[...], 512), from_narrow[...])
    return mine + dot(row_hot(pair_row[...], 512), from_pair[...])


def residual_narrow_kernel(from_narrow, b_row, ib, fb, r_b, send, norm):
    rest = -(dot(row_hot(b_row[...], 512), from_narrow[...]) + RIDGE * fb[...])
    r_b[...] = rest
    norm[...] = rows_of(inner(rest, rest))
    send[...] = gather(ib[...], rest)


def residual_wide_kernel(
    from_wide, from_narrow, from_pair, a_row, c_row, pair_row, ia, ic, count_third, fa, fc, part,
    r_a, r_c, send, norm,
):
    rest_a = -(dot(row_hot(a_row[...], 512), from_wide[...]) + RIDGE * fa[...])
    sum_c = third_sum(from_narrow, from_pair, c_row, pair_row)
    rest_c = -(sum_c + RIDGE * fc[...])
    r_a[...] = rest_a
    r_c[...] = rest_c
    send[...] = wide_rows(ia[...], ic[...], rest_a, rest_c).astype(BF16)
    third = inner(rest_c, rest_c) * count_third[0:1, :]
    norm[...] = rows_of(part[0:1, :] + inner(rest_a, rest_a) + third)


def update_narrow_kernel(from_narrow, b_row, ib, r_b, n_b, send, sums, scalars):
    spare = spare_sums(from_narrow[...], 32, from_narrow.shape[0] // SIDE)
    norm = jnp.sum(spare[0:1], axis=1, keepdims=True)
    curved = RIDGE * norm + jnp.sum(spare[1:2], axis=1, keepdims=True)
    alpha = norm / curved
    image = dot(row_hot(b_row[...], 512), from_narrow[...]) + RIDGE * r_b[...]
    rest = r_b[...] - alpha * image
    n_b[...] = rest
    send[...] = gather(ib[...], rest)
    sums[...] = rows_of(inner(rest, rest), inner(rest, image))
    scalars[...] = rows_of(norm, curved, alpha)


def update_wide_kernel(
    from_wide, from_narrow, from_pair, a_row, c_row, pair_row, ia, ic, count_third, r_a, r_c, part,
    scalars, n_a, n_c, send, sums,
):
    alpha = scalars[2:3, 0:1]
    image_a = dot(row_hot(a_row[...], 512), from_wide[...]) + RIDGE * r_a[...]
    image_c = third_sum(from_narrow, from_pair, c_row, pair_row) + RIDGE * r_c[...]
    rest_a = r_a[...] - alpha * image_a
    rest_c = r_c[...] - alpha * image_c
    n_a[...] = rest_a
    n_c[...] = rest_c
    send[...] = wide_rows(ia[...], ic[...], rest_a, rest_c).astype(BF16)
    count = count_third[0:1, :]
    sums[...] = rows_of(
        part[0:1, :] + inner(rest_a, rest_a) + count * inner(rest_c, rest_c),
        part[1:2, :] + inner(rest_a, image_a) + count * inner(rest_c, image_c),
    )


def step_kernel(received, scalars, r_a, r_b, r_c, n_a, n_b, n_c, s_a, s_b, s_c):
    total = jnp.sum(received[...], axis=0, keepdims=True)
    new, cross, energy = total[:, 0:1], total[:, 1:2], total[:, 2:3]
    norm, curved, alpha = scalars[0:1, 0:1], scalars[1:2, 0:1], scalars[2:3, 0:1]
    beta = new / norm
    second = new / (RIDGE * new + energy + 2.0 * beta * cross + beta * beta * curved)
    for old, rest, out in ((r_a, n_a, s_a), (r_b, n_b, s_b), (r_c, n_c, s_c)):
        out[...] = alpha * old[...] + second * (rest[...] + beta * old[...])


def call(kernel, outs, *operands, name, limit=24, scratch=()):
    return pl.pallas_call(
        kernel,
        out_shape=outs,
        scratch_shapes=scratch,
        name=name,
        cost_estimate=pl.CostEstimate(flops=10**8, bytes_accessed=3 << 20, transcendentals=0),
        compiler_params=pltpu.CompilerParams(vmem_limit_bytes=limit << 20),
    )(*operands)


def block_call(kernel, outs, out_specs, in_specs, scratch, *operands, name, cost=5 * 10**9):
    return pl.pallas_call(
        kernel,
        grid=(STEPS,),
        in_specs=in_specs,
        out_specs=out_specs,
        out_shape=outs,
        scratch_shapes=scratch,
        name=name,
        cost_estimate=pl.CostEstimate(flops=cost, bytes_accessed=12 << 20, transcendentals=0),
        compiler_params=pltpu.CompilerParams(
            vmem_limit_bytes=50 << 20, dimension_semantics=("arbitrary",)
        ),
    )(*operands)


def exchange(x, axis):
    return lax.all_to_all(x, axis, split_axis=0, concat_axis=0, tiled=True)


def after(x, earlier):
    return lax.optimization_barrier((x, earlier))[0]


def local(entries, factor_a, factor_b, factor_c, index_a, index_b, index_c):
    rows = SIDE * ENTRY
    ia, ib, ic = index_a.reshape(1, BLOCK), index_b.reshape(1, BLOCK), index_c.reshape(1, DEPTH)
    rows_bf16, block_bf16 = struct((rows, RANK), BF16), struct((BLOCK, RANK), BF16)
    block_f32 = struct((BLOCK, RANK), F32)
    small = struct((8, RANK), F32)
    table = struct((512, RANK), F32)

    send_narrow = call(
        first_narrow_kernel, rows_bf16, ib, ic, factor_b, name="first_narrow", limit=60
    )
    from_narrow = exchange(send_narrow, "narrow")
    send_wide = call(
        first_wide_kernel, rows_bf16, ia, ic, factor_a, factor_c, name="first_wide", limit=60
    )
    from_wide = exchange(after(send_wide, from_narrow), "wide")
    group_index = from_narrow.reshape(SIDE, ENTRY, RANK)[:, 16:18, :DEPTH].astype(F32)
    group_index = (group_index[:, 0] * 16.0 + group_index[:, 1]).astype(I32)

    def none(width):
        return jnp.full((SIDE, width), -1, I32)

    def place(*parts):
        return jnp.concatenate(parts, axis=1).reshape(1, -1)

    a_row = place(index_a.reshape(SIDE, 16), none(ENTRY - 16))

    core = lax.axis_index("narrow") % 2
    by_core = group_index.reshape(SIDE, SIDE, 2)
    own_half = jnp.where(core == 0, by_core[:, :, 0], by_core[:, :, 1])
    pair_half = jnp.where(core == 0, by_core[:, :, 1], by_core[:, :, 0])

    def narrow_places(spare):
        return (
            place(index_b.reshape(SIDE, 16), none(16 + spare)),
            place(none(16), own_half, none(spare)),
            place(none(16), pair_half, none(spare)),
        )

    count_third = jnp.broadcast_to((lax.axis_index("narrow") == 0).astype(F32), (8, RANK))

    def give_back(send, to_b, spare):
        from_wide = exchange(send, "wide")
        shape = (SIDE * (32 + spare), RANK)
        send = call(
            pack_kernel, struct(shape, BF16), from_wide, to_b,
            name="pack", scratch=[pltpu.VMEM(shape, F32)],
        )
        return from_wide, send, exchange(send, "narrow")

    def from_other_core(x):
        return lax.ppermute(x, "narrow", [(n, n ^ 1) for n in range(SIDE)])

    slab = pl.BlockSpec(memory_space=pl.ANY)
    cube = (BLOCK, DEPTH, BLOCK)
    arrivals = pltpu.SemaphoreType.DMA((STEPS,))
    both_scratch = [
        pltpu.VMEM(cube, BF16), arrivals,
        pltpu.VMEM((BLOCK, RANK), F32), pltpu.VMEM((DEPTH, RANK), F32),
        pltpu.VMEM((BLOCK, 2 * RANK), BF16),
    ]
    sum_scratch = [
        pltpu.VMEM((BLOCK, RANK), F32), pltpu.VMEM((DEPTH, RANK), F32),
        pltpu.VMEM((RANK, BLOCK), F32), pltpu.VMEM((rows, RANK), F32),
    ]
    total_scratch = [pltpu.VMEM((8, BLOCK), F32)]

    places_first, places_second = narrow_places(0), narrow_places(8)
    from_wide = after(from_wide, (places_first, places_second, a_row))
    send, to_b, a, b, c = block_call(
        gradient_kernel,
        (rows_bf16, block_f32, block_f32, block_bf16, struct((DEPTH, RANK), F32)),
        (
            full((rows, RANK)), full((BLOCK, RANK)), full((BLOCK, RANK)), full((BLOCK, RANK)),
            full((DEPTH, RANK)),
        ),
        [full((rows, RANK)), full((rows, RANK)), slab],
        [pltpu.VMEM(cube, I32), arrivals] + sum_scratch,
        from_wide, from_narrow, entries,
        name="gradient",
    )
    back_wide, packed, back_narrow = give_back(send, to_b, 0)
    weight = block_call(
        weight_kernel,
        pltpu.HBM(cube, BF16),
        slab,
        [slab, full((BLOCK, RANK)), full((BLOCK, RANK)), full((DEPTH, RANK))],
        [pltpu.VMEM(cube, I32), pltpu.VMEM(cube, BF16), arrivals, arrivals],
        entries, after(a, packed), b, c,
        name="weight", cost=6 * 10**9,
    )
    back_narrow, weight = lax.optimization_barrier((back_narrow, weight))
    b_row, c_row, pair_row = places_first
    r_b, send_narrow, part = call(
        residual_narrow_kernel,
        (table, block_bf16, small),
        back_narrow, b_row, ib, factor_b,
        name="residual_narrow",
    )
    from_narrow = exchange(send_narrow, "narrow")
    back_pair = from_other_core(after(back_narrow, send_narrow))
    r_a, r_c, send_wide, norm = call(
        residual_wide_kernel,
        (table, table, rows_bf16, small),
        back_wide, back_narrow, back_pair, a_row, c_row, pair_row, ia, ic, count_third, factor_a,
        factor_c, part,
        name="residual_wide",
    )
    from_wide = exchange(after(send_wide, from_narrow), "wide")
    fixed_specs = [
        full((rows, RANK)), full((BLOCK, RANK)), slab,
        full((BLOCK, RANK)), full((BLOCK, RANK)), full((DEPTH, RANK)), full((8, RANK)),
    ]
    send, to_b = block_call(
        image_kernel,
        (rows_bf16, block_f32),
        (full((rows, RANK)), full((BLOCK, RANK))),
        fixed_specs,
        both_scratch + sum_scratch + total_scratch,
        from_wide, from_narrow, weight, a, b, c, norm,
        name="image",
    )
    back_wide, packed, back_narrow = give_back(send, to_b, 8)
    b_row, c_row, pair_row = places_second
    n_b, send_narrow, part, scalars = call(
        update_narrow_kernel,
        (table, block_bf16, small, small),
        back_narrow, b_row, ib, r_b,
        name="update_narrow",
    )
    from_narrow = exchange(send_narrow, "narrow")
    back_pair = from_other_core(after(back_narrow, send_narrow))
    n_a, n_c, send_wide, sums = call(
        update_wide_kernel,
        (table, table, rows_bf16, small),
        back_wide, back_narrow, back_pair, a_row, c_row, pair_row, ia, ic, count_third, r_a,
        r_c, part, scalars,
        name="update_wide",
    )
    from_wide = exchange(after(send_wide, from_narrow), "wide")
    partial = block_call(
        energy_kernel,
        block_f32,
        full((BLOCK, RANK)),
        fixed_specs,
        both_scratch + total_scratch,
        from_wide, from_narrow, weight, a, b, c, sums,
        name="energy",
    )
    received = exchange(partial, ("wide", "narrow"))
    return call(
        step_kernel,
        (table, table, table),
        received, scalars, r_a, r_b, r_c, n_a, n_b, n_c,
        name="step",
    )


def solution(mesh):
    placed = (
        P(("wide", "narrow"), None, None),
        P(("wide", "narrow"), None),
        P(("wide", "narrow"), None),
        P("wide", None),
        P(("wide", "narrow")),
        P(("wide", "narrow")),
        P(("wide", "narrow")),
    )
    return jax.shard_map(
        local,
        mesh=mesh,
        in_specs=placed,
        out_specs=(P(("wide", "narrow"), None), P(("wide", "narrow"), None), P("wide", None)),
        check_vma=False,
    )
```

```python
import jax
import jax.numpy as jnp
from jax import lax
from jax.experimental import pallas as pl
from jax.experimental.pallas import tpu as pltpu
from jax.sharding import PartitionSpec as P

RIDGE = 25.0
F32, BF16, I32 = jnp.float32, jnp.bfloat16, jnp.int32

RANK = 128
SIDE = 16
BLOCK = 256
DEPTH = 32
ENTRY = 24
SLABS = ((0, 32), (32, 96), (128, 128))
EVEN_SLABS = ((0, 64), (64, 64), (128, 64), (192, 64))
SUB_I = 8
WIDE_SUB = 16


def full(shape):
    return pl.BlockSpec(memory_space=pltpu.VMEM)


def struct(shape, dtype):
    return jax.ShapeDtypeStruct(shape, dtype)


def dot(x, y, dims=(1, 0)):
    return lax.dot_general(
        x, y, (((dims[0],), (dims[1],)), ((), ())), preferred_element_type=F32
    )


def hot(x):
    return jnp.where(x, 1.0, 0.0).astype(BF16)


def row_hot(index_row, height):
    columns = index_row.shape[1]
    return hot(lax.broadcasted_iota(I32, (height, columns), 0) == index_row)


def parts_of(x):
    high = x.astype(BF16).astype(F32)
    middle = (x - high).astype(BF16).astype(F32)
    return [high, middle, x - high - middle]


def spare_sums(x, first, width):
    k = lax.broadcasted_iota(I32, (8, x.shape[0]), 0)
    p = lax.broadcasted_iota(I32, (8, x.shape[0]), 1) % width - first
    return dot(hot((p >= 3 * k) & (p < 3 * k + 3) & (k < 2)), x)


def pick_main():
    q = lax.broadcasted_iota(I32, (BLOCK, SIDE * ENTRY), 0)
    p = lax.broadcasted_iota(I32, (BLOCK, SIDE * ENTRY), 1)
    return hot(p == (q >> 4) * ENTRY + (q & 15))


def pick_third():
    q = lax.broadcasted_iota(I32, (DEPTH, SIDE * ENTRY), 0)
    p = lax.broadcasted_iota(I32, (DEPTH, SIDE * ENTRY), 1)
    return hot(p == (q >> 1) * ENTRY + 16 + (q & 1))


def spread(width, per_peer, offset):
    shift = per_peer.bit_length() - 1
    p = lax.broadcasted_iota(I32, (SIDE * ENTRY, width), 0)
    q = lax.broadcasted_iota(I32, (SIDE * ENTRY, width), 1)
    return hot(p == (q >> shift) * ENTRY + offset + (q & (per_peer - 1)))


def gather(index_row, table):
    return dot(row_hot(index_row, 512), table.astype(BF16), (0, 0)).astype(BF16)


def wide_rows(ia, ic, table_a, table_c):
    return dot(spread(BLOCK, 16, 0), gather(ia, table_a)) + dot(
        spread(DEPTH, 2, 16), gather(ic, table_c)
    )


def first_narrow_kernel(ib, ic, fb, send):
    rows = dot(row_hot(ib[...], 512), fb[...].astype(BF16), (0, 0)).reshape(SIDE, 16, RANK)
    lane = lax.broadcasted_iota(I32, (DEPTH, RANK), 1)
    to_lanes = hot(lane == lax.broadcasted_iota(I32, (DEPTH, RANK), 0))
    high, low = (ic[...] >> 4).astype(BF16), (ic[...] & 15).astype(BF16)
    spare = jnp.zeros((ENTRY - 18, RANK), F32)
    tail = jnp.concatenate([dot(high, to_lanes), dot(low, to_lanes), spare], axis=0)
    tail = jnp.broadcast_to(tail[None], (SIDE, ENTRY - 16, RANK))
    send[...] = jnp.concatenate([rows, tail], axis=1).reshape(SIDE * ENTRY, RANK).astype(BF16)


def first_wide_kernel(ia, ic, fa, fc, send):
    send[...] = wide_rows(ia[...], ic[...], fa[...], fc[...]).astype(BF16)


def chunk_copy(source, held, arrived, k, slabs=SLABS):
    here = pl.ds(*slabs[k])
    return pltpu.make_async_copy(source.at[here], held.at[here], arrived.at[k])


def bring(source, held, arrived, slabs=SLABS):
    for k in range(len(slabs)):
        chunk_copy(source, held, arrived, k, slabs).start()


def slab_parts(step, size, slabs=SLABS):
    start, count = slabs[step]
    return range(start, start + count, size)


def accumulate(upstream, pairs, a_part, c, b, to_a, to_c, to_bt, first_row):
    over = dot(upstream, b).reshape(-1, DEPTH, RANK)
    to_a[pl.ds(first_row, a_part.shape[0]), :] = jnp.sum(over * c[None], axis=1)
    to_c[...] += jnp.sum(over * a_part[:, None, :], axis=0)
    to_bt[...] += dot(pairs, upstream, (0, 0))


def fill_send(send, to_b, acc_a, acc_c, acc_bt, spare, rows):
    to_b[...] = acc_bt[...].T
    for peer in range(SIDE):
        base = peer * ENTRY
        rows[base : base + 16, :] = acc_a[peer * 16 : peer * 16 + 16, :]
        tail = jnp.concatenate([acc_c[2 * peer : 2 * peer + 2, :], spare], axis=0)
        rows[base + 16 : base + ENTRY, :] = tail
    send[...] = rows[...].astype(BF16)


def gradient_kernel(
    from_wide, from_narrow, codes_from, send, to_b, a_out, b_out, c_out,
    codes, arrived, to_a, to_c, to_bt, rows,
):
    bring(codes_from, codes, arrived)
    a_out[...] = dot(pick_main(), from_wide[...])
    c_out[...] = dot(pick_third(), from_wide[...])
    b_out[...] = dot(pick_main(), from_narrow[...]).astype(BF16)
    to_c[...] = jnp.zeros_like(to_c)
    to_bt[...] = jnp.zeros_like(to_bt)

    for step in range(len(SLABS)):
        b_half = 0.5 * b_out[...]
        c = c_out[...]
        chunk_copy(codes_from, codes, arrived, step).wait()
        for first_row in slab_parts(step, WIDE_SUB):
            a_part = a_out[pl.ds(first_row, WIDE_SUB), :]
            pairs = (a_part[:, None, :] * c[None]).astype(BF16).reshape(-1, RANK)
            half = jnp.tanh(dot(pairs, b_half, (1, 1)))
            code = codes[pl.ds(first_row, WIDE_SUB)].reshape(-1, BLOCK)
            twice = half + jnp.where(code == 2, -1.0, 1.0)
            twice = jnp.where(code > 0, twice, 0.0).astype(BF16)
            accumulate(twice, pairs, a_part, c, b_half, to_a, to_c, to_bt, first_row)

    to_bt[...] = 0.5 * to_bt[...]
    fill_send(send, to_b, to_a, to_c, to_bt, jnp.zeros((ENTRY - 18, RANK), F32), rows)


def weight_kernel(codes_from, a, b, c, weight_to, codes, weight, arrived, left):
    bring(codes_from, codes, arrived, EVEN_SLABS)

    for step in range(len(EVEN_SLABS)):
        b_half = 0.5 * b[...]
        chunk_copy(codes_from, codes, arrived, step, EVEN_SLABS).wait()
        for first_row in slab_parts(step, WIDE_SUB, EVEN_SLABS):
            inside = pl.ds(first_row, WIDE_SUB)
            pairs = (a[inside, :][:, None, :] * c[...][None]).astype(BF16).reshape(-1, RANK)
            half = jnp.tanh(dot(pairs, b_half, (1, 1)))
            value = jnp.where(codes[inside].reshape(-1, BLOCK) > 0, 1.0 - half * half, 0.0)
            weight[inside] = value.astype(BF16).reshape(WIDE_SUB, DEPTH, BLOCK)
        chunk_copy(weight, weight_to, left, step, EVEN_SLABS).start()

    for k in range(len(EVEN_SLABS)):
        chunk_copy(weight, weight_to, left, k, EVEN_SLABS).wait()


def moved_setup(from_wide, from_narrow, b, d_first, d_third, both):
    d_first[...] = dot(pick_main(), from_wide[...])
    d_third[...] = dot(pick_third(), from_wide[...])
    both[:, :RANK] = 0.25 * b[...]
    both[:, RANK:] = 0.25 * from_narrow[...]


def quarter_change(a_part, d_part, c, d_third, both):
    pairs = (a_part[:, None, :] * c[None]).astype(BF16).reshape(-1, RANK)
    mixed = d_part[:, None, :] * c[None] + a_part[:, None, :] * d_third[None]
    mixed = mixed.astype(BF16).reshape(-1, RANK)
    return pairs, dot(jnp.concatenate([mixed, pairs], axis=1), both, (1, 1))


def fold(x):
    return jnp.sum(x.reshape(-1, 8, BLOCK), axis=0)


def image_kernel(
    from_wide, from_narrow, weight_from, a, b, c, norm, send, to_b,
    weight, arrived, d_first, d_third, both, to_a, to_c, to_bt, rows, total,
):
    bring(weight_from, weight, arrived)
    moved_setup(from_wide, from_narrow, b, d_first, d_third, both)
    to_c[...] = jnp.zeros_like(to_c)
    to_bt[...] = jnp.zeros_like(to_bt)
    total[...] = jnp.zeros_like(total)

    for step in range(len(SLABS)):
        third = c[...]
        chunk_copy(weight_from, weight, arrived, step).wait()
        for first_row in slab_parts(step, SUB_I):
            inside = pl.ds(first_row, SUB_I)
            a_part = a[inside, :]
            d_part = d_first[inside, :]
            pairs, change = quarter_change(a_part, d_part, third, d_third[...], both[...])
            scaled = weight[inside].reshape(-1, BLOCK).astype(F32) * change
            total[...] += fold(scaled * change)
            upstream = scaled.astype(BF16)
            accumulate(upstream, pairs, a_part, third, b[...], to_a, to_c, to_bt, first_row)

    energy = 4.0 * jnp.sum(total[:, :RANK] + total[:, RANK:], axis=0, keepdims=True)
    spare = jnp.concatenate(parts_of(norm[0:1, :]) + parts_of(energy), axis=0)
    fill_send(send, to_b, to_a, to_c, to_bt, spare, rows)


def energy_kernel(
    from_wide, from_narrow, weight_from, a, b, c, sums, send,
    weight, arrived, d_first, d_third, both, total,
):
    bring(weight_from, weight, arrived)
    moved_setup(from_wide, from_narrow, b, d_first, d_third, both)
    total[...] = jnp.zeros_like(total)

    for step in range(len(SLABS)):
        third = c[...]
        chunk_copy(weight_from, weight, arrived, step).wait()
        for first_row in slab_parts(step, SUB_I):
            inside = pl.ds(first_row, SUB_I)
            _, change = quarter_change(
                a[inside, :], d_first[inside, :], third, d_third[...], both[...]
            )
            total[...] += fold(weight[inside].reshape(-1, BLOCK).astype(F32) * change * change)

    energy = 4.0 * jnp.sum(total[...], keepdims=True)
    norm = jnp.sum(sums[0:1, :], axis=1, keepdims=True)
    cross = jnp.sum(sums[1:2, :], axis=1, keepdims=True)
    lane = lax.broadcasted_iota(I32, (1, RANK), 1)
    row = jnp.where(lane == 0, norm, jnp.where(lane == 1, cross, energy))
    send[...] = jnp.broadcast_to(row, send.shape)


def pick_half(core):
    q = lax.broadcasted_iota(I32, (SIDE, SIDE * ENTRY), 0)
    p = lax.broadcasted_iota(I32, (SIDE, SIDE * ENTRY), 1)
    return hot(p == q * ENTRY + 16 + core)


def pack_kernel(from_wide, to_b, send, rows):
    width = send.shape[0] // SIDE
    halves = [dot(pick_half(core), from_wide[...]) for core in range(2)]
    if width > 32:
        sums = spare_sums(from_wide[...], 18, ENTRY)
        spare = parts_of(sums[0:1]) + parts_of(sums[1:2]) + [jnp.zeros((2, RANK), F32)]
        halves = [jnp.concatenate([half] + spare, axis=0) for half in halves]
    for peer in range(SIDE):
        rows[peer * width : peer * width + 16, :] = to_b[peer * 16 : peer * 16 + 16, :]
        rows[peer * width + 16 : peer * width + width, :] = halves[peer % 2]
    send[...] = rows[...].astype(BF16)


def inner(x, y):
    return jnp.sum(x * y, axis=0, keepdims=True)


def rows_of(*values):
    row = lax.broadcasted_iota(I32, (8, RANK), 0)
    out = jnp.broadcast_to(values[-1], (8, RANK))
    for k in range(len(values) - 1):
        out = jnp.where(row == k, values[k], out)
    return out


def third_sum(from_narrow, from_pair, c_row, pair_row):
    mine = dot(row_hot(c_row[...], 512), from_narrow[...])
    return mine + dot(row_hot(pair_row[...], 512), from_pair[...])


def residual_narrow_kernel(from_narrow, b_row, ib, fb, r_b, send, norm):
    rest = -(dot(row_hot(b_row[...], 512), from_narrow[...]) + RIDGE * fb[...])
    r_b[...] = rest
    norm[...] = rows_of(inner(rest, rest))
    send[...] = gather(ib[...], rest)


def residual_wide_kernel(
    from_wide, from_narrow, from_pair, a_row, c_row, pair_row, ia, ic, count_third, fa, fc, part,
    r_a, r_c, send, norm,
):
    rest_a = -(dot(row_hot(a_row[...], 512), from_wide[...]) + RIDGE * fa[...])
    sum_c = third_sum(from_narrow, from_pair, c_row, pair_row)
    rest_c = -(sum_c + RIDGE * fc[...])
    r_a[...] = rest_a
    r_c[...] = rest_c
    send[...] = wide_rows(ia[...], ic[...], rest_a, rest_c).astype(BF16)
    third = inner(rest_c, rest_c) * count_third[0:1, :]
    norm[...] = rows_of(part[0:1, :] + inner(rest_a, rest_a) + third)


def update_narrow_kernel(from_narrow, b_row, ib, r_b, n_b, send, sums, scalars):
    spare = spare_sums(from_narrow[...], 32, from_narrow.shape[0] // SIDE)
    norm = jnp.sum(spare[0:1], axis=1, keepdims=True)
    curved = RIDGE * norm + jnp.sum(spare[1:2], axis=1, keepdims=True)
    alpha = norm / curved
    image = dot(row_hot(b_row[...], 512), from_narrow[...]) + RIDGE * r_b[...]
    rest = r_b[...] - alpha * image
    n_b[...] = rest
    send[...] = gather(ib[...], rest)
    sums[...] = rows_of(inner(rest, rest), inner(rest, image))
    scalars[...] = rows_of(norm, curved, alpha)


def update_wide_kernel(
    from_wide, from_narrow, from_pair, a_row, c_row, pair_row, ia, ic, count_third, r_a, r_c, part,
    scalars, n_a, n_c, send, sums,
):
    alpha = scalars[2:3, 0:1]
    image_a = dot(row_hot(a_row[...], 512), from_wide[...]) + RIDGE * r_a[...]
    image_c = third_sum(from_narrow, from_pair, c_row, pair_row) + RIDGE * r_c[...]
    rest_a = r_a[...] - alpha * image_a
    rest_c = r_c[...] - alpha * image_c
    n_a[...] = rest_a
    n_c[...] = rest_c
    send[...] = wide_rows(ia[...], ic[...], rest_a, rest_c).astype(BF16)
    count = count_third[0:1, :]
    sums[...] = rows_of(
        part[0:1, :] + inner(rest_a, rest_a) + count * inner(rest_c, rest_c),
        part[1:2, :] + inner(rest_a, image_a) + count * inner(rest_c, image_c),
    )


def step_kernel(received, scalars, r_a, r_b, r_c, n_a, n_b, n_c, s_a, s_b, s_c):
    total = jnp.sum(received[...], axis=0, keepdims=True)
    new, cross, energy = total[:, 0:1], total[:, 1:2], total[:, 2:3]
    norm, curved, alpha = scalars[0:1, 0:1], scalars[1:2, 0:1], scalars[2:3, 0:1]
    beta = new / norm
    second = new / (RIDGE * new + energy + 2.0 * beta * cross + beta * beta * curved)
    for old, rest, out in ((r_a, n_a, s_a), (r_b, n_b, s_b), (r_c, n_c, s_c)):
        out[...] = alpha * old[...] + second * (rest[...] + beta * old[...])


def call(kernel, outs, *operands, name, limit=24, scratch=()):
    return pl.pallas_call(
        kernel,
        out_shape=outs,
        scratch_shapes=scratch,
        name=name,
        cost_estimate=pl.CostEstimate(flops=10**8, bytes_accessed=3 << 20, transcendentals=0),
        compiler_params=pltpu.CompilerParams(vmem_limit_bytes=limit << 20),
    )(*operands)


def block_call(kernel, outs, out_specs, in_specs, scratch, *operands, name, cost=5 * 10**9):
    return pl.pallas_call(
        kernel,
        in_specs=in_specs,
        out_specs=out_specs,
        out_shape=outs,
        scratch_shapes=scratch,
        name=name,
        cost_estimate=pl.CostEstimate(flops=cost, bytes_accessed=12 << 20, transcendentals=0),
        compiler_params=pltpu.CompilerParams(
            vmem_limit_bytes=50 << 20
        ),
    )(*operands)


def exchange(x, axis):
    return lax.all_to_all(x, axis, split_axis=0, concat_axis=0, tiled=True)


def after(x, earlier):
    return lax.optimization_barrier((x, earlier))[0]


def local(entries, factor_a, factor_b, factor_c, index_a, index_b, index_c):
    rows = SIDE * ENTRY
    ia, ib, ic = index_a.reshape(1, BLOCK), index_b.reshape(1, BLOCK), index_c.reshape(1, DEPTH)
    rows_bf16, block_bf16 = struct((rows, RANK), BF16), struct((BLOCK, RANK), BF16)
    block_f32 = struct((BLOCK, RANK), F32)
    small = struct((8, RANK), F32)
    table = struct((512, RANK), F32)

    send_narrow = call(
        first_narrow_kernel, rows_bf16, ib, ic, factor_b, name="first_narrow", limit=60
    )
    from_narrow = exchange(send_narrow, "narrow")
    send_wide = call(
        first_wide_kernel, rows_bf16, ia, ic, factor_a, factor_c, name="first_wide", limit=60
    )
    from_wide = exchange(after(send_wide, from_narrow), "wide")
    group_index = from_narrow.reshape(SIDE, ENTRY, RANK)[:, 16:18, :DEPTH].astype(F32)
    group_index = (group_index[:, 0] * 16.0 + group_index[:, 1]).astype(I32)

    def none(width):
        return jnp.full((SIDE, width), -1, I32)

    def place(*parts):
        return jnp.concatenate(parts, axis=1).reshape(1, -1)

    a_row = place(index_a.reshape(SIDE, 16), none(ENTRY - 16))

    core = lax.axis_index("narrow") % 2
    by_core = group_index.reshape(SIDE, SIDE, 2)
    own_half = jnp.where(core == 0, by_core[:, :, 0], by_core[:, :, 1])
    pair_half = jnp.where(core == 0, by_core[:, :, 1], by_core[:, :, 0])

    def narrow_places(spare):
        return (
            place(index_b.reshape(SIDE, 16), none(16 + spare)),
            place(none(16), own_half, none(spare)),
            place(none(16), pair_half, none(spare)),
        )

    count_third = jnp.broadcast_to((lax.axis_index("narrow") == 0).astype(F32), (8, RANK))

    def give_back(send, to_b, spare):
        from_wide = exchange(send, "wide")
        shape = (SIDE * (32 + spare), RANK)
        send = call(
            pack_kernel, struct(shape, BF16), from_wide, to_b,
            name="pack", scratch=[pltpu.VMEM(shape, F32)],
        )
        return from_wide, send, exchange(send, "narrow")

    def from_other_core(x):
        return lax.ppermute(x, "narrow", [(n, n ^ 1) for n in range(SIDE)])

    slab = pl.BlockSpec(memory_space=pl.ANY)
    cube = (BLOCK, DEPTH, BLOCK)
    arrivals = pltpu.SemaphoreType.DMA((len(EVEN_SLABS),))
    both_scratch = [
        pltpu.VMEM(cube, BF16), arrivals,
        pltpu.VMEM((BLOCK, RANK), F32), pltpu.VMEM((DEPTH, RANK), F32),
        pltpu.VMEM((BLOCK, 2 * RANK), BF16),
    ]
    sum_scratch = [
        pltpu.VMEM((BLOCK, RANK), F32), pltpu.VMEM((DEPTH, RANK), F32),
        pltpu.VMEM((RANK, BLOCK), F32), pltpu.VMEM((rows, RANK), F32),
    ]
    total_scratch = [pltpu.VMEM((8, BLOCK), F32)]

    places_first, places_second = narrow_places(0), narrow_places(8)
    from_wide = after(from_wide, (places_first, places_second, a_row))
    send, to_b, a, b, c = block_call(
        gradient_kernel,
        (rows_bf16, block_f32, block_f32, block_bf16, struct((DEPTH, RANK), F32)),
        (
            full((rows, RANK)), full((BLOCK, RANK)), full((BLOCK, RANK)), full((BLOCK, RANK)),
            full((DEPTH, RANK)),
        ),
        [full((rows, RANK)), full((rows, RANK)), slab],
        [pltpu.VMEM(cube, I32), arrivals] + sum_scratch,
        from_wide, from_narrow, entries,
        name="gradient",
    )
    back_wide, packed, back_narrow = give_back(send, to_b, 0)
    weight = block_call(
        weight_kernel,
        pltpu.HBM(cube, BF16),
        slab,
        [slab, full((BLOCK, RANK)), full((BLOCK, RANK)), full((DEPTH, RANK))],
        [pltpu.VMEM(cube, I32), pltpu.VMEM(cube, BF16), arrivals, arrivals],
        entries, after(a, packed), b, c,
        name="weight", cost=6 * 10**9,
    )
    back_narrow, weight = lax.optimization_barrier((back_narrow, weight))
    b_row, c_row, pair_row = places_first
    r_b, send_narrow, part = call(
        residual_narrow_kernel,
        (table, block_bf16, small),
        back_narrow, b_row, ib, factor_b,
        name="residual_narrow",
    )
    from_narrow = exchange(send_narrow, "narrow")
    back_pair = from_other_core(after(back_narrow, send_narrow))
    r_a, r_c, send_wide, norm = call(
        residual_wide_kernel,
        (table, table, rows_bf16, small),
        back_wide, back_narrow, back_pair, a_row, c_row, pair_row, ia, ic, count_third, factor_a,
        factor_c, part,
        name="residual_wide",
    )
    from_wide = exchange(after(send_wide, from_narrow), "wide")
    fixed_specs = [
        full((rows, RANK)), full((BLOCK, RANK)), slab,
        full((BLOCK, RANK)), full((BLOCK, RANK)), full((DEPTH, RANK)), full((8, RANK)),
    ]
    send, to_b = block_call(
        image_kernel,
        (rows_bf16, block_f32),
        (full((rows, RANK)), full((BLOCK, RANK))),
        fixed_specs,
        both_scratch + sum_scratch + total_scratch,
        from_wide, from_narrow, weight, a, b, c, norm,
        name="image",
    )
    back_wide, packed, back_narrow = give_back(send, to_b, 8)
    b_row, c_row, pair_row = places_second
    n_b, send_narrow, part, scalars = call(
        update_narrow_kernel,
        (table, block_bf16, small, small),
        back_narrow, b_row, ib, r_b,
        name="update_narrow",
    )
    from_narrow = exchange(send_narrow, "narrow")
    back_pair = from_other_core(after(back_narrow, send_narrow))
    n_a, n_c, send_wide, sums = call(
        update_wide_kernel,
        (table, table, rows_bf16, small),
        back_wide, back_narrow, back_pair, a_row, c_row, pair_row, ia, ic, count_third, r_a,
        r_c, part, scalars,
        name="update_wide",
    )
    from_wide = exchange(after(send_wide, from_narrow), "wide")
    partial = block_call(
        energy_kernel,
        block_f32,
        full((BLOCK, RANK)),
        fixed_specs,
        both_scratch + total_scratch,
        from_wide, from_narrow, weight, a, b, c, sums,
        name="energy",
    )
    received = exchange(partial, ("wide", "narrow"))
    return call(
        step_kernel,
        (table, table, table),
        received, scalars, r_a, r_b, r_c, n_a, n_b, n_c,
        name="step",
    )


def solution(mesh):
    placed = (
        P(("wide", "narrow"), None, None),
        P(("wide", "narrow"), None),
        P(("wide", "narrow"), None),
        P("wide", None),
        P(("wide", "narrow")),
        P(("wide", "narrow")),
        P(("wide", "narrow")),
    )
    return jax.shard_map(
        local,
        mesh=mesh,
        in_specs=placed,
        out_specs=(P(("wide", "narrow"), None), P(("wide", "narrow"), None), P("wide", None)),
        check_vma=False,
    )
```

```python
import jax
import jax.numpy as jnp
from jax import lax
from jax.experimental import pallas as pl
from jax.experimental.pallas import tpu as pltpu
from jax.sharding import PartitionSpec as P

RIDGE = 25.0
F32, BF16, I32 = jnp.float32, jnp.bfloat16, jnp.int32

RANK = 128
SIDE = 16
BLOCK = 256
DEPTH = 32
ENTRY = 24
SLABS = ((0, 32), (32, 96), (128, 128))
EVEN_SLABS = ((0, 64), (64, 64), (128, 64), (192, 64))
SUB_I = 8
WIDE_SUB = 16


def full(shape):
    return pl.BlockSpec(memory_space=pltpu.VMEM)


def struct(shape, dtype):
    return jax.ShapeDtypeStruct(shape, dtype)


def dot(x, y, dims=(1, 0)):
    return lax.dot_general(
        x, y, (((dims[0],), (dims[1],)), ((), ())), preferred_element_type=F32
    )


def hot(x):
    return jnp.where(x, 1.0, 0.0).astype(BF16)


def row_hot(index_row, height):
    columns = index_row.shape[1]
    return hot(lax.broadcasted_iota(I32, (height, columns), 0) == index_row)


def parts_of(x):
    high = x.astype(BF16).astype(F32)
    middle = (x - high).astype(BF16).astype(F32)
    return [high, middle, x - high - middle]


def spare_sums(x, first, width):
    k = lax.broadcasted_iota(I32, (8, x.shape[0]), 0)
    p = lax.broadcasted_iota(I32, (8, x.shape[0]), 1) % width - first
    return dot(hot((p >= 3 * k) & (p < 3 * k + 3) & (k < 2)), x)


def pick_main():
    q = lax.broadcasted_iota(I32, (BLOCK, SIDE * ENTRY), 0)
    p = lax.broadcasted_iota(I32, (BLOCK, SIDE * ENTRY), 1)
    return hot(p == (q >> 4) * ENTRY + (q & 15))


def pick_third():
    q = lax.broadcasted_iota(I32, (DEPTH, SIDE * ENTRY), 0)
    p = lax.broadcasted_iota(I32, (DEPTH, SIDE * ENTRY), 1)
    return hot(p == (q >> 1) * ENTRY + 16 + (q & 1))


def spread(width, per_peer, offset):
    shift = per_peer.bit_length() - 1
    p = lax.broadcasted_iota(I32, (SIDE * ENTRY, width), 0)
    q = lax.broadcasted_iota(I32, (SIDE * ENTRY, width), 1)
    return hot(p == (q >> shift) * ENTRY + offset + (q & (per_peer - 1)))


def gather(index_row, table):
    return dot(row_hot(index_row, 512), table.astype(BF16), (0, 0)).astype(BF16)


def wide_rows(ia, ic, table_a, table_c):
    return dot(spread(BLOCK, 16, 0), gather(ia, table_a)) + dot(
        spread(DEPTH, 2, 16), gather(ic, table_c)
    )


def first_narrow_kernel(ib, ic, fb, send):
    rows = dot(row_hot(ib[...], 512), fb[...].astype(BF16), (0, 0)).reshape(SIDE, 16, RANK)
    lane = lax.broadcasted_iota(I32, (DEPTH, RANK), 1)
    to_lanes = hot(lane == lax.broadcasted_iota(I32, (DEPTH, RANK), 0))
    high, low = (ic[...] >> 4).astype(BF16), (ic[...] & 15).astype(BF16)
    spare = jnp.zeros((ENTRY - 18, RANK), F32)
    tail = jnp.concatenate([dot(high, to_lanes), dot(low, to_lanes), spare], axis=0)
    tail = jnp.broadcast_to(tail[None], (SIDE, ENTRY - 16, RANK))
    send[...] = jnp.concatenate([rows, tail], axis=1).reshape(SIDE * ENTRY, RANK).astype(BF16)


def first_wide_kernel(ia, ic, fa, fc, send):
    send[...] = wide_rows(ia[...], ic[...], fa[...], fc[...]).astype(BF16)


def chunk_copy(source, held, arrived, k, slabs=SLABS):
    here = pl.ds(*slabs[k])
    return pltpu.make_async_copy(source.at[here], held.at[here], arrived.at[k])


def bring(source, held, arrived, slabs=SLABS):
    for k in range(len(slabs)):
        chunk_copy(source, held, arrived, k, slabs).start()


def slab_parts(step, size, slabs=SLABS):
    start, count = slabs[step]
    return range(start, start + count, size)


def accumulate(upstream, pairs, a_part, c, b, to_a, to_c, to_bt, first_row):
    over = dot(upstream, b).reshape(-1, DEPTH, RANK)
    to_a[pl.ds(first_row, a_part.shape[0]), :] = jnp.sum(over * c[None], axis=1)
    to_c[...] += jnp.sum(over * a_part[:, None, :], axis=0)
    to_bt[...] += dot(pairs, upstream, (0, 0))


def fill_send(send, to_b, acc_a, acc_c, acc_bt, spare, rows):
    to_b[...] = acc_bt[...].T
    for peer in range(SIDE):
        base = peer * ENTRY
        rows[base : base + 16, :] = acc_a[peer * 16 : peer * 16 + 16, :]
        tail = jnp.concatenate([acc_c[2 * peer : 2 * peer + 2, :], spare], axis=0)
        rows[base + 16 : base + ENTRY, :] = tail
    send[...] = rows[...].astype(BF16)


def gradient_kernel(
    from_wide, from_narrow, codes_from, send, to_b, a_out, b_out, c_out,
    codes, arrived, to_a, to_c, to_bt, rows,
):
    bring(codes_from, codes, arrived)
    a_out[...] = dot(pick_main(), from_wide[...])
    c_out[...] = dot(pick_third(), from_wide[...])
    b_out[...] = dot(pick_main(), from_narrow[...]).astype(BF16)
    to_c[...] = jnp.zeros_like(to_c)
    to_bt[...] = jnp.zeros_like(to_bt)

    for step in range(len(SLABS)):
        b_half = 0.5 * b_out[...]
        c = c_out[...]
        chunk_copy(codes_from, codes, arrived, step).wait()
        for first_row in slab_parts(step, WIDE_SUB):
            a_part = a_out[pl.ds(first_row, WIDE_SUB), :]
            pairs = (a_part[:, None, :] * c[None]).astype(BF16).reshape(-1, RANK)
            half = jnp.tanh(dot(pairs, b_half, (1, 1)))
            code = codes[pl.ds(first_row, WIDE_SUB)].reshape(-1, BLOCK)
            twice = half + jnp.where(code == 2, -1.0, 1.0)
            twice = jnp.where(code > 0, twice, 0.0).astype(BF16)
            accumulate(twice, pairs, a_part, c, b_half, to_a, to_c, to_bt, first_row)

    to_bt[...] = 0.5 * to_bt[...]
    fill_send(send, to_b, to_a, to_c, to_bt, jnp.zeros((ENTRY - 18, RANK), F32), rows)


def weight_kernel(codes_from, a, b, c, weight_to, codes, weight, arrived, left):
    bring(codes_from, codes, arrived, EVEN_SLABS)

    for step in range(len(EVEN_SLABS)):
        b_half = 0.5 * b[...]
        chunk_copy(codes_from, codes, arrived, step, EVEN_SLABS).wait()
        for first_row in slab_parts(step, WIDE_SUB, EVEN_SLABS):
            inside = pl.ds(first_row, WIDE_SUB)
            pairs = (a[inside, :][:, None, :] * c[...][None]).astype(BF16).reshape(-1, RANK)
            half = jnp.tanh(dot(pairs, b_half, (1, 1)))
            value = jnp.where(codes[inside].reshape(-1, BLOCK) > 0, 1.0 - half * half, 0.0)
            weight[inside] = value.astype(BF16).reshape(WIDE_SUB, DEPTH, BLOCK)
        chunk_copy(weight, weight_to, left, step, EVEN_SLABS).start()

    for k in range(len(EVEN_SLABS)):
        chunk_copy(weight, weight_to, left, k, EVEN_SLABS).wait()


def moved_setup(from_wide, from_narrow, b, d_first, d_third, both):
    d_first[...] = dot(pick_main(), from_wide[...])
    d_third[...] = dot(pick_third(), from_wide[...])
    both[:, :RANK] = 0.25 * b[...]
    both[:, RANK:] = 0.25 * from_narrow[...]


def quarter_change(a_part, d_part, c, d_third, both):
    pairs = (a_part[:, None, :] * c[None]).astype(BF16).reshape(-1, RANK)
    mixed = d_part[:, None, :] * c[None] + a_part[:, None, :] * d_third[None]
    mixed = mixed.astype(BF16).reshape(-1, RANK)
    return pairs, dot(jnp.concatenate([mixed, pairs], axis=1), both, (1, 1))


def fold(x):
    return jnp.sum(x.reshape(-1, 8, BLOCK), axis=0)


def image_kernel(
    from_wide, from_narrow, weight_from, a, b, c, norm, send, to_b,
    weight, arrived, d_first, d_third, both, to_a, to_c, to_bt, rows, total,
):
    bring(weight_from, weight, arrived)
    moved_setup(from_wide, from_narrow, b, d_first, d_third, both)
    to_c[...] = jnp.zeros_like(to_c)
    to_bt[...] = jnp.zeros_like(to_bt)
    total[...] = jnp.zeros_like(total)

    for step in range(len(SLABS)):
        third = c[...]
        chunk_copy(weight_from, weight, arrived, step).wait()
        for first_row in slab_parts(step, SUB_I):
            inside = pl.ds(first_row, SUB_I)
            a_part = a[inside, :]
            d_part = d_first[inside, :]
            pairs, change = quarter_change(a_part, d_part, third, d_third[...], both[...])
            scaled = weight[inside].reshape(-1, BLOCK).astype(F32) * change
            total[...] += fold(scaled * change)
            upstream = scaled.astype(BF16)
            accumulate(upstream, pairs, a_part, third, b[...], to_a, to_c, to_bt, first_row)

    energy = 4.0 * jnp.sum(total[:, :RANK] + total[:, RANK:], axis=0, keepdims=True)
    spare = jnp.concatenate(parts_of(norm[0:1, :]) + parts_of(energy), axis=0)
    fill_send(send, to_b, to_a, to_c, to_bt, spare, rows)


def energy_kernel(
    from_wide, from_narrow, weight_from, a, b, c, sums, send,
    weight, arrived, d_first, d_third, both, total,
):
    bring(weight_from, weight, arrived)
    moved_setup(from_wide, from_narrow, b, d_first, d_third, both)
    total[...] = jnp.zeros_like(total)

    for step in range(len(SLABS)):
        third = c[...]
        chunk_copy(weight_from, weight, arrived, step).wait()
        for first_row in slab_parts(step, SUB_I):
            inside = pl.ds(first_row, SUB_I)
            _, change = quarter_change(
                a[inside, :], d_first[inside, :], third, d_third[...], both[...]
            )
            total[...] += fold(weight[inside].reshape(-1, BLOCK).astype(F32) * change * change)

    energy = 4.0 * jnp.sum(total[...], keepdims=True)
    norm = jnp.sum(sums[0:1, :], axis=1, keepdims=True)
    cross = jnp.sum(sums[1:2, :], axis=1, keepdims=True)
    lane = lax.broadcasted_iota(I32, (1, RANK), 1)
    row = jnp.where(lane == 0, norm, jnp.where(lane == 1, cross, energy))
    send[...] = jnp.broadcast_to(row, send.shape)


def pick_half(core):
    q = lax.broadcasted_iota(I32, (SIDE, SIDE * ENTRY), 0)
    p = lax.broadcasted_iota(I32, (SIDE, SIDE * ENTRY), 1)
    return hot(p == q * ENTRY + 16 + core)


def pack_kernel(from_wide, to_b, send, rows):
    width = send.shape[0] // SIDE
    halves = [dot(pick_half(core), from_wide[...]) for core in range(2)]
    if width > 32:
        sums = spare_sums(from_wide[...], 18, ENTRY)
        spare = parts_of(sums[0:1]) + parts_of(sums[1:2]) + [jnp.zeros((2, RANK), F32)]
        halves = [jnp.concatenate([half] + spare, axis=0) for half in halves]
    for peer in range(SIDE):
        rows[peer * width : peer * width + 16, :] = to_b[peer * 16 : peer * 16 + 16, :]
        rows[peer * width + 16 : peer * width + width, :] = halves[peer % 2]
    send[...] = rows[...].astype(BF16)


def inner(x, y):
    return jnp.sum(x * y, axis=0, keepdims=True)


def rows_of(*values):
    row = lax.broadcasted_iota(I32, (8, RANK), 0)
    out = jnp.broadcast_to(values[-1], (8, RANK))
    for k in range(len(values) - 1):
        out = jnp.where(row == k, values[k], out)
    return out


def third_sum(from_narrow, from_pair, c_row, pair_row):
    mine = dot(row_hot(c_row[...], 512), from_narrow[...])
    return mine + dot(row_hot(pair_row[...], 512), from_pair[...])


def residual_narrow_kernel(from_narrow, b_row, ib, fb, r_b, send, norm):
    rest = -(dot(row_hot(b_row[...], 512), from_narrow[...]) + RIDGE * fb[...])
    r_b[...] = rest
    norm[...] = rows_of(inner(rest, rest))
    send[...] = gather(ib[...], rest)


def residual_wide_kernel(
    from_wide, from_narrow, from_pair, a_row, c_row, pair_row, ia, ic, count_third, fa, fc, part,
    r_a, r_c, send, norm,
):
    rest_a = -(dot(row_hot(a_row[...], 512), from_wide[...]) + RIDGE * fa[...])
    sum_c = third_sum(from_narrow, from_pair, c_row, pair_row)
    rest_c = -(sum_c + RIDGE * fc[...])
    r_a[...] = rest_a
    r_c[...] = rest_c
    send[...] = wide_rows(ia[...], ic[...], rest_a, rest_c).astype(BF16)
    third = inner(rest_c, rest_c) * count_third[0:1, :]
    norm[...] = rows_of(part[0:1, :] + inner(rest_a, rest_a) + third)


def update_narrow_kernel(from_narrow, b_row, ib, r_b, n_b, send, sums, scalars):
    spare = spare_sums(from_narrow[...], 32, from_narrow.shape[0] // SIDE)
    norm = jnp.sum(spare[0:1], axis=1, keepdims=True)
    curved = RIDGE * norm + jnp.sum(spare[1:2], axis=1, keepdims=True)
    alpha = norm / curved
    image = dot(row_hot(b_row[...], 512), from_narrow[...]) + RIDGE * r_b[...]
    rest = r_b[...] - alpha * image
    n_b[...] = rest
    send[...] = gather(ib[...], rest)
    sums[...] = rows_of(inner(rest, rest), inner(rest, image))
    scalars[...] = rows_of(norm, curved, alpha)


def update_wide_kernel(
    from_wide, from_narrow, from_pair, a_row, c_row, pair_row, ia, ic, count_third, r_a, r_c, part,
    scalars, n_a, n_c, send, sums,
):
    alpha = scalars[2:3, 0:1]
    image_a = dot(row_hot(a_row[...], 512), from_wide[...]) + RIDGE * r_a[...]
    image_c = third_sum(from_narrow, from_pair, c_row, pair_row) + RIDGE * r_c[...]
    rest_a = r_a[...] - alpha * image_a
    rest_c = r_c[...] - alpha * image_c
    n_a[...] = rest_a
    n_c[...] = rest_c
    send[...] = wide_rows(ia[...], ic[...], rest_a, rest_c).astype(BF16)
    count = count_third[0:1, :]
    sums[...] = rows_of(
        part[0:1, :] + inner(rest_a, rest_a) + count * inner(rest_c, rest_c),
        part[1:2, :] + inner(rest_a, image_a) + count * inner(rest_c, image_c),
    )


def step_kernel(received, scalars, r_a, r_b, r_c, n_a, n_b, n_c, s_a, s_b, s_c):
    total = jnp.sum(received[...], axis=0, keepdims=True)
    new, cross, energy = total[:, 0:1], total[:, 1:2], total[:, 2:3]
    norm, curved, alpha = scalars[0:1, 0:1], scalars[1:2, 0:1], scalars[2:3, 0:1]
    beta = new / norm
    second = new / (RIDGE * new + energy + 2.0 * beta * cross + beta * beta * curved)
    for old, rest, out in ((r_a, n_a, s_a), (r_b, n_b, s_b), (r_c, n_c, s_c)):
        out[...] = alpha * old[...] + second * (rest[...] + beta * old[...])


def call(kernel, outs, *operands, name, limit=24, scratch=()):
    return pl.pallas_call(
        kernel,
        out_shape=outs,
        scratch_shapes=scratch,
        name=name,
        cost_estimate=pl.CostEstimate(flops=10**8, bytes_accessed=3 << 20, transcendentals=0),
        compiler_params=pltpu.CompilerParams(vmem_limit_bytes=limit << 20),
    )(*operands)


def block_call(kernel, outs, out_specs, in_specs, scratch, *operands, name, cost=5 * 10**9):
    return pl.pallas_call(
        kernel,
        in_specs=in_specs,
        out_specs=out_specs,
        out_shape=outs,
        scratch_shapes=scratch,
        name=name,
        cost_estimate=pl.CostEstimate(flops=cost, bytes_accessed=12 << 20, transcendentals=0),
        compiler_params=pltpu.CompilerParams(
            vmem_limit_bytes=50 << 20
        ),
    )(*operands)


def exchange(x, axis):
    return lax.all_to_all(x, axis, split_axis=0, concat_axis=0, tiled=True)


def after(x, earlier):
    return lax.optimization_barrier((x, earlier))[0]


def local(entries, factor_a, factor_b, factor_c, index_a, index_b, index_c):
    rows = SIDE * ENTRY
    ia, ib, ic = index_a.reshape(1, BLOCK), index_b.reshape(1, BLOCK), index_c.reshape(1, DEPTH)
    rows_bf16, block_bf16 = struct((rows, RANK), BF16), struct((BLOCK, RANK), BF16)
    block_f32 = struct((BLOCK, RANK), F32)
    small = struct((8, RANK), F32)
    table = struct((512, RANK), F32)

    send_narrow = call(
        first_narrow_kernel, rows_bf16, ib, ic, factor_b, name="first_narrow", limit=60
    )
    from_narrow = exchange(send_narrow, "narrow")
    send_wide = call(
        first_wide_kernel, rows_bf16, ia, ic, factor_a, factor_c, name="first_wide", limit=60
    )
    from_wide = exchange(after(send_wide, from_narrow), "wide")
    group_index = from_narrow.reshape(SIDE, ENTRY, RANK)[:, 16:18, :DEPTH].astype(F32)
    group_index = (group_index[:, 0] * 16.0 + group_index[:, 1]).astype(I32)

    def none(width):
        return jnp.full((SIDE, width), -1, I32)

    def place(*parts):
        return jnp.concatenate(parts, axis=1).reshape(1, -1)

    late_a, late_b = after((index_a, index_b), from_narrow)
    a_row = place(late_a.reshape(SIDE, 16), none(ENTRY - 16))

    core = lax.axis_index("narrow") % 2
    by_core = group_index.reshape(SIDE, SIDE, 2)
    own_half = jnp.where(core == 0, by_core[:, :, 0], by_core[:, :, 1])
    pair_half = jnp.where(core == 0, by_core[:, :, 1], by_core[:, :, 0])

    def narrow_places(spare):
        return (
            place(late_b.reshape(SIDE, 16), none(16 + spare)),
            place(none(16), own_half, none(spare)),
            place(none(16), pair_half, none(spare)),
        )

    count_third = jnp.broadcast_to((lax.axis_index("narrow") == 0).astype(F32), (8, RANK))

    def give_back(send, to_b, spare):
        from_wide = exchange(send, "wide")
        shape = (SIDE * (32 + spare), RANK)
        send = call(
            pack_kernel, struct(shape, BF16), from_wide, to_b,
            name="pack", scratch=[pltpu.VMEM(shape, F32)],
        )
        return from_wide, send, exchange(send, "narrow")

    def from_other_core(x):
        return lax.ppermute(x, "narrow", [(n, n ^ 1) for n in range(SIDE)])

    slab = pl.BlockSpec(memory_space=pl.ANY)
    cube = (BLOCK, DEPTH, BLOCK)
    arrivals = pltpu.SemaphoreType.DMA((len(EVEN_SLABS),))
    both_scratch = [
        pltpu.VMEM(cube, BF16), arrivals,
        pltpu.VMEM((BLOCK, RANK), F32), pltpu.VMEM((DEPTH, RANK), F32),
        pltpu.VMEM((BLOCK, 2 * RANK), BF16),
    ]
    sum_scratch = [
        pltpu.VMEM((BLOCK, RANK), F32), pltpu.VMEM((DEPTH, RANK), F32),
        pltpu.VMEM((RANK, BLOCK), F32), pltpu.VMEM((rows, RANK), F32),
    ]
    total_scratch = [pltpu.VMEM((8, BLOCK), F32)]

    places_first, places_second = narrow_places(0), narrow_places(8)
    from_wide = after(from_wide, (places_first, places_second, a_row))
    send, to_b, a, b, c = block_call(
        gradient_kernel,
        (rows_bf16, block_f32, block_f32, block_bf16, struct((DEPTH, RANK), F32)),
        (
            full((rows, RANK)), full((BLOCK, RANK)), full((BLOCK, RANK)), full((BLOCK, RANK)),
            full((DEPTH, RANK)),
        ),
        [full((rows, RANK)), full((rows, RANK)), slab],
        [pltpu.VMEM(cube, I32), arrivals] + sum_scratch,
        from_wide, from_narrow, entries,
        name="gradient",
    )
    back_wide, packed, back_narrow = give_back(send, to_b, 0)
    weight = block_call(
        weight_kernel,
        pltpu.HBM(cube, BF16),
        slab,
        [slab, full((BLOCK, RANK)), full((BLOCK, RANK)), full((DEPTH, RANK))],
        [pltpu.VMEM(cube, I32), pltpu.VMEM(cube, BF16), arrivals, arrivals],
        entries, after(a, packed), b, c,
        name="weight", cost=6 * 10**9,
    )
    back_narrow, weight = lax.optimization_barrier((back_narrow, weight))
    b_row, c_row, pair_row = places_first
    r_b, send_narrow, part = call(
        residual_narrow_kernel,
        (table, block_bf16, small),
        back_narrow, b_row, ib, factor_b,
        name="residual_narrow",
    )
    from_narrow = exchange(send_narrow, "narrow")
    back_pair = from_other_core(after(back_narrow, send_narrow))
    r_a, r_c, send_wide, norm = call(
        residual_wide_kernel,
        (table, table, rows_bf16, small),
        back_wide, back_narrow, back_pair, a_row, c_row, pair_row, ia, ic, count_third, factor_a,
        factor_c, part,
        name="residual_wide",
    )
    from_wide = exchange(after(send_wide, from_narrow), "wide")
    fixed_specs = [
        full((rows, RANK)), full((BLOCK, RANK)), slab,
        full((BLOCK, RANK)), full((BLOCK, RANK)), full((DEPTH, RANK)), full((8, RANK)),
    ]
    send, to_b = block_call(
        image_kernel,
        (rows_bf16, block_f32),
        (full((rows, RANK)), full((BLOCK, RANK))),
        fixed_specs,
        both_scratch + sum_scratch + total_scratch,
        from_wide, from_narrow, weight, a, b, c, norm,
        name="image",
    )
    back_wide, packed, back_narrow = give_back(send, to_b, 8)
    b_row, c_row, pair_row = places_second
    n_b, send_narrow, part, scalars = call(
        update_narrow_kernel,
        (table, block_bf16, small, small),
        back_narrow, b_row, ib, r_b,
        name="update_narrow",
    )
    from_narrow = exchange(send_narrow, "narrow")
    back_pair = from_other_core(after(back_narrow, send_narrow))
    n_a, n_c, send_wide, sums = call(
        update_wide_kernel,
        (table, table, rows_bf16, small),
        back_wide, back_narrow, back_pair, a_row, c_row, pair_row, ia, ic, count_third, r_a,
        r_c, part, scalars,
        name="update_wide",
    )
    from_wide = exchange(after(send_wide, from_narrow), "wide")
    partial = block_call(
        energy_kernel,
        block_f32,
        full((BLOCK, RANK)),
        fixed_specs,
        both_scratch + total_scratch,
        from_wide, from_narrow, weight, a, b, c, sums,
        name="energy",
    )
    received = exchange(partial, ("wide", "narrow"))
    return call(
        step_kernel,
        (table, table, table),
        received, scalars, r_a, r_b, r_c, n_a, n_b, n_c,
        name="step",
    )


def solution(mesh):
    placed = (
        P(("wide", "narrow"), None, None),
        P(("wide", "narrow"), None),
        P(("wide", "narrow"), None),
        P("wide", None),
        P(("wide", "narrow")),
        P(("wide", "narrow")),
        P(("wide", "narrow")),
    )
    return jax.shard_map(
        local,
        mesh=mesh,
        in_specs=placed,
        out_specs=(P(("wide", "narrow"), None), P(("wide", "narrow"), None), P("wide", None)),
        check_vma=False,
    )
```

```python
import jax
import jax.numpy as jnp
from jax import lax
from jax.experimental import pallas as pl
from jax.experimental.pallas import tpu as pltpu
from jax.sharding import PartitionSpec as P

RIDGE = 25.0
F32, BF16, I32 = jnp.float32, jnp.bfloat16, jnp.int32

RANK = 128
SIDE = 16
BLOCK = 256
DEPTH = 32
ENTRY = 24
SLABS = ((0, 32), (32, 96), (128, 128))
EVEN_SLABS = ((0, 64), (64, 64), (128, 64), (192, 64))
SUB_I = 8
WIDE_SUB = 16


def full(shape):
    return pl.BlockSpec(memory_space=pltpu.VMEM)


def struct(shape, dtype):
    return jax.ShapeDtypeStruct(shape, dtype)


def dot(x, y, dims=(1, 0)):
    return lax.dot_general(
        x, y, (((dims[0],), (dims[1],)), ((), ())), preferred_element_type=F32
    )


def hot(x):
    return jnp.where(x, 1.0, 0.0).astype(BF16)


def row_hot(index_row, height):
    columns = index_row.shape[1]
    return hot(lax.broadcasted_iota(I32, (height, columns), 0) == index_row)


def parts_of(x):
    high = x.astype(BF16).astype(F32)
    middle = (x - high).astype(BF16).astype(F32)
    return [high, middle, x - high - middle]


def spare_sums(x, first, width):
    k = lax.broadcasted_iota(I32, (8, x.shape[0]), 0)
    p = lax.broadcasted_iota(I32, (8, x.shape[0]), 1) % width - first
    return dot(hot((p >= 3 * k) & (p < 3 * k + 3) & (k < 2)), x)


def pick_main():
    q = lax.broadcasted_iota(I32, (BLOCK, SIDE * ENTRY), 0)
    p = lax.broadcasted_iota(I32, (BLOCK, SIDE * ENTRY), 1)
    return hot(p == (q >> 4) * ENTRY + (q & 15))


def pick_third():
    q = lax.broadcasted_iota(I32, (DEPTH, SIDE * ENTRY), 0)
    p = lax.broadcasted_iota(I32, (DEPTH, SIDE * ENTRY), 1)
    return hot(p == (q >> 1) * ENTRY + 16 + (q & 1))


def spread(width, per_peer, offset):
    shift = per_peer.bit_length() - 1
    p = lax.broadcasted_iota(I32, (SIDE * ENTRY, width), 0)
    q = lax.broadcasted_iota(I32, (SIDE * ENTRY, width), 1)
    return hot(p == (q >> shift) * ENTRY + offset + (q & (per_peer - 1)))


def gather(index_row, table):
    return dot(row_hot(index_row, 512), table.astype(BF16), (0, 0)).astype(BF16)


def wide_rows(ia, ic, table_a, table_c):
    return dot(spread(BLOCK, 16, 0), gather(ia, table_a)) + dot(
        spread(DEPTH, 2, 16), gather(ic, table_c)
    )


def first_narrow_kernel(ib, ic, fb, send):
    rows = dot(row_hot(ib[...], 512), fb[...].astype(BF16), (0, 0)).reshape(SIDE, 16, RANK)
    lane = lax.broadcasted_iota(I32, (DEPTH, RANK), 1)
    to_lanes = hot(lane == lax.broadcasted_iota(I32, (DEPTH, RANK), 0))
    high, low = (ic[...] >> 4).astype(BF16), (ic[...] & 15).astype(BF16)
    spare = jnp.zeros((ENTRY - 18, RANK), F32)
    tail = jnp.concatenate([dot(high, to_lanes), dot(low, to_lanes), spare], axis=0)
    tail = jnp.broadcast_to(tail[None], (SIDE, ENTRY - 16, RANK))
    send[...] = jnp.concatenate([rows, tail], axis=1).reshape(SIDE * ENTRY, RANK).astype(BF16)


def first_wide_kernel(ia, ic, fa, fc, send):
    send[...] = wide_rows(ia[...], ic[...], fa[...], fc[...]).astype(BF16)


def chunk_copy(source, held, arrived, k, slabs=SLABS):
    here = pl.ds(*slabs[k])
    return pltpu.make_async_copy(source.at[here], held.at[here], arrived.at[k])


def bring(source, held, arrived, slabs=SLABS):
    for k in range(len(slabs)):
        chunk_copy(source, held, arrived, k, slabs).start()


def slab_parts(step, size, slabs=SLABS):
    start, count = slabs[step]
    return range(start, start + count, size)


def accumulate(upstream, pairs, a_part, c, b, to_a, to_c, to_bt, first_row):
    over = dot(upstream, b).reshape(-1, DEPTH, RANK)
    to_a[pl.ds(first_row, a_part.shape[0]), :] = jnp.sum(over * c[None], axis=1)
    to_c[...] += jnp.sum(over * a_part[:, None, :], axis=0)
    to_bt[...] += dot(pairs, upstream, (0, 0))


def fill_send(send, to_b, acc_a, acc_c, acc_bt, spare, rows):
    to_b[...] = acc_bt[...].T
    for peer in range(SIDE):
        base = peer * ENTRY
        rows[base : base + 16, :] = acc_a[peer * 16 : peer * 16 + 16, :]
        tail = jnp.concatenate([acc_c[2 * peer : 2 * peer + 2, :], spare], axis=0)
        rows[base + 16 : base + ENTRY, :] = tail
    send[...] = rows[...].astype(BF16)


def gradient_kernel(
    from_wide, from_narrow, codes_from, send, to_b, a_out, b_out, c_out,
    codes, arrived, to_a, to_c, to_bt, rows,
):
    bring(codes_from, codes, arrived)
    a_out[...] = dot(pick_main(), from_wide[...])
    c_out[...] = dot(pick_third(), from_wide[...])
    b_out[...] = dot(pick_main(), from_narrow[...]).astype(BF16)
    to_c[...] = jnp.zeros_like(to_c)
    to_bt[...] = jnp.zeros_like(to_bt)

    for step in range(len(SLABS)):
        b_half = 0.5 * b_out[...]
        c = c_out[...]
        chunk_copy(codes_from, codes, arrived, step).wait()
        for first_row in slab_parts(step, WIDE_SUB):
            a_part = a_out[pl.ds(first_row, WIDE_SUB), :]
            pairs = (a_part[:, None, :] * c[None]).astype(BF16).reshape(-1, RANK)
            half = jnp.tanh(dot(pairs, b_half, (1, 1)))
            code = codes[pl.ds(first_row, WIDE_SUB)].reshape(-1, BLOCK)
            twice = half + jnp.where(code == 2, -1.0, 1.0)
            twice = jnp.where(code > 0, twice, 0.0).astype(BF16)
            accumulate(twice, pairs, a_part, c, b_half, to_a, to_c, to_bt, first_row)

    to_bt[...] = 0.5 * to_bt[...]
    fill_send(send, to_b, to_a, to_c, to_bt, jnp.zeros((ENTRY - 18, RANK), F32), rows)


def weight_kernel(codes_from, a, b, c, weight_to, codes, weight, arrived, left):
    bring(codes_from, codes, arrived, EVEN_SLABS)

    for step in range(len(EVEN_SLABS)):
        b_half = 0.5 * b[...]
        chunk_copy(codes_from, codes, arrived, step, EVEN_SLABS).wait()
        for first_row in slab_parts(step, WIDE_SUB, EVEN_SLABS):
            inside = pl.ds(first_row, WIDE_SUB)
            pairs = (a[inside, :][:, None, :] * c[...][None]).astype(BF16).reshape(-1, RANK)
            half = jnp.tanh(dot(pairs, b_half, (1, 1)))
            value = jnp.where(codes[inside].reshape(-1, BLOCK) > 0, 1.0 - half * half, 0.0)
            weight[inside] = value.astype(BF16).reshape(WIDE_SUB, DEPTH, BLOCK)
        chunk_copy(weight, weight_to, left, step, EVEN_SLABS).start()

    for k in range(len(EVEN_SLABS)):
        chunk_copy(weight, weight_to, left, k, EVEN_SLABS).wait()


def moved_setup(from_wide, from_narrow, b, d_first, d_third, both):
    d_first[...] = dot(pick_main(), from_wide[...])
    d_third[...] = dot(pick_third(), from_wide[...])
    both[:, :RANK] = 0.25 * b[...]
    both[:, RANK:] = 0.25 * from_narrow[...]


def quarter_change(a_part, d_part, c, d_third, both):
    pairs = (a_part[:, None, :] * c[None]).astype(BF16).reshape(-1, RANK)
    mixed = d_part[:, None, :] * c[None] + a_part[:, None, :] * d_third[None]
    mixed = mixed.astype(BF16).reshape(-1, RANK)
    return pairs, dot(jnp.concatenate([mixed, pairs], axis=1), both, (1, 1))


def fold(x):
    return jnp.sum(x.reshape(-1, 8, BLOCK), axis=0)


def image_kernel(
    from_wide, from_narrow, weight_from, a, b, c, norm, send, to_b,
    weight, arrived, d_first, d_third, both, to_a, to_c, to_bt, rows, total,
):
    bring(weight_from, weight, arrived)
    moved_setup(from_wide, from_narrow, b, d_first, d_third, both)
    to_c[...] = jnp.zeros_like(to_c)
    to_bt[...] = jnp.zeros_like(to_bt)
    total[...] = jnp.zeros_like(total)

    for step in range(len(SLABS)):
        third = c[...]
        chunk_copy(weight_from, weight, arrived, step).wait()
        for first_row in slab_parts(step, SUB_I):
            inside = pl.ds(first_row, SUB_I)
            a_part = a[inside, :]
            d_part = d_first[inside, :]
            pairs, change = quarter_change(a_part, d_part, third, d_third[...], both[...])
            scaled = weight[inside].reshape(-1, BLOCK).astype(F32) * change
            total[...] += fold(scaled * change)
            upstream = scaled.astype(BF16)
            accumulate(upstream, pairs, a_part, third, b[...], to_a, to_c, to_bt, first_row)

    energy = 4.0 * jnp.sum(total[:, :RANK] + total[:, RANK:], axis=0, keepdims=True)
    spare = jnp.concatenate(parts_of(norm[0:1, :]) + parts_of(energy), axis=0)
    fill_send(send, to_b, to_a, to_c, to_bt, spare, rows)


def energy_kernel(
    from_wide, from_narrow, weight_from, a, b, c, sums, send,
    weight, arrived, d_first, d_third, both, total,
):
    bring(weight_from, weight, arrived)
    moved_setup(from_wide, from_narrow, b, d_first, d_third, both)
    total[...] = jnp.zeros_like(total)

    for step in range(len(SLABS)):
        third = c[...]
        chunk_copy(weight_from, weight, arrived, step).wait()
        for first_row in slab_parts(step, SUB_I):
            inside = pl.ds(first_row, SUB_I)
            _, change = quarter_change(
                a[inside, :], d_first[inside, :], third, d_third[...], both[...]
            )
            total[...] += fold(weight[inside].reshape(-1, BLOCK).astype(F32) * change * change)

    energy = 4.0 * jnp.sum(total[...], keepdims=True)
    norm = jnp.sum(sums[0:1, :], axis=1, keepdims=True)
    cross = jnp.sum(sums[1:2, :], axis=1, keepdims=True)
    lane = lax.broadcasted_iota(I32, (1, RANK), 1)
    row = jnp.where(lane == 0, norm, jnp.where(lane == 1, cross, energy))
    send[...] = jnp.broadcast_to(row, send.shape)


def pick_half(core):
    q = lax.broadcasted_iota(I32, (SIDE, SIDE * ENTRY), 0)
    p = lax.broadcasted_iota(I32, (SIDE, SIDE * ENTRY), 1)
    return hot(p == q * ENTRY + 16 + core)


def pack_kernel(from_wide, to_b, send, rows):
    width = send.shape[0] // SIDE
    halves = [dot(pick_half(core), from_wide[...]) for core in range(2)]
    if width > 32:
        sums = spare_sums(from_wide[...], 18, ENTRY)
        spare = parts_of(sums[0:1]) + parts_of(sums[1:2]) + [jnp.zeros((2, RANK), F32)]
        halves = [jnp.concatenate([half] + spare, axis=0) for half in halves]
    for peer in range(SIDE):
        rows[peer * width : peer * width + 16, :] = to_b[peer * 16 : peer * 16 + 16, :]
        rows[peer * width + 16 : peer * width + width, :] = halves[peer % 2]
    send[...] = rows[...].astype(BF16)


def inner(x, y):
    return jnp.sum(x * y, axis=0, keepdims=True)


def rows_of(*values):
    row = lax.broadcasted_iota(I32, (8, RANK), 0)
    out = jnp.broadcast_to(values[-1], (8, RANK))
    for k in range(len(values) - 1):
        out = jnp.where(row == k, values[k], out)
    return out


def third_sum(from_narrow, from_pair, c_row, pair_row):
    mine = dot(row_hot(c_row[...], 512), from_narrow[...])
    return mine + dot(row_hot(pair_row[...], 512), from_pair[...])


def residual_narrow_kernel(from_narrow, b_row, ib, fb, r_b, send, norm):
    rest = -(dot(row_hot(b_row[...], 512), from_narrow[...]) + RIDGE * fb[...])
    r_b[...] = rest
    norm[...] = rows_of(inner(rest, rest))
    send[...] = gather(ib[...], rest)


def residual_wide_kernel(
    from_wide, from_narrow, from_pair, a_row, c_row, pair_row, ia, ic, count_third, fa, fc, part,
    r_a, r_c, send, norm,
):
    rest_a = -(dot(row_hot(a_row[...], 512), from_wide[...]) + RIDGE * fa[...])
    sum_c = third_sum(from_narrow, from_pair, c_row, pair_row)
    rest_c = -(sum_c + RIDGE * fc[...])
    r_a[...] = rest_a
    r_c[...] = rest_c
    send[...] = wide_rows(ia[...], ic[...], rest_a, rest_c).astype(BF16)
    third = inner(rest_c, rest_c) * count_third[0:1, :]
    norm[...] = rows_of(part[0:1, :] + inner(rest_a, rest_a) + third)


def update_narrow_kernel(from_narrow, b_row, ib, r_b, n_b, send, sums, scalars):
    spare = spare_sums(from_narrow[...], 32, from_narrow.shape[0] // SIDE)
    norm = jnp.sum(spare[0:1], axis=1, keepdims=True)
    curved = RIDGE * norm + jnp.sum(spare[1:2], axis=1, keepdims=True)
    alpha = norm / curved
    image = dot(row_hot(b_row[...], 512), from_narrow[...]) + RIDGE * r_b[...]
    rest = r_b[...] - alpha * image
    n_b[...] = rest
    send[...] = gather(ib[...], rest)
    sums[...] = rows_of(inner(rest, rest), inner(rest, image))
    scalars[...] = rows_of(norm, curved, alpha)


def update_wide_kernel(
    from_wide, from_narrow, from_pair, a_row, c_row, pair_row, ia, ic, count_third, r_a, r_c, part,
    scalars, n_a, n_c, send, sums,
):
    alpha = scalars[2:3, 0:1]
    image_a = dot(row_hot(a_row[...], 512), from_wide[...]) + RIDGE * r_a[...]
    image_c = third_sum(from_narrow, from_pair, c_row, pair_row) + RIDGE * r_c[...]
    rest_a = r_a[...] - alpha * image_a
    rest_c = r_c[...] - alpha * image_c
    n_a[...] = rest_a
    n_c[...] = rest_c
    send[...] = wide_rows(ia[...], ic[...], rest_a, rest_c).astype(BF16)
    count = count_third[0:1, :]
    sums[...] = rows_of(
        part[0:1, :] + inner(rest_a, rest_a) + count * inner(rest_c, rest_c),
        part[1:2, :] + inner(rest_a, image_a) + count * inner(rest_c, image_c),
    )


def step_kernel(received, scalars, r_a, r_b, r_c, n_a, n_b, n_c, s_a, s_b, s_c):
    total = jnp.sum(received[...], axis=0, keepdims=True)
    new, cross, energy = total[:, 0:1], total[:, 1:2], total[:, 2:3]
    norm, curved, alpha = scalars[0:1, 0:1], scalars[1:2, 0:1], scalars[2:3, 0:1]
    beta = new / norm
    second = new / (RIDGE * new + energy + 2.0 * beta * cross + beta * beta * curved)
    for old, rest, out in ((r_a, n_a, s_a), (r_b, n_b, s_b), (r_c, n_c, s_c)):
        out[...] = alpha * old[...] + second * (rest[...] + beta * old[...])


def call(kernel, outs, *operands, name, limit=24, scratch=()):
    return pl.pallas_call(
        kernel,
        out_shape=outs,
        scratch_shapes=scratch,
        name=name,
        cost_estimate=pl.CostEstimate(flops=10**8, bytes_accessed=3 << 20, transcendentals=0),
        compiler_params=pltpu.CompilerParams(vmem_limit_bytes=limit << 20),
    )(*operands)


def block_call(kernel, outs, out_specs, in_specs, scratch, *operands, name, cost=5 * 10**9):
    return pl.pallas_call(
        kernel,
        in_specs=in_specs,
        out_specs=out_specs,
        out_shape=outs,
        scratch_shapes=scratch,
        name=name,
        cost_estimate=pl.CostEstimate(flops=cost, bytes_accessed=12 << 20, transcendentals=0),
        compiler_params=pltpu.CompilerParams(
            vmem_limit_bytes=50 << 20
        ),
    )(*operands)


def exchange(x, axis):
    return lax.all_to_all(x, axis, split_axis=0, concat_axis=0, tiled=True)


def after(x, earlier):
    return lax.optimization_barrier((x, earlier))[0]


def local(entries, factor_a, factor_b, factor_c, index_a, index_b, index_c):
    rows = SIDE * ENTRY
    ia, ib, ic = index_a.reshape(1, BLOCK), index_b.reshape(1, BLOCK), index_c.reshape(1, DEPTH)
    rows_bf16, block_bf16 = struct((rows, RANK), BF16), struct((BLOCK, RANK), BF16)
    block_f32 = struct((BLOCK, RANK), F32)
    small = struct((8, RANK), F32)
    table = struct((512, RANK), F32)

    send_narrow = call(
        first_narrow_kernel, rows_bf16, ib, ic, factor_b, name="first_narrow", limit=60
    )
    from_narrow = exchange(send_narrow, "narrow")
    send_wide = call(
        first_wide_kernel, rows_bf16, ia, ic, factor_a, factor_c, name="first_wide", limit=60
    )
    from_wide = exchange(after(send_wide, from_narrow), "wide")
    group_index = from_narrow.reshape(SIDE, ENTRY, RANK)[:, 16:18, :DEPTH].astype(F32)
    group_index = (group_index[:, 0] * 16.0 + group_index[:, 1]).astype(I32)

    def none(width):
        return jnp.full((SIDE, width), -1, I32)

    def place(*parts):
        return jnp.concatenate(parts, axis=1).reshape(1, -1)

    late_a, late_b = after((index_a, index_b), from_narrow)
    a_row = place(late_a.reshape(SIDE, 16), none(ENTRY - 16))

    core = lax.axis_index("narrow") % 2
    by_core = group_index.reshape(SIDE, SIDE, 2)
    own_half = jnp.where(core == 0, by_core[:, :, 0], by_core[:, :, 1])
    pair_half = jnp.where(core == 0, by_core[:, :, 1], by_core[:, :, 0])

    def narrow_places(spare):
        return (
            place(late_b.reshape(SIDE, 16), none(16 + spare)),
            place(none(16), own_half, none(spare)),
            place(none(16), pair_half, none(spare)),
        )

    count_third = jnp.broadcast_to((lax.axis_index("narrow") == 0).astype(F32), (8, RANK))

    def give_back(send, to_b, spare):
        from_wide = exchange(send, "wide")
        shape = (SIDE * (32 + spare), RANK)
        send = call(
            pack_kernel, struct(shape, BF16), from_wide, to_b,
            name="pack", scratch=[pltpu.VMEM(shape, F32)],
        )
        return from_wide, send, exchange(send, "narrow")

    def from_other_core(x):
        return lax.ppermute(x, "narrow", [(n, n ^ 1) for n in range(SIDE)])

    slab = pl.BlockSpec(memory_space=pl.ANY)
    cube = (BLOCK, DEPTH, BLOCK)
    arrivals = pltpu.SemaphoreType.DMA((len(EVEN_SLABS),))
    both_scratch = [
        pltpu.VMEM(cube, BF16), arrivals,
        pltpu.VMEM((BLOCK, RANK), F32), pltpu.VMEM((DEPTH, RANK), F32),
        pltpu.VMEM((BLOCK, 2 * RANK), BF16),
    ]
    sum_scratch = [
        pltpu.VMEM((BLOCK, RANK), F32), pltpu.VMEM((DEPTH, RANK), F32),
        pltpu.VMEM((RANK, BLOCK), F32), pltpu.VMEM((rows, RANK), F32),
    ]
    total_scratch = [pltpu.VMEM((8, BLOCK), F32)]

    places_first, places_second = narrow_places(0), narrow_places(8)
    from_wide = after(from_wide, (places_first, places_second, a_row))
    send, to_b, a, b, c = block_call(
        gradient_kernel,
        (rows_bf16, block_f32, block_f32, block_bf16, struct((DEPTH, RANK), F32)),
        (
            full((rows, RANK)), full((BLOCK, RANK)), full((BLOCK, RANK)), full((BLOCK, RANK)),
            full((DEPTH, RANK)),
        ),
        [full((rows, RANK)), full((rows, RANK)), slab],
        [pltpu.VMEM(cube, I32), arrivals] + sum_scratch,
        from_wide, from_narrow, entries,
        name="gradient",
    )
    back_wide, packed, back_narrow = give_back(send, to_b, 0)
    b_row, c_row, pair_row = places_first
    r_b, send_narrow, part = call(
        residual_narrow_kernel,
        (table, block_bf16, small),
        back_narrow, b_row, ib, factor_b,
        name="residual_narrow",
    )
    from_narrow = exchange(send_narrow, "narrow")
    back_pair = from_other_core(after(back_narrow, send_narrow))
    r_a, r_c, send_wide, norm = call(
        residual_wide_kernel,
        (table, table, rows_bf16, small),
        back_wide, back_narrow, back_pair, a_row, c_row, pair_row, ia, ic, count_third, factor_a,
        factor_c, part,
        name="residual_wide",
    )
    from_wide = exchange(after(send_wide, from_narrow), "wide")
    weight = block_call(
        weight_kernel,
        pltpu.HBM(cube, BF16),
        slab,
        [slab, full((BLOCK, RANK)), full((BLOCK, RANK)), full((DEPTH, RANK))],
        [pltpu.VMEM(cube, I32), pltpu.VMEM(cube, BF16), arrivals, arrivals],
        entries, after(a, send_wide), b, c,
        name="weight", cost=6 * 10**9,
    )
    fixed_specs = [
        full((rows, RANK)), full((BLOCK, RANK)), slab,
        full((BLOCK, RANK)), full((BLOCK, RANK)), full((DEPTH, RANK)), full((8, RANK)),
    ]
    send, to_b = block_call(
        image_kernel,
        (rows_bf16, block_f32),
        (full((rows, RANK)), full((BLOCK, RANK))),
        fixed_specs,
        both_scratch + sum_scratch + total_scratch,
        from_wide, from_narrow, weight, a, b, c, norm,
        name="image",
    )
    back_wide, packed, back_narrow = give_back(send, to_b, 8)
    b_row, c_row, pair_row = places_second
    n_b, send_narrow, part, scalars = call(
        update_narrow_kernel,
        (table, block_bf16, small, small),
        back_narrow, b_row, ib, r_b,
        name="update_narrow",
    )
    from_narrow = exchange(send_narrow, "narrow")
    back_pair = from_other_core(after(back_narrow, send_narrow))
    n_a, n_c, send_wide, sums = call(
        update_wide_kernel,
        (table, table, rows_bf16, small),
        back_wide, back_narrow, back_pair, a_row, c_row, pair_row, ia, ic, count_third, r_a,
        r_c, part, scalars,
        name="update_wide",
    )
    from_wide = exchange(after(send_wide, from_narrow), "wide")
    partial = block_call(
        energy_kernel,
        block_f32,
        full((BLOCK, RANK)),
        fixed_specs,
        both_scratch + total_scratch,
        from_wide, from_narrow, weight, a, b, c, sums,
        name="energy",
    )
    received = exchange(partial, ("wide", "narrow"))
    return call(
        step_kernel,
        (table, table, table),
        received, scalars, r_a, r_b, r_c, n_a, n_b, n_c,
        name="step",
    )


def solution(mesh):
    placed = (
        P(("wide", "narrow"), None, None),
        P(("wide", "narrow"), None),
        P(("wide", "narrow"), None),
        P("wide", None),
        P(("wide", "narrow")),
        P(("wide", "narrow")),
        P(("wide", "narrow")),
    )
    return jax.shard_map(
        local,
        mesh=mesh,
        in_specs=placed,
        out_specs=(P(("wide", "narrow"), None), P(("wide", "narrow"), None), P("wide", None)),
        check_vma=False,
    )
```
